256 devices in a mesh: dp: 64 (over x, z, core), cache: 4 (over y).
Axes of the slice: x: 4, y: 4, z: 8, core: 2. Of those that a mesh axis runs over, the one named last changes fastest.
Arguments:
- student_feats: bfloat16 [2048, 32, 1024], P('dp'), may hold values from -6 to 6
- head_weight: bfloat16 [1024, 5120], P(None, 'cache'), may hold values from -0.1875 to 0.1875
- teacher_cache: bfloat16 [4096, 32, 5120], P('dp', None, 'cache'), may hold values from -410 to 410, as said below
- holder_index: int32 [2048], replicated, may hold values from 0 to 63, as said below
- valid_count: int32 [2048], P('dp'), may hold values from 1 to 32
- image_embed: bfloat16 [2048, 768], P(('dp', 'cache')), may hold values from -5 to 5
- text_embed: bfloat16 [2048, 768], P(('dp', 'cache')), may hold values from -15 to 15
- pair_ids: int32 [2048], P(('dp', 'cache')), may hold values from 0 to 2047, each once
Outputs:
- head_grad: float32 [1024, 5120], P('dp', 'cache')
- image_loss: float32 [2048], P(('dp', 'cache'))
The draws below stay inside these ranges and needn't reach their ends.
Inputs may be any that keep to these rules, and one draw needn't show every extreme that they name: `holder_index`: each dp index holds the teacher rows of exactly 64 images or of none, and of at most 1 of the images of one dp index, a count that is reached. `teacher_cache`: along dp index h, slot s holds the teacher rows of the image with the s-th smallest index among those whose holder is h; the other slots belong to no image.
All inputs are finite; a program needn't handle non-finite values.
Results may differ from the reference program's by a relative error of at most 0.00098.
Values may be sent and summed in bfloat16 or wider, within the bound.
No kernel may reach another device: no remote copies, remote signals or barrier semaphores. Data moves between devices by JAX's collectives and lax.ppermute only.
A program may use at most 128 MiB of HBM per device.

```python
import jax
import jax.numpy as jnp
from jax import lax

DS = 1024
DT = 5120
DE = 768
PATCH = 32
IMG_DEV = 32
IMAGES = 2048
PAIR = 1
HOLD_DEV = 64
N_DP = 64


def embed_pair(key):
    image_key, text_key = jax.random.split(key)
    images = jnp.clip(jax.random.normal(image_key, (IMAGES, DE), jnp.float32) * 2.0, -5.0, 5.0)
    texts = jnp.clip(jax.random.normal(text_key, (IMAGES, DE), jnp.float32) * 2.0, -5.0, 5.0)
    return (images, texts)


def draw_image_embed(key, part):
    images, texts = embed_pair(key)
    return images.astype(jnp.bfloat16)


def draw_text_embed(key, part):
    images, texts = embed_pair(key)
    return texts.astype(jnp.bfloat16)


def draw_teacher_cache(key, part):
    key = jax.random.fold_in(key, 5)
    col_key, row_key, offset_key, base_key = jax.random.split(key, 4)
    shape = (N_DP * HOLD_DEV, PATCH, DT)
    col_scale = jnp.exp(jax.random.uniform(col_key, (DT,), jnp.float32) * jnp.log(10.0))
    row_scale = jnp.exp(jax.random.uniform(row_key, (N_DP * HOLD_DEV, PATCH, 1), jnp.float32) * jnp.log(10.0))
    offsets = jnp.clip(jax.random.normal(offset_key, (N_DP * HOLD_DEV, PATCH, 1), jnp.float32) * 2.0, -6.0, 6.0)
    base = jnp.clip(jax.random.normal(base_key, shape, jnp.float32), -4.0, 4.0)
    values = offsets + row_scale * col_scale * base
    return values.astype(jnp.bfloat16)


def draw_holder_index(key, part):
    key = jax.random.fold_in(key, 11)
    busy_key, offset_key, order_key = jax.random.split(key, 3)
    half_count = N_DP // 2
    middle = 1 + jax.random.permutation(busy_key, N_DP - 2)
    ends = jnp.array([0, N_DP - 1], dtype=jnp.int32)
    busy = jnp.concatenate([ends, middle[:half_count - 2].astype(jnp.int32)])
    offsets = jax.random.permutation(offset_key, half_count)
    owner_keys = jax.random.split(order_key, N_DP)
    orders = jax.vmap(lambda one_key: jax.random.permutation(one_key, IMG_DEV))(owner_keys)
    owners = jnp.arange(N_DP, dtype=jnp.int32)[:, None]
    shifted = offsets[orders // PAIR]
    holders = busy[(owners + shifted) % half_count]
    return holders.reshape(IMAGES).astype(jnp.int32)


def draw_valid_count(key, part):
    key = jax.random.fold_in(key, 13)
    count_key, spot_key = jax.random.split(key)
    counts = jax.random.randint(count_key, (IMAGES,), 1, PATCH + 1)
    spot = jax.random.randint(spot_key, (), 0, IMAGES)
    return counts.at[spot].set(PATCH).astype(jnp.int32)


def block_levels(rng, shape, cuts, smallest, largest):
    gain, own = 1.0, jax.random.fold_in(rng, 6)
    for axis_at, parts in cuts:
        steps = jnp.exp(jax.random.uniform(jax.random.fold_in(own, axis_at), (parts,), jnp.float32, smallest / len(cuts), largest / len(cuts)))
        gain = gain * jnp.repeat(steps, shape[axis_at] // parts).reshape([-1 if axis == axis_at else 1 for axis in range(len(shape))])
    return gain


def bell_draw(own_key, extent, spread, limit, cuts=(), kind=jnp.bfloat16):
    values = spread * jax.random.normal(own_key, extent, jnp.float32)
    if cuts:
        values = values * block_levels(own_key, extent, cuts, -0.22, 0.18)
    return jnp.clip(values, -limit, limit).astype(kind)


def setup_inputs(seed: int = 0) -> dict:
    streams_of = jax.random.split(jax.random.key(seed), 9)
    student_feats = bell_draw(streams_of[0], (IMAGES, PATCH, DS), 1.0, 6.0, ((0, 64),))
    head_weight = bell_draw(streams_of[1], (DS, DT), DS ** -0.5, 0.1875, ((1, 4),))
    teacher_cache = draw_teacher_cache(jax.random.fold_in(streams_of[8], 71), 0)
    holder_index = draw_holder_index(jax.random.fold_in(streams_of[8], 71), 0)
    valid_count = draw_valid_count(jax.random.fold_in(streams_of[8], 71), 0)
    image_embed = draw_image_embed(jax.random.fold_in(streams_of[8], 71), 0)
    text_embed = draw_text_embed(jax.random.fold_in(streams_of[8], 71), 0)
    pair_ids = jax.random.permutation(streams_of[7], IMAGES).astype(jnp.int32)
    return dict(student_feats=student_feats, head_weight=head_weight, teacher_cache=teacher_cache, holder_index=holder_index, valid_count=valid_count, image_embed=image_embed, text_embed=text_embed, pair_ids=pair_ids)


eps = 1e-06
loss_scale = 128.0

def reference(student_feats, head_weight, teacher_cache, holder_index, valid_count, image_embed, text_embed, pair_ids):
    images = student_feats.shape[0]
    patch_rows = student_feats.shape[1]
    student_width = student_feats.shape[2]
    full_cols = head_weight.shape[1]
    positions = jnp.arange(images, dtype=jnp.int32)
    same_holder = (holder_index[:, None] == holder_index[None, :]) & (positions[None, :] < positions[:, None])
    holder_rank = lax.optimization_barrier(jnp.sum(same_holder.astype(jnp.int32), axis=1)).astype(jnp.int32)
    cache_slot = (holder_index * HOLD_DEV + holder_rank).astype(jnp.int32)
    block_imgs = IMG_DEV
    block_count = images // block_imgs

    def absorb_block(grad_sum, block_index):
        first_img = (block_index * block_imgs).astype(jnp.int32)
        student_rows = lax.dynamic_slice_in_dim(student_feats, first_img, block_imgs, 0)
        slots = lax.dynamic_slice_in_dim(cache_slot, first_img, block_imgs, 0)
        counts = lax.dynamic_slice_in_dim(valid_count, first_img, block_imgs, 0)
        teacher = jnp.take(teacher_cache, slots, axis=0).astype(jnp.float32)
        flat_rows = student_rows.reshape(block_imgs * patch_rows, student_width)
        predicted = jnp.dot(flat_rows, head_weight, preferred_element_type=jnp.float32)
        predicted = predicted.reshape(block_imgs, patch_rows, full_cols)
        first_sum = lax.optimization_barrier(jnp.sum(teacher, axis=-1))
        square_sum = lax.optimization_barrier(jnp.sum(teacher * teacher, axis=-1))
        row_mean = first_sum / full_cols
        inv_scale = lax.rsqrt(square_sum / full_cols - row_mean * row_mean + eps)
        residue = predicted - (teacher - row_mean[..., None]) * inv_scale[..., None]
        valid_mask = (jnp.arange(patch_rows, dtype=jnp.int32)[None, :] < counts[:, None]).astype(jnp.float32)
        row_weight = valid_mask / counts.astype(jnp.float32)[:, None]
        regress = lax.optimization_barrier(jnp.sum(row_weight * lax.optimization_barrier(jnp.sum(residue * residue, axis=-1)), axis=-1)) / full_cols
        row_grad = (2.0 * loss_scale / full_cols * row_weight[..., None] * residue).astype(jnp.bfloat16)
        row_grad = row_grad.reshape(block_imgs * patch_rows, full_cols)
        grad_sum = grad_sum + jnp.dot(flat_rows.T, row_grad, preferred_element_type=jnp.float32)
        return (grad_sum, regress)
    head_grad, regress = lax.scan(absorb_block, jnp.zeros((student_width, full_cols), jnp.float32), jnp.arange(block_count, dtype=jnp.int32))
    regress = regress.reshape(images)
    score_scale = image_embed.shape[1] ** (-0.5)
    scores = jnp.dot(image_embed, text_embed.T, preferred_element_type=jnp.float32) * score_scale
    best_score = lax.optimization_barrier(jnp.max(scores, axis=1))
    denom_sum = lax.optimization_barrier(jnp.sum(jnp.exp(scores - best_score[:, None]), axis=1))
    target = jnp.take_along_axis(scores, pair_ids[:, None].astype(jnp.int32), axis=1)[:, 0]
    contrast = best_score + jnp.log(denom_sum) - target
    return (head_grad, regress + contrast)
```

```python
import jax
import jax.numpy as jnp
from jax import lax
from jax.experimental import pallas as pl
from jax.experimental.pallas import tpu as pltpu
from jax.sharding import PartitionSpec as P

eps = 1e-06
loss_scale = 128.0

N_X, N_Z, N_CORE = 4, 8, 2
EXT = 128
VMEM_BYTES = 60 * 1024 * 1024

X_GROUPS = [[x * N_Z * N_CORE + r for x in range(N_X)] for r in range(N_Z * N_CORE)]
Z_GROUPS = [
    [(x * N_Z + z) * N_CORE + c for z in range(N_Z)] for x in range(N_X) for c in range(N_CORE)
]


def params():
    return pltpu.CompilerParams(vmem_limit_bytes=VMEM_BYTES)


def dispatch_rows(student_feats, image_of, cache_pos, cols):
    n_dp = image_of.shape[0]
    rows = student_feats.shape[1]

    def kernel(scalars, feats, out, sems):
        first = pl.multiple_of(scalars[n_dp] * cols, cols)

        def copy(h):
            return pltpu.make_async_copy(
                feats.at[scalars[h], :, pl.ds(first, cols)], out.at[h], sems.at[h]
            )

        for h in range(n_dp):
            copy(h).start()
        for h in range(n_dp):
            copy(h).wait()

    scalars = jnp.concatenate([image_of, cache_pos[None]]).astype(jnp.int32)
    return pl.pallas_call(
        kernel,
        grid_spec=pltpu.PrefetchScalarGridSpec(
            num_scalar_prefetch=1,
            grid=(1,),
            in_specs=[pl.BlockSpec(memory_space=pl.ANY)],
            out_specs=pl.BlockSpec(memory_space=pl.ANY),
            scratch_shapes=[pltpu.SemaphoreType.DMA((n_dp,))],
        ),
        out_shape=jax.ShapeDtypeStruct((n_dp, rows, cols), student_feats.dtype),
        compiler_params=params(),
        name="dispatch_rows",
    )(scalars, student_feats)


def head_terms(scalars, x_own, x_prev, x_next, x_far_a, x_far_b, head_weight, teacher, row_info, full_cols):
    rows, part = x_own.shape
    width, cols = head_weight.shape
    n_part = width // part
    block = 256
    steps = rows // block
    half = steps // 2
    patch = 32
    img_block = block // patch
    n_img = rows // patch
    owner_rows = width // n_img
    out_rows = width // N_CORE

    def kernel(sc, x0, x1, x2, x3a, x3b, w_ref, t_ref, info_ref, keep, send, acc, r_scr):
        step = pl.program_id(0)
        here, core = sc[0], sc[1]
        far = jnp.where(step < half, x3a[...], x3b[...])
        xs = [x0[...], x1[...], x2[...], far]
        places = [lax.rem(here + off, n_part) for off in (0, n_part - 1, 1, 2)]
        pred = jnp.zeros((block, cols), jnp.float32)
        for x, place in zip(xs, places):
            first = pl.multiple_of(place * part, part)
            pred = pred + jnp.dot(
                x, w_ref[pl.ds(first, part), :], preferred_element_type=jnp.float32
            )
        info = info_ref[...]
        mean, inv, coef, weight = (info[:, k : k + 1] for k in range(4))
        residue = pred - (t_ref[...].astype(jnp.float32) - mean) * inv
        row_grad = (coef * residue).astype(jnp.bfloat16)
        row_loss = weight * jnp.sum(residue * residue, axis=-1, keepdims=True)
        row_loss = jnp.broadcast_to(row_loss, (block, EXT)).reshape(img_block, patch, EXT)
        r_scr[pl.ds(pl.multiple_of(step * img_block, img_block), img_block), :] = (
            jnp.sum(row_loss, axis=1) / full_cols
        )
        for x, place in zip(xs, places):
            term = lax.dot_general(
                x, row_grad, (((0,), (0,)), ((), ())), preferred_element_type=jnp.float32
            )

            @pl.when(step == 0)
            def _():
                acc[place] = term

            @pl.when(step > 0)
            def _():
                acc[place] += term

        @pl.when(step == steps - 1)
        def _():
            lane = lax.broadcasted_iota(jnp.int32, (1, EXT), 1)
            top = lax.broadcasted_iota(jnp.int32, (owner_rows, EXT), 0) == 0
            for pair in range(n_img // N_CORE):
                place, z = divmod(pair, N_Z)
                for ref, own in ((keep, core), (send, 1 - core)):
                    src = pl.multiple_of(z * N_CORE * owner_rows + own * owner_rows, owner_rows)
                    dst = slice(pair * owner_rows, (pair + 1) * owner_rows)
                    ref[dst, :cols] = acc[place, pl.ds(src, owner_rows), :]
                    image = pair * N_CORE + own
                    line = jnp.where(lane == sc[2 + image], r_scr[pl.ds(image, 1), :], 0.0)
                    ref[dst, cols:] = jnp.where(top, line, 0.0)

    row_spec = lambda c: pl.BlockSpec((block, c), lambda i, s: (i, 0))
    out_spec = pl.BlockSpec((out_rows, cols + EXT), lambda i, s: (0, 0))
    out = jax.ShapeDtypeStruct((out_rows, cols + EXT), jnp.float32)
    return pl.pallas_call(
        kernel,
        grid_spec=pltpu.PrefetchScalarGridSpec(
            num_scalar_prefetch=1,
            grid=(steps,),
            in_specs=[
                row_spec(part),
                row_spec(part),
                row_spec(part),
                pl.BlockSpec((block, part), lambda i, s: (jnp.minimum(i, half - 1), 0)),
                pl.BlockSpec((block, part), lambda i, s: (jnp.maximum(i - half, 0), 0)),
                pl.BlockSpec((width, cols), lambda i, s: (0, 0)),
                row_spec(cols),
                row_spec(row_info.shape[1]),
            ],
            out_specs=[out_spec, out_spec],
            scratch_shapes=[
                pltpu.VMEM((n_part, part, cols), jnp.float32),
                pltpu.VMEM((n_img, EXT), jnp.float32),
            ],
        ),
        out_shape=[out, out],
        compiler_params=params(),
        cost_estimate=pl.CostEstimate(
            flops=4 * rows * width * cols, bytes_accessed=20 * 2**20, transcendentals=0
        ),
        name="head_terms",
    )(scalars, x_own, x_prev, x_next, x_far_a, x_far_b, head_weight, teacher, row_info)


def exponent(part):
    top = jnp.max(jnp.abs(part), axis=-1, keepdims=True)
    return jnp.ceil(jnp.log(jnp.maximum(top, 2.0**-100)) * 1.4426950408889634)


def code(values):
    cols = values.shape[-1] - EXT
    main, extra = values[:, :cols], values[:, cols:]
    main_exp, extra_exp = exponent(main), exponent(extra)
    main_code = jnp.floor(main * jnp.exp2(14.0 - main_exp) + 0.5).astype(jnp.int32)
    extra_code = jnp.floor(extra * jnp.exp2(14.0 - extra_exp) + 0.5)
    lane = lax.broadcasted_iota(jnp.int32, extra.shape, 1)
    extra_code = jnp.where(
        lane == EXT - 2, main_exp, jnp.where(lane == EXT - 1, extra_exp, extra_code)
    ).astype(jnp.int32)
    return main_code.astype(jnp.int16), extra_code.astype(jnp.int16)


def decode(codes):
    cols = codes.shape[-1] - EXT
    wide = codes.astype(jnp.int32).astype(jnp.float32)
    main, extra = wide[:, :cols], wide[:, cols:]
    main_exp = extra[:, EXT - 2 : EXT - 1]
    extra_exp = extra[:, EXT - 1 :]
    lane = lax.broadcasted_iota(jnp.int32, extra.shape, 1)
    extra = jnp.where(lane < EXT - 2, extra, 0.0)
    return main * jnp.exp2(main_exp - 14.0), extra * jnp.exp2(extra_exp - 14.0)


def add_and_code(keep, received):
    rows, cols = keep.shape
    block = rows // N_X

    def kernel(a, b, out):
        main, extra = code(a[...] + b[...])
        out[:, : cols - EXT] = main
        out[:, cols - EXT :] = extra

    spec = pl.BlockSpec((block, cols), lambda i: (i, 0))
    return pl.pallas_call(
        kernel,
        grid=(N_X,),
        in_specs=[spec, spec],
        out_specs=spec,
        out_shape=jax.ShapeDtypeStruct((rows, cols), jnp.int16),
        compiler_params=params(),
        name="add_and_code",
    )(keep, received)


def sum_and_code(received):
    n, rows, cols = received.shape
    block = 32

    def kernel(src, out):
        main, extra = decode(src[0])
        for k in range(1, n):
            m, e = decode(src[k])
            main, extra = main + m, extra + e
        main, extra = code(jnp.concatenate([main, extra], axis=1))
        out[:, : cols - EXT] = main
        out[:, cols - EXT :] = extra

    return pl.pallas_call(
        kernel,
        grid=(rows // block,),
        in_specs=[pl.BlockSpec((n, block, cols), lambda i: (0, i, 0))],
        out_specs=pl.BlockSpec((block, cols), lambda i: (i, 0)),
        out_shape=jax.ShapeDtypeStruct((rows, cols), jnp.int16),
        compiler_params=params(),
        name="sum_and_code",
    )(received)


def sum_blocks(received):
    n, rows, cols = received.shape

    def kernel(src, out, ext):
        main, extra = decode(src[0])
        for k in range(1, n):
            m, e = decode(src[k])
            main, extra = main + m, extra + e
        out[...] = main
        ext[...] = extra

    return pl.pallas_call(
        kernel,
        out_shape=[
            jax.ShapeDtypeStruct((rows, cols - EXT), jnp.float32),
            jax.ShapeDtypeStruct((rows, EXT), jnp.float32),
        ],
        compiler_params=params(),
        name="sum_blocks",
    )(received)


def local(
    student_feats,
    head_weight,
    teacher_cache,
    holder_index,
    valid_count,
    image_embed,
    text_embed,
    pair_ids,
):
    n_dp = lax.axis_size("dp")
    n_cache = lax.axis_size("cache")
    own_index = lax.axis_index("dp")
    cache_pos = lax.axis_index("cache")
    core = own_index % N_CORE
    img_dev, patch_rows, student_width = student_feats.shape
    slots, _, local_cols = teacher_cache.shape
    full_cols = local_cols * n_cache
    part = student_width // n_cache
    shard_rows, embed = image_embed.shape
    assert slots == n_dp and n_dp == N_X * N_Z * N_CORE

    def ring(x, step):
        return lax.ppermute(x, "cache", [(i, (i + step) % n_cache) for i in range(n_cache)])

    img_order = jnp.arange(img_dev, dtype=jnp.int32)
    own_holders = lax.dynamic_slice_in_dim(holder_index, own_index * img_dev, img_dev, 0)
    dp_order = jnp.arange(n_dp, dtype=jnp.int32)
    image_of = jnp.sum(
        jnp.where(own_holders[None, :] == dp_order[:, None], img_order[None, :], 0), axis=1
    )
    outgoing = dispatch_rows(student_feats, image_of, cache_pos, part)

    counts_line = jnp.zeros((shard_rows, EXT), jnp.bfloat16).at[0, :img_dev].set(
        valid_count.astype(jnp.bfloat16)
    )
    text_all = lax.all_gather(
        jnp.concatenate([text_embed, counts_line], axis=1), "dp", axis=0, tiled=True
    )
    pair_cols = jnp.concatenate(
        [
            (pair_ids // 64)[:, None],
            (pair_ids % 64)[:, None],
            jnp.zeros((shard_rows, EXT - 2), jnp.int32),
        ],
        axis=1,
    ).astype(jnp.bfloat16)
    image_all = lax.all_gather(
        jnp.concatenate([image_embed, pair_cols], axis=1), "cache", axis=0, tiled=True
    )

    with jax.named_scope("student_exchange"):
        mine = lax.all_to_all(outgoing, "dp", split_axis=0, concat_axis=0, tiled=True)
    with jax.named_scope("student_ring"):
        from_prev = ring(mine, 1)
        from_next = ring(mine, -1)
        far_a = ring(from_prev[: n_dp // 2], 1)
        far_b = ring(from_next[n_dp // 2 :], -1)

    with jax.named_scope("teacher_sums"):
        wide = teacher_cache.astype(jnp.float32)
        sums = jnp.stack([jnp.sum(wide, axis=-1), jnp.sum(wide * wide, axis=-1)])
        sums = sums + ring(sums, 1) + ring(sums, 2) + ring(sums, 3)
        row_mean = sums[0] / full_cols
        inv_scale = lax.rsqrt(sums[1] / full_cols - row_mean * row_mean + eps)

    is_held = holder_index.reshape(n_dp, img_dev) == own_index
    counts_all = text_all.reshape(n_dp, shard_rows, embed + EXT)[:, 0, embed : embed + img_dev]
    place_of = jnp.sum(jnp.where(is_held, img_order[None, :], 0), axis=1)
    held_count = jnp.sum(jnp.where(is_held, counts_all.astype(jnp.float32), 0.0), axis=1)
    row_index = jnp.arange(patch_rows, dtype=jnp.int32).astype(jnp.float32)
    valid_mask = (row_index[None, :] < held_count[:, None]).astype(jnp.float32)
    row_weight = valid_mask / jnp.maximum(held_count, 1.0)[:, None]
    coef = 2.0 * loss_scale / full_cols * row_weight
    inv_scale = jnp.where(held_count[:, None] > 0, inv_scale, 0.0)
    row_info = jnp.stack([row_mean, inv_scale, coef, row_weight], axis=-1).reshape(
        n_dp * patch_rows, 4
    )

    with jax.named_scope("contrast"):
        images, pair_code = image_all[:, :embed], image_all[:, embed:].astype(jnp.int32)
        pairs = pair_code[:, 0] * 64 + pair_code[:, 1]
        logits = jnp.dot(
            images, text_all[:, :embed].T, preferred_element_type=jnp.float32
        ) * (embed ** (-0.5))
        column = jnp.arange(n_dp * shard_rows, dtype=jnp.int32)
        text_id = (column // shard_rows) * img_dev + cache_pos * shard_rows + column % shard_rows
        best = jnp.max(logits, axis=1)
        denom = jnp.sum(jnp.exp(logits - best[:, None]), axis=1)
        target = jnp.sum(jnp.where(pairs[:, None] == text_id[None, :], logits, 0.0), axis=1)

    scalars = jnp.concatenate([jnp.stack([cache_pos, core]).astype(jnp.int32), place_of])
    flat = lambda x: x.reshape(-1, x.shape[-1])
    keep, send = head_terms(
        scalars,
        flat(mine),
        flat(from_prev),
        flat(from_next),
        flat(far_a),
        flat(far_b),
        head_weight,
        flat(teacher_cache),
        row_info,
        full_cols,
    )
    with jax.named_scope("grad_core"):
        received = lax.ppermute(send, "dp", [(i, i ^ 1) for i in range(n_dp)])
    codes = add_and_code(keep, received)
    with jax.named_scope("grad_x"):
        codes = lax.all_to_all(
            codes.reshape(N_X, -1, local_cols + EXT), "dp", 0, 0, axis_index_groups=X_GROUPS, tiled=True
        )
    codes = sum_and_code(codes)
    with jax.named_scope("grad_z"):
        codes = lax.all_to_all(
            codes.reshape(N_Z, -1, local_cols + EXT), "dp", 0, 0, axis_index_groups=Z_GROUPS, tiled=True
        )
    head_grad, extra = sum_blocks(codes)

    with jax.named_scope("loss_parts"):
        parts = jnp.stack([extra[0, :img_dev], best, denom, target])
        parts = parts.reshape(4, n_cache, shard_rows).transpose(1, 0, 2)
        parts = lax.all_to_all(parts, "cache", split_axis=0, concat_axis=0, tiled=True)
        top = jnp.max(parts[:, 1], axis=0)
        total = jnp.sum(parts[:, 2] * jnp.exp(parts[:, 1] - top[None, :]), axis=0)
        contrast = top + jnp.log(total) - jnp.sum(parts[:, 3], axis=0)
        image_loss = jnp.sum(parts[:, 0], axis=0) + contrast
    return (head_grad, image_loss)


def solution(mesh):
    in_specs = (
        P("dp", None, None),
        P(None, "cache"),
        P("dp", None, "cache"),
        P(),
        P("dp"),
        P(("dp", "cache"), None),
        P(("dp", "cache"), None),
        P(("dp", "cache")),
    )
    out_specs = (P("dp", "cache"), P(("dp", "cache")))
    return jax.shard_map(local, mesh=mesh, in_specs=in_specs, out_specs=out_specs, check_vma=False)
```

```python
import jax
import jax.numpy as jnp
from jax import lax
from jax.experimental import pallas as pl
from jax.experimental.pallas import tpu as pltpu
from jax.sharding import PartitionSpec as P

eps = 1e-06
loss_scale = 128.0

N_X, N_Z, N_CORE = 4, 8, 2
EXT = 128
VMEM_BYTES = 60 * 1024 * 1024

X_GROUPS = [[x * N_Z * N_CORE + r for x in range(N_X)] for r in range(N_Z * N_CORE)]
Z_GROUPS = [
    [(x * N_Z + z) * N_CORE + c for z in range(N_Z)] for x in range(N_X) for c in range(N_CORE)
]


def params():
    return pltpu.CompilerParams(vmem_limit_bytes=VMEM_BYTES)


def dispatch_rows(student_feats, image_of, cache_pos, cols):
    n_dp = image_of.shape[0]
    images, rows, _ = student_feats.shape

    def kernel(scalars, feats, out):
        for h in range(n_dp):
            out[h] = feats[scalars[h]]

    scalars = jnp.concatenate([image_of, cache_pos[None]]).astype(jnp.int32)
    return pl.pallas_call(
        kernel,
        grid_spec=pltpu.PrefetchScalarGridSpec(
            num_scalar_prefetch=1,
            grid=(1,),
            in_specs=[pl.BlockSpec((images, rows, cols), lambda i, s: (0, 0, s[n_dp]))],
            out_specs=pl.BlockSpec((n_dp, rows, cols), lambda i, s: (0, 0, 0)),
        ),
        out_shape=jax.ShapeDtypeStruct((n_dp, rows, cols), student_feats.dtype),
        compiler_params=params(),
        name="dispatch_rows",
    )(scalars, student_feats)


def predict_rows(cache_pos, x_own, x_prev, x_next, x_far_a, x_far_b, head_weight, teacher, row_info, first_row, full_cols):
    rows, part = x_own.shape
    width, cols = head_weight.shape
    n_part = width // part
    block = 256
    steps = rows // block
    half = steps // 2
    first_step = first_row // block
    patch = 32
    img_block = block // patch

    def kernel(sc, x0, x1, x2, x3a, x3b, w_ref, t_ref, info_ref, x_out, grad_out, r_out):
        step = pl.program_id(0)
        far = jnp.where(step < half, x3a[...], x3b[...])
        xs = [x0[...], x1[...], x2[...], far]
        for x, off in zip(xs, (0, n_part - 1, 1, 2)):
            place = lax.rem(sc[0] + off, n_part)
            x_out[:, pl.ds(pl.multiple_of(place * part, part), part)] = x
        pred = jnp.dot(x_out[...], w_ref[...], preferred_element_type=jnp.float32)
        info = info_ref[...]
        mean, inv, coef, weight = (info[:, k : k + 1] for k in range(4))
        residue = pred - (t_ref[...].astype(jnp.float32) - mean) * inv
        grad_out[...] = (coef * residue).astype(jnp.bfloat16)
        row_loss = weight * jnp.sum(residue * residue, axis=-1, keepdims=True)
        row_loss = jnp.broadcast_to(row_loss, (block, EXT)).reshape(img_block, patch, EXT)
        r_out[...] = jnp.sum(row_loss, axis=1) / full_cols

    row_spec = lambda c: pl.BlockSpec((block, c), lambda i, s: (i, 0))
    at_spec = lambda c: pl.BlockSpec((block, c), lambda i, s: (i + first_step, 0))
    return pl.pallas_call(
        kernel,
        grid_spec=pltpu.PrefetchScalarGridSpec(
            num_scalar_prefetch=1,
            grid=(steps,),
            in_specs=[
                row_spec(part),
                row_spec(part),
                row_spec(part),
                pl.BlockSpec((block, part), lambda i, s: (jnp.minimum(i, half - 1), 0)),
                pl.BlockSpec((block, part), lambda i, s: (jnp.maximum(i - half, 0), 0)),
                pl.BlockSpec((width, cols), lambda i, s: (0, 0)),
                at_spec(cols),
                at_spec(row_info.shape[1]),
            ],
            out_specs=[
                row_spec(width),
                row_spec(cols),
                pl.BlockSpec((img_block, EXT), lambda i, s: (i, 0)),
            ],
        ),
        out_shape=[
            jax.ShapeDtypeStruct((rows, width), jnp.bfloat16),
            jax.ShapeDtypeStruct((rows, cols), jnp.bfloat16),
            jax.ShapeDtypeStruct((rows // patch, EXT), jnp.float32),
        ],
        compiler_params=params(),
        cost_estimate=pl.CostEstimate(
            flops=2 * rows * width * cols, bytes_accessed=12 * 2**20, transcendentals=0
        ),
        name="predict_rows",
    )(cache_pos[None].astype(jnp.int32), x_own, x_prev, x_next, x_far_a, x_far_b, head_weight, teacher, row_info)


OUTER = (((0,), (0,)), ((), ()))


def grad_part(student, row_grad):
    rows, width = student.shape
    cols = row_grad.shape[1]
    tile = 256

    def kernel(x_ref, g_ref, out):
        out[...] = lax.dot_general(x_ref[...], g_ref[...], OUTER, preferred_element_type=jnp.float32)

    return pl.pallas_call(
        kernel,
        grid=(cols // tile,),
        in_specs=[
            pl.BlockSpec((rows, width), lambda i: (0, 0)),
            pl.BlockSpec((rows, tile), lambda i: (0, i)),
        ],
        out_specs=pl.BlockSpec((width, tile), lambda i: (0, i)),
        out_shape=jax.ShapeDtypeStruct((width, cols), jnp.float32),
        compiler_params=params(),
        cost_estimate=pl.CostEstimate(
            flops=2 * rows * width * cols, bytes_accessed=10 * 2**20, transcendentals=0
        ),
        name="grad_part",
    )(student, row_grad)


def grad_split(core, student, row_grad, before):
    rows, width = student.shape
    cols = row_grad.shape[1]
    tile = 256
    pairs = N_X * N_Z
    owner_rows = width // (pairs * N_CORE)
    out_rows = width // N_CORE

    def kernel(sc, x_ref, g_ref, before_ref, keep, send):
        term = before_ref[...] + lax.dot_general(
            x_ref[...], g_ref[...], OUTER, preferred_element_type=jnp.float32
        )
        term = term.reshape(pairs, N_CORE, owner_rows, tile)
        for mine, (first, second) in enumerate(((keep, send), (send, keep))):

            @pl.when(sc[0] == mine)
            def _():
                first[...] = term[:, 0].reshape(out_rows, tile)
                second[...] = term[:, 1].reshape(out_rows, tile)

    out_spec = pl.BlockSpec((out_rows, tile), lambda i, s: (0, i))
    out = jax.ShapeDtypeStruct((out_rows, cols), jnp.float32)
    return pl.pallas_call(
        kernel,
        grid_spec=pltpu.PrefetchScalarGridSpec(
            num_scalar_prefetch=1,
            grid=(cols // tile,),
            in_specs=[
                pl.BlockSpec((rows, width), lambda i, s: (0, 0)),
                pl.BlockSpec((rows, tile), lambda i, s: (0, i)),
                pl.BlockSpec((width, tile), lambda i, s: (0, i)),
            ],
            out_specs=[out_spec, out_spec],
        ),
        out_shape=[out, out],
        compiler_params=params(),
        cost_estimate=pl.CostEstimate(
            flops=2 * rows * width * cols, bytes_accessed=15 * 2**20, transcendentals=0
        ),
        name="grad_split",
    )(core[None].astype(jnp.int32), student, row_grad, before)


def exponent(part):
    top = jnp.max(jnp.abs(part), axis=-1, keepdims=True)
    return jnp.ceil(jnp.log(jnp.maximum(top, 2.0**-100)) * 1.4426950408889634)


def code(main, extra):
    main_exp, extra_exp = exponent(main), exponent(extra)
    main_code = jnp.floor(main * jnp.exp2(14.0 - main_exp) + 0.5).astype(jnp.int32)
    extra_code = jnp.floor(extra * jnp.exp2(14.0 - extra_exp) + 0.5)
    lane = lax.broadcasted_iota(jnp.int32, extra.shape, 1)
    extra_code = jnp.where(
        lane == EXT - 2, main_exp, jnp.where(lane == EXT - 1, extra_exp, extra_code)
    ).astype(jnp.int32)
    return main_code.astype(jnp.int16), extra_code.astype(jnp.int16)


def decode(codes):
    cols = codes.shape[-1] - EXT
    wide = codes.astype(jnp.int32).astype(jnp.float32)
    main, extra = wide[:, :cols], wide[:, cols:]
    main_exp = extra[:, EXT - 2 : EXT - 1]
    extra_exp = extra[:, EXT - 1 :]
    lane = lax.broadcasted_iota(jnp.int32, extra.shape, 1)
    extra = jnp.where(lane < EXT - 2, extra, 0.0)
    return main * jnp.exp2(main_exp - 14.0), extra * jnp.exp2(extra_exp - 14.0)


def add_and_code(keep, received, losses):
    rows, cols = keep.shape
    pairs = losses.shape[0]
    owner_rows = rows // pairs
    block = rows // N_X

    def kernel(a, b, line_ref, out):
        n = block // owner_rows
        lines = jnp.broadcast_to(line_ref[...][:, None, :], (n, owner_rows, EXT))
        top = lax.broadcasted_iota(jnp.int32, lines.shape, 1) == 0
        lines = jnp.where(top, lines, 0.0).reshape(block, EXT)
        main, extra = code(a[...] + b[...], lines)
        out[:, :cols] = main
        out[:, cols:] = extra

    spec = lambda r, c: pl.BlockSpec((r, c), lambda i: (i, 0))
    return pl.pallas_call(
        kernel,
        grid=(N_X,),
        in_specs=[spec(block, cols), spec(block, cols), spec(pairs // N_X, EXT)],
        out_specs=spec(block, cols + EXT),
        out_shape=jax.ShapeDtypeStruct((rows, cols + EXT), jnp.int16),
        compiler_params=params(),
        name="add_and_code",
    )(keep, received, losses)


def sum_and_code(received):
    n, rows, cols = received.shape
    block = 32

    def kernel(src, out):
        main, extra = decode(src[0])
        for k in range(1, n):
            m, e = decode(src[k])
            main, extra = main + m, extra + e
        main, extra = code(main, extra)
        out[:, : cols - EXT] = main
        out[:, cols - EXT :] = extra

    return pl.pallas_call(
        kernel,
        grid=(rows // block,),
        in_specs=[pl.BlockSpec((n, block, cols), lambda i: (0, i, 0))],
        out_specs=pl.BlockSpec((block, cols), lambda i: (i, 0)),
        out_shape=jax.ShapeDtypeStruct((rows, cols), jnp.int16),
        compiler_params=params(),
        name="sum_and_code",
    )(received)


def sum_blocks(received):
    n, rows, cols = received.shape

    def kernel(src, out, ext):
        main, extra = decode(src[0])
        for k in range(1, n):
            m, e = decode(src[k])
            main, extra = main + m, extra + e
        out[...] = main
        ext[...] = extra

    return pl.pallas_call(
        kernel,
        out_shape=[
            jax.ShapeDtypeStruct((rows, cols - EXT), jnp.float32),
            jax.ShapeDtypeStruct((rows, EXT), jnp.float32),
        ],
        compiler_params=params(),
        name="sum_blocks",
    )(received)


def local(
    student_feats,
    head_weight,
    teacher_cache,
    holder_index,
    valid_count,
    image_embed,
    text_embed,
    pair_ids,
):
    n_dp = lax.axis_size("dp")
    n_cache = lax.axis_size("cache")
    own_index = lax.axis_index("dp")
    cache_pos = lax.axis_index("cache")
    core = own_index % N_CORE
    img_dev, patch_rows, student_width = student_feats.shape
    slots, _, local_cols = teacher_cache.shape
    full_cols = local_cols * n_cache
    part = student_width // n_cache
    shard_rows, embed = image_embed.shape
    assert slots == n_dp and n_dp == N_X * N_Z * N_CORE

    def ring(x, step):
        return lax.ppermute(x, "cache", [(i, (i + step) % n_cache) for i in range(n_cache)])

    def flat(x):
        return x.reshape(-1, x.shape[-1])

    img_order = jnp.arange(img_dev, dtype=jnp.int32)
    own_holders = lax.dynamic_slice_in_dim(holder_index, own_index * img_dev, img_dev, 0)
    dp_order = jnp.arange(n_dp, dtype=jnp.int32)
    image_of = jnp.sum(
        jnp.where(own_holders[None, :] == dp_order[:, None], img_order[None, :], 0), axis=1
    )
    outgoing = dispatch_rows(student_feats, image_of, cache_pos, part)

    text_all = lax.all_gather(text_embed, ("dp", "cache"), axis=0, tiled=True)

    with jax.named_scope("student_exchange"):
        mine = lax.all_to_all(outgoing, "dp", split_axis=0, concat_axis=0, tiled=True)
    chunk = n_dp // 2
    chunks = []
    with jax.named_scope("student_ring"):
        for first in range(0, n_dp, chunk):
            own = mine[first : first + chunk]
            from_prev = ring(own, 1)
            from_next = ring(own, -1)
            far_a = ring(from_prev[: chunk // 2], 1)
            far_b = ring(from_next[chunk // 2 :], -1)
            chunks.append([flat(x) for x in (own, from_prev, from_next, far_a, far_b)])

    with jax.named_scope("teacher_sums"):
        wide = teacher_cache.astype(jnp.float32)
        sums = jnp.stack([jnp.sum(wide, axis=-1), jnp.sum(wide * wide, axis=-1)])
        sums = sums + ring(sums, 1) + ring(sums, 2) + ring(sums, 3)
        row_mean = sums[0] / full_cols
        inv_scale = lax.rsqrt(sums[1] / full_cols - row_mean * row_mean + eps)

    is_held = holder_index.reshape(n_dp, img_dev) == own_index
    counts_all = lax.all_gather(valid_count, "dp").reshape(n_dp, img_dev)
    place_of = jnp.sum(jnp.where(is_held, img_order[None, :], 0), axis=1)
    held_count = jnp.sum(jnp.where(is_held, counts_all.astype(jnp.float32), 0.0), axis=1)
    row_index = jnp.arange(patch_rows, dtype=jnp.int32).astype(jnp.float32)
    valid_mask = (row_index[None, :] < held_count[:, None]).astype(jnp.float32)
    row_weight = valid_mask / jnp.maximum(held_count, 1.0)[:, None]
    coef = 2.0 * loss_scale / full_cols * row_weight
    inv_scale = jnp.where(held_count[:, None] > 0, inv_scale, 0.0)
    row_info = jnp.stack([row_mean, inv_scale, coef, row_weight], axis=-1).reshape(
        n_dp * patch_rows, 4
    )

    with jax.named_scope("contrast"):
        logits = jnp.dot(
            image_embed, text_all.T, preferred_element_type=jnp.float32
        ) * (embed ** (-0.5))
        column = jnp.arange(text_all.shape[0], dtype=jnp.int32)
        best = jnp.max(logits, axis=1)
        denom = jnp.sum(jnp.exp(logits - best[:, None]), axis=1)
        target = jnp.sum(jnp.where(pair_ids[:, None] == column[None, :], logits, 0.0), axis=1)
        contrast = best + jnp.log(denom) - target

    outs = [
        predict_rows(cache_pos, *rows, head_weight, flat(teacher_cache), row_info, k * chunk * patch_rows, full_cols)
        for k, rows in enumerate(chunks)
    ]
    with jax.named_scope("image_sums"):
        r = jnp.concatenate([o[2] for o in outs])
        r = r + ring(r, 1) + ring(r, 2) + ring(r, 3)
        other_r = lax.ppermute(r, "dp", [(i, i ^ 1) for i in range(n_dp)])
        other_held = holder_index.reshape(n_dp, img_dev) == (own_index ^ 1)
        other_place = jnp.sum(jnp.where(other_held, img_order[None, :], 0), axis=1)
        lane = jnp.arange(EXT, dtype=jnp.int32)[None, :]
        losses = jnp.where(lane == place_of[:, None], r, 0.0) + jnp.where(
            lane == other_place[:, None], other_r, 0.0
        )
        losses = losses.reshape(n_dp // N_CORE, N_CORE, EXT)
        losses = jnp.where(core == 0, losses[:, 0], losses[:, 1])
    before = grad_part(outs[0][0], outs[0][1])
    keep, send = grad_split(core, outs[1][0], outs[1][1], before)
    with jax.named_scope("grad_core"):
        received = lax.ppermute(send, "dp", [(i, i ^ 1) for i in range(n_dp)])
    codes = add_and_code(keep, received, losses)
    with jax.named_scope("grad_x"):
        codes = lax.all_to_all(
            codes.reshape(N_X, -1, local_cols + EXT), "dp", 0, 0, axis_index_groups=X_GROUPS, tiled=True
        )
    codes = sum_and_code(codes)
    with jax.named_scope("grad_z"):
        codes = lax.all_to_all(
            codes.reshape(N_Z, -1, local_cols + EXT), "dp", 0, 0, axis_index_groups=Z_GROUPS, tiled=True
        )
    head_grad, extra = sum_blocks(codes)

    regress = lax.dynamic_slice_in_dim(extra[0], cache_pos * shard_rows, shard_rows, 0)
    image_loss = regress + contrast
    return (head_grad, image_loss)


def solution(mesh):
    in_specs = (
        P("dp", None, None),
        P(None, "cache"),
        P("dp", None, "cache"),
        P(),
        P("dp"),
        P(("dp", "cache"), None),
        P(("dp", "cache"), None),
        P(("dp", "cache")),
    )
    out_specs = (P("dp", "cache"), P(("dp", "cache")))
    return jax.shard_map(local, mesh=mesh, in_specs=in_specs, out_specs=out_specs, check_vma=False)
```

```python
import jax
import jax.numpy as jnp
from jax import lax
from jax.experimental import pallas as pl
from jax.experimental.pallas import tpu as pltpu
from jax.sharding import PartitionSpec as P

eps = 1e-06
loss_scale = 128.0

N_X, N_Z, N_CORE = 4, 8, 2
EXT = 128
VMEM_BYTES = 60 * 1024 * 1024

X_GROUPS = [[x * N_Z * N_CORE + r for x in range(N_X)] for r in range(N_Z * N_CORE)]
Z_GROUPS = [
    [(x * N_Z + z) * N_CORE + c for z in range(N_Z)] for x in range(N_X) for c in range(N_CORE)
]


def params():
    return pltpu.CompilerParams(vmem_limit_bytes=VMEM_BYTES)


def dispatch_rows(student_feats, image_of, cache_pos, cols):
    n_dp = image_of.shape[0]
    images, rows, _ = student_feats.shape

    def kernel(scalars, feats, out):
        for h in range(n_dp):
            out[h] = feats[scalars[h]]

    scalars = jnp.concatenate([image_of, cache_pos[None]]).astype(jnp.int32)
    return pl.pallas_call(
        kernel,
        grid_spec=pltpu.PrefetchScalarGridSpec(
            num_scalar_prefetch=1,
            grid=(1,),
            in_specs=[pl.BlockSpec((images, rows, cols), lambda i, s: (0, 0, s[n_dp]))],
            out_specs=pl.BlockSpec((n_dp, rows, cols), lambda i, s: (0, 0, 0)),
        ),
        out_shape=jax.ShapeDtypeStruct((n_dp, rows, cols), student_feats.dtype),
        compiler_params=params(),
        name="dispatch_rows",
    )(scalars, student_feats)


OUTER = (((0,), (0,)), ((), ()))


def head_terms(scalars, rows_by_place, head_weight, teacher, row_info, first_row, full_cols, before=None):
    rows, part = rows_by_place[0].shape
    width, cols = head_weight.shape
    n_part = width // part
    block, tile, patch = 256, 256, 32
    steps = rows // block
    half = steps // 2
    first_step = first_row // block
    img_block = block // patch
    pairs = N_X * N_Z
    owner_rows = width // (pairs * N_CORE)
    out_rows = width // N_CORE
    last = before is not None

    def kernel(sc, x0, x1, x2, x3a, x3b, w_ref, t_ref, info_ref, *rest):
        before_ref = rest[0] if last else None
        grads, (r_out, x_scr, g_scr) = (rest[1:3], rest[3:]) if last else (rest[:1], rest[1:])
        step = pl.program_id(0)

        @pl.when(step < steps)
        def _():
            here = pl.ds(pl.multiple_of(step * block, block), block)
            far = jnp.where(step < half, x3a[...], x3b[...])
            xs = [x0[...], x1[...], x2[...], far]
            for x, off in zip(xs, (0, n_part - 1, 1, 2)):
                place = lax.rem(sc[0] + off, n_part)
                x_scr[here, pl.ds(pl.multiple_of(place * part, part), part)] = x
            pred = jnp.dot(x_scr[here, :], w_ref[...], preferred_element_type=jnp.float32)
            info = info_ref[...]
            mean, inv, coef, weight = (info[:, k : k + 1] for k in range(4))
            residue = pred - (t_ref[...].astype(jnp.float32) - mean) * inv
            g_scr[here, :] = (coef * residue).astype(jnp.bfloat16)
            row_loss = weight * jnp.sum(residue * residue, axis=-1, keepdims=True)
            row_loss = jnp.broadcast_to(row_loss, (block, EXT)).reshape(img_block, patch, EXT)
            r_out[pl.ds(pl.multiple_of(step * img_block, img_block), img_block), :] = (
                jnp.sum(row_loss, axis=1) / full_cols
            )

        @pl.when(step >= steps)
        def _():
            first = pl.multiple_of((step - steps) * tile, tile)
            term = lax.dot_general(
                x_scr[...], g_scr[:, pl.ds(first, tile)], OUTER, preferred_element_type=jnp.float32
            )
            if not last:
                grads[0][...] = term
                return
            term = (before_ref[...] + term).reshape(pairs, N_CORE, owner_rows, tile)
            keep, send = grads
            for mine, (one, two) in enumerate(((keep, send), (send, keep))):

                @pl.when(sc[1] == mine)
                def _():
                    one[...] = term[:, 0].reshape(out_rows, tile)
                    two[...] = term[:, 1].reshape(out_rows, tile)

    row_at = lambda i: jnp.minimum(i, steps - 1)
    col_at = lambda i: jnp.maximum(i - steps, 0)
    row_spec = lambda c: pl.BlockSpec((block, c), lambda i, s: (row_at(i), 0))
    at_spec = lambda c: pl.BlockSpec((block, c), lambda i, s: (row_at(i) + first_step, 0))
    far_spec = lambda f: pl.BlockSpec((block, part), lambda i, s: (jnp.clip(f(i), 0, half - 1), 0))
    col_spec = lambda r: pl.BlockSpec((r, tile), lambda i, s: (0, col_at(i)))
    grad_shapes = [(out_rows, cols)] * 2 if last else [(width, cols)]
    return pl.pallas_call(
        kernel,
        grid_spec=pltpu.PrefetchScalarGridSpec(
            num_scalar_prefetch=1,
            grid=(steps + cols // tile,),
            in_specs=[
                row_spec(part),
                row_spec(part),
                row_spec(part),
                far_spec(lambda i: i),
                far_spec(lambda i: i - half),
                pl.BlockSpec((width, cols), lambda i, s: (0, 0)),
                at_spec(cols),
                at_spec(row_info.shape[1]),
            ]
            + ([col_spec(width)] if last else []),
            out_specs=[col_spec(g[0]) for g in grad_shapes]
            + [pl.BlockSpec((rows // patch, EXT), lambda i, s: (0, 0))],
            scratch_shapes=[
                pltpu.VMEM((rows, width), jnp.bfloat16),
                pltpu.VMEM((rows, cols), jnp.bfloat16),
            ],
        ),
        out_shape=[jax.ShapeDtypeStruct(g, jnp.float32) for g in grad_shapes]
        + [jax.ShapeDtypeStruct((rows // patch, EXT), jnp.float32)],
        compiler_params=params(),
        cost_estimate=pl.CostEstimate(
            flops=4 * rows * width * cols, bytes_accessed=20 * 2**20, transcendentals=0
        ),
        name="head_terms",
    )(scalars, *rows_by_place, head_weight, teacher, row_info, *([before] if last else []))


def quantize(part):
    top = jnp.max(jnp.abs(part), axis=-1, keepdims=True)
    exp = jnp.ceil(jnp.log(jnp.maximum(top, 2.0**-100)) * 1.4426950408889634)
    codes = jnp.floor(part * jnp.exp2(14.0 - exp) + 0.5).astype(jnp.int32)
    return codes.astype(jnp.int16), exp


def widen(codes):
    return codes.astype(jnp.int32).astype(jnp.float32)


def add_and_code(keep, received):
    rows, cols = keep.shape
    block = rows // N_X

    def kernel(a, b, out):
        out[:, :cols], exp = quantize(a[...] + b[...])
        out[:, cols:] = jnp.broadcast_to(exp, (block, EXT)).astype(jnp.int32).astype(jnp.int16)

    spec = lambda c: pl.BlockSpec((block, c), lambda i: (i, 0))
    return pl.pallas_call(
        kernel,
        grid=(N_X,),
        in_specs=[spec(cols), spec(cols)],
        out_specs=spec(cols + EXT),
        out_shape=jax.ShapeDtypeStruct((rows, cols + EXT), jnp.int16),
        compiler_params=params(),
        name="add_and_code",
    )(keep, received)


def sum_codes(src, n, cols):
    total = 0.0
    for k in range(n):
        total = total + widen(src[k, :, :cols]) * jnp.exp2(widen(src[k, :, cols:])[:, EXT - 1 :] - 14.0)
    return total


def sum_and_code(received, losses):
    n, rows, wide = received.shape
    cols = wide - EXT
    block = 32

    def kernel(src, loss_ref, out):
        out[:, :cols], exp = quantize(sum_codes(src, n, cols))
        loss = loss_ref[...]
        loss_code, loss_exp = quantize(loss)
        lane = lax.broadcasted_iota(jnp.int32, loss.shape, 1)
        extra = jnp.where(lane == EXT - 2, loss_exp, widen(loss_code))
        extra = jnp.where(lane == EXT - 1, exp, extra)
        out[:, cols:] = extra.astype(jnp.int32).astype(jnp.int16)

    return pl.pallas_call(
        kernel,
        grid=(rows // block,),
        in_specs=[
            pl.BlockSpec((n, block, wide), lambda i: (0, i, 0)),
            pl.BlockSpec((block, EXT), lambda i: (i, 0)),
        ],
        out_specs=pl.BlockSpec((block, wide), lambda i: (i, 0)),
        out_shape=jax.ShapeDtypeStruct((rows, wide), jnp.int16),
        compiler_params=params(),
        name="sum_and_code",
    )(received, losses)


def sum_blocks(received):
    n, rows, wide = received.shape
    cols = wide - EXT

    def kernel(src, out, ext):
        out[...] = sum_codes(src, n, cols)
        total = 0.0
        for k in range(n):
            extra = widen(src[k, :, cols:])
            total = total + extra * jnp.exp2(extra[:, EXT - 2 : EXT - 1] - 14.0)
        ext[...] = total

    return pl.pallas_call(
        kernel,
        out_shape=[
            jax.ShapeDtypeStruct((rows, cols), jnp.float32),
            jax.ShapeDtypeStruct((rows, EXT), jnp.float32),
        ],
        compiler_params=params(),
        name="sum_blocks",
    )(received)


def local(
    student_feats,
    head_weight,
    teacher_cache,
    holder_index,
    valid_count,
    image_embed,
    text_embed,
    pair_ids,
):
    n_dp = lax.axis_size("dp")
    n_cache = lax.axis_size("cache")
    own_index = lax.axis_index("dp")
    cache_pos = lax.axis_index("cache")
    core = own_index % N_CORE
    img_dev, patch_rows, student_width = student_feats.shape
    slots, _, local_cols = teacher_cache.shape
    full_cols = local_cols * n_cache
    part = student_width // n_cache
    shard_rows, embed = image_embed.shape
    assert slots == n_dp and n_dp == N_X * N_Z * N_CORE

    def ring(x, step):
        return lax.ppermute(x, "cache", [(i, (i + step) % n_cache) for i in range(n_cache)])

    def flat(x):
        return x.reshape(-1, x.shape[-1])

    img_order = jnp.arange(img_dev, dtype=jnp.int32)
    own_holders = lax.dynamic_slice_in_dim(holder_index, own_index * img_dev, img_dev, 0)
    dp_order = jnp.arange(n_dp, dtype=jnp.int32)
    image_of = jnp.sum(
        jnp.where(own_holders[None, :] == dp_order[:, None], img_order[None, :], 0), axis=1
    )
    outgoing = dispatch_rows(student_feats, image_of, cache_pos, part)

    def swap(x, bit):
        return lax.ppermute(x, "dp", [(i, i ^ bit) for i in range(n_dp)])

    def both(x, other, bit, index):
        upper = (index // bit) % 2 == 1
        return jnp.concatenate([jnp.where(upper, other, x), jnp.where(upper, x, other)])

    with jax.named_scope("texts"):
        counts_line = jnp.zeros((shard_rows, EXT), jnp.bfloat16).at[0, :img_dev].set(
            valid_count.astype(jnp.bfloat16)
        )
        texts = jnp.concatenate([text_embed, counts_line], axis=1)
        for bit in (1, 2 * N_Z, 4 * N_Z):
            texts = both(texts, swap(texts, bit), bit, own_index)
        counts_line = texts.reshape(N_X * N_CORE, shard_rows, embed + EXT)[:, 0, embed:]
        texts = texts[:, :embed]
        for bit in (1, 2):
            other = lax.ppermute(texts, "cache", [(i, i ^ bit) for i in range(n_cache)])
            texts = both(texts, other, bit, cache_pos)
    with jax.named_scope("images"):
        pair_cols = jnp.concatenate(
            [
                (pair_ids // 64)[:, None],
                (pair_ids % 64)[:, None],
                jnp.zeros((shard_rows, EXT - 2), jnp.int32),
            ],
            axis=1,
        ).astype(jnp.bfloat16)
        images = jnp.concatenate([image_embed, pair_cols, counts_line], axis=1)
        for bit in (2, 4, 8):
            images = both(images, swap(images, bit), bit, own_index)

    with jax.named_scope("student_exchange"):
        mine = lax.all_to_all(outgoing, "dp", split_axis=0, concat_axis=0, tiled=True)
    chunk = n_dp // 2
    chunks = []
    with jax.named_scope("student_ring"):
        for first in range(0, n_dp, chunk):
            own = mine[first : first + chunk]
            if chunks:
                own = lax.optimization_barrier((own, from_prev, from_next))[0]
            from_prev = ring(own, 1)
            from_next = ring(own, -1)
            far_a = ring(from_prev[: chunk // 2], 1)
            far_b = ring(from_next[chunk // 2 :], -1)
            chunks.append([flat(x) for x in (own, from_prev, from_next, far_a, far_b)])

    with jax.named_scope("teacher_sums"):
        wide = teacher_cache.astype(jnp.float32)
        sums = jnp.stack([jnp.sum(wide, axis=-1), jnp.sum(wide * wide, axis=-1)])
        sums = sums + ring(sums, 1) + ring(sums, 2) + ring(sums, 3)
        row_mean = sums[0] / full_cols
        inv_scale = lax.rsqrt(sums[1] / full_cols - row_mean * row_mean + eps)

    is_held = holder_index.reshape(n_dp, img_dev) == own_index
    counts_all = (
        images[:, embed + EXT : embed + EXT + img_dev]
        .reshape(N_Z, N_X, N_CORE, img_dev)
        .transpose(1, 0, 2, 3)
        .reshape(n_dp, img_dev)
    )
    place_of = jnp.sum(jnp.where(is_held, img_order[None, :], 0), axis=1)
    held_count = jnp.sum(jnp.where(is_held, counts_all.astype(jnp.float32), 0.0), axis=1)
    row_index = jnp.arange(patch_rows, dtype=jnp.int32).astype(jnp.float32)
    valid_mask = (row_index[None, :] < held_count[:, None]).astype(jnp.float32)
    row_weight = valid_mask / jnp.maximum(held_count, 1.0)[:, None]
    coef = 2.0 * loss_scale / full_cols * row_weight
    inv_scale = jnp.where(held_count[:, None] > 0, inv_scale, 0.0)
    row_info = jnp.stack([row_mean, inv_scale, coef, row_weight], axis=-1).reshape(
        n_dp * patch_rows, 4
    )

    with jax.named_scope("contrast"):
        pair_code = images[:, embed : embed + 2].astype(jnp.int32)
        pairs = pair_code[:, 0] * 64 + pair_code[:, 1]
        logits = jnp.dot(
            images[:, :embed], texts.T, preferred_element_type=jnp.float32
        ) * (embed ** (-0.5))
        column = jnp.arange(texts.shape[0], dtype=jnp.int32)
        text_row, text_core = column % shard_rows, column // shard_rows % N_CORE
        text_x = column // (shard_rows * N_CORE) % N_X
        text_y = column // (shard_rows * N_CORE * N_X)
        text_dp = (text_x * N_Z + own_index // N_CORE % N_Z) * N_CORE + text_core
        text_id = text_dp * img_dev + text_y * shard_rows + text_row
        best = jnp.max(logits, axis=1)
        denom = jnp.sum(jnp.exp(logits - best[:, None]), axis=1)
        target = jnp.sum(jnp.where(pairs[:, None] == text_id[None, :], logits, 0.0), axis=1)
    row_info, best, denom, target = lax.optimization_barrier((row_info, best, denom, target))

    scalars = jnp.stack([cache_pos, core]).astype(jnp.int32)
    before, r_first = head_terms(
        scalars, chunks[0], head_weight, flat(teacher_cache), row_info, 0, full_cols
    )
    keep, send, r_second = head_terms(
        scalars,
        chunks[1],
        head_weight,
        flat(teacher_cache),
        row_info,
        chunk * patch_rows,
        full_cols,
        before,
    )
    with jax.named_scope("grad_core"):
        received = swap(send, 1)
    codes = add_and_code(keep, received)
    codes, r_first, r_second, best, denom, target = lax.optimization_barrier(
        (codes, r_first, r_second, best, denom, target)
    )
    with jax.named_scope("grad_x"):
        codes = lax.all_to_all(
            codes.reshape(N_X, -1, local_cols + EXT), "dp", 0, 0, axis_index_groups=X_GROUPS, tiled=True
        )
    with jax.named_scope("image_sums"):
        r = jnp.concatenate([r_first, r_second])
        r = r + ring(r, 1) + ring(r, 2) + ring(r, 3)
        other_r = swap(r, 1)
        other_held = holder_index.reshape(n_dp, img_dev) == (own_index ^ 1)
        other_place = jnp.sum(jnp.where(other_held, img_order[None, :], 0), axis=1)
        lane = jnp.arange(EXT, dtype=jnp.int32)[None, :]
        losses = jnp.where(lane == place_of[:, None], r, 0.0) + jnp.where(
            lane == other_place[:, None], other_r, 0.0
        )
        losses = losses.reshape(N_X, N_Z, N_CORE, EXT)
        losses = jnp.where(core == 0, losses[:, :, 0], losses[:, :, 1])
        own_x = own_index // (N_Z * N_CORE)

        def for_x(step):
            return lax.dynamic_index_in_dim(losses, (own_x + step) % N_X, 0, keepdims=False)

        x_stride = N_Z * N_CORE
        total = for_x(0)
        for step in range(1, N_X):
            total = total + lax.ppermute(
                for_x(step), "dp", [(i, (i + step * x_stride) % n_dp) for i in range(n_dp)]
            )
        owner_rows = student_width // n_dp
        losses = jnp.zeros((N_Z, owner_rows, EXT), jnp.float32).at[:, 0].set(total)
        losses = losses.reshape(N_Z * owner_rows, EXT)
    with jax.named_scope("contrast_merge"):
        for bit in (2, 4, 8):
            other = swap(jnp.stack([best, denom, target]), bit)
            top = jnp.maximum(best, other[0])
            denom = denom * jnp.exp(best - top) + other[1] * jnp.exp(other[0] - top)
            best, target = top, target + other[2]
        contrast = best + jnp.log(denom) - target
        own_z = own_index // N_CORE % N_Z
        contrast = lax.dynamic_slice_in_dim(contrast, own_z * shard_rows, shard_rows, 0)
    codes = sum_and_code(codes, losses)
    with jax.named_scope("grad_z"):
        codes = lax.all_to_all(
            codes.reshape(N_Z, -1, local_cols + EXT), "dp", 0, 0, axis_index_groups=Z_GROUPS, tiled=True
        )
    head_grad, extra = sum_blocks(codes)

    regress = lax.dynamic_slice_in_dim(extra[0], cache_pos * shard_rows, shard_rows, 0)
    image_loss = regress + contrast
    return (head_grad, image_loss)


def solution(mesh):
    in_specs = (
        P("dp", None, None),
        P(None, "cache"),
        P("dp", None, "cache"),
        P(),
        P("dp"),
        P(("dp", "cache"), None),
        P(("dp", "cache"), None),
        P(("dp", "cache")),
    )
    out_specs = (P("dp", "cache"), P(("dp", "cache")))
    return jax.shard_map(local, mesh=mesh, in_specs=in_specs, out_specs=out_specs, check_vma=False)
```

```python
import jax
import jax.numpy as jnp
from jax import lax
from jax.experimental import pallas as pl
from jax.experimental.pallas import tpu as pltpu
from jax.sharding import PartitionSpec as P

eps = 1e-06
loss_scale = 128.0

N_X, N_Z, N_CORE = 4, 8, 2
EXT = 128
VMEM_BYTES = 60 * 1024 * 1024

Z_GROUPS = [
    [(x * N_Z + z) * N_CORE + c for z in range(N_Z)] for x in range(N_X) for c in range(N_CORE)
]


def params():
    return pltpu.CompilerParams(vmem_limit_bytes=VMEM_BYTES)


def dispatch_rows(student_feats, image_of, cache_pos, cols):
    n_dp = image_of.shape[0]
    images, rows, _ = student_feats.shape

    def kernel(scalars, feats, out):
        for h in range(n_dp):
            out[h] = feats[scalars[h]]

    scalars = jnp.concatenate([image_of, cache_pos[None]]).astype(jnp.int32)
    return pl.pallas_call(
        kernel,
        grid_spec=pltpu.PrefetchScalarGridSpec(
            num_scalar_prefetch=1,
            grid=(1,),
            in_specs=[pl.BlockSpec((images, rows, cols), lambda i, s: (0, 0, s[n_dp]))],
            out_specs=pl.BlockSpec((n_dp, rows, cols), lambda i, s: (0, 0, 0)),
        ),
        out_shape=jax.ShapeDtypeStruct((n_dp, rows, cols), student_feats.dtype),
        compiler_params=params(),
        name="dispatch_rows",
    )(scalars, student_feats)


OUTER = (((0,), (0,)), ((), ()))


def head_terms(scalars, rows_by_place, head_weight, teacher, row_info, first_row, full_cols, before=None):
    rows, part = rows_by_place[0].shape
    width, cols = head_weight.shape
    n_part = width // part
    block, tile, patch = 256, 256, 32
    steps = rows // block
    half = steps // 2
    first_step = first_row // block
    img_block = block // patch
    pairs = N_X * N_Z
    owner_rows = width // (pairs * N_CORE)
    out_rows = width // N_CORE
    last = before is not None

    def kernel(sc, x0, x1, x2, x3a, x3b, w_ref, t_ref, info_ref, *rest):
        before_ref = rest[0] if last else None
        grads, (r_out, x_scr, g_scr) = (rest[1:3], rest[3:]) if last else (rest[:1], rest[1:])
        step = pl.program_id(0)

        @pl.when(step < steps)
        def _():
            here = pl.ds(pl.multiple_of(step * block, block), block)
            far = jnp.where(step < half, x3a[...], x3b[...])
            xs = [x0[...], x1[...], x2[...], far]
            for x, off in zip(xs, (0, n_part - 1, 1, 2)):
                place = lax.rem(sc[0] + off, n_part)
                x_scr[here, pl.ds(pl.multiple_of(place * part, part), part)] = x
            pred = jnp.dot(x_scr[here, :], w_ref[...], preferred_element_type=jnp.float32)
            info = info_ref[...]
            mean, inv, coef, weight = (info[:, k : k + 1] for k in range(4))
            residue = pred - (t_ref[...].astype(jnp.float32) - mean) * inv
            g_scr[here, :] = (coef * residue).astype(jnp.bfloat16)
            row_loss = weight * jnp.sum(residue * residue, axis=-1, keepdims=True)
            row_loss = jnp.broadcast_to(row_loss, (block, EXT)).reshape(img_block, patch, EXT)
            r_out[pl.ds(pl.multiple_of(step * img_block, img_block), img_block), :] = (
                jnp.sum(row_loss, axis=1) / full_cols
            )

        @pl.when(step >= steps)
        def _():
            first = pl.multiple_of((step - steps) * tile, tile)
            term = lax.dot_general(
                x_scr[...], g_scr[:, pl.ds(first, tile)], OUTER, preferred_element_type=jnp.float32
            )
            if not last:
                grads[0][...] = term
                return
            term = (before_ref[...] + term).reshape(pairs, N_CORE, owner_rows, tile)
            keep, send = grads
            for mine, (one, two) in enumerate(((keep, send), (send, keep))):

                @pl.when(sc[1] == mine)
                def _():
                    one[...] = term[:, 0].reshape(out_rows, tile)
                    two[...] = term[:, 1].reshape(out_rows, tile)

    row_at = lambda i: jnp.minimum(i, steps - 1)
    col_at = lambda i: jnp.maximum(i - steps, 0)
    row_spec = lambda c: pl.BlockSpec((block, c), lambda i, s: (row_at(i), 0))
    at_spec = lambda c: pl.BlockSpec((block, c), lambda i, s: (row_at(i) + first_step, 0))
    far_spec = lambda f: pl.BlockSpec((block, part), lambda i, s: (jnp.clip(f(i), 0, half - 1), 0))
    col_spec = lambda r: pl.BlockSpec((r, tile), lambda i, s: (0, col_at(i)))
    grad_shapes = [(out_rows, cols)] * 2 if last else [(width, cols)]
    return pl.pallas_call(
        kernel,
        grid_spec=pltpu.PrefetchScalarGridSpec(
            num_scalar_prefetch=1,
            grid=(steps + cols // tile,),
            in_specs=[
                row_spec(part),
                row_spec(part),
                row_spec(part),
                far_spec(lambda i: i),
                far_spec(lambda i: i - half),
                pl.BlockSpec((width, cols), lambda i, s: (0, 0)),
                at_spec(cols),
                at_spec(row_info.shape[1]),
            ]
            + ([col_spec(width)] if last else []),
            out_specs=[col_spec(g[0]) for g in grad_shapes]
            + [pl.BlockSpec((rows // patch, EXT), lambda i, s: (0, 0))],
            scratch_shapes=[
                pltpu.VMEM((rows, width), jnp.bfloat16),
                pltpu.VMEM((rows, cols), jnp.bfloat16),
            ],
        ),
        out_shape=[jax.ShapeDtypeStruct(g, jnp.float32) for g in grad_shapes]
        + [jax.ShapeDtypeStruct((rows // patch, EXT), jnp.float32)],
        compiler_params=params(),
        cost_estimate=pl.CostEstimate(
            flops=4 * rows * width * cols, bytes_accessed=20 * 2**20, transcendentals=0
        ),
        name="head_terms",
    )(scalars, *rows_by_place, head_weight, teacher, row_info, *([before] if last else []))


def quantize(part):
    top = jnp.max(jnp.abs(part), axis=-1, keepdims=True)
    exp = jnp.ceil(jnp.log(jnp.maximum(top, 2.0**-100)) * 1.4426950408889634)
    codes = jnp.floor(part * jnp.exp2(14.0 - exp) + 0.5).astype(jnp.int32)
    return codes.astype(jnp.int16), exp


def widen(codes):
    return codes.astype(jnp.int32).astype(jnp.float32)


def add_and_code(own_x, keep, received):
    rows, cols = keep.shape
    block = rows // N_X
    order = (2, 1, 3, 0)

    def kernel(sc, a, b, *outs):
        codes, exp = quantize(a[...] + b[...])
        exp = jnp.broadcast_to(exp, (block, EXT)).astype(jnp.int32).astype(jnp.int16)
        for k, ahead in enumerate(order):

            @pl.when(pl.program_id(0) == k)
            def _():
                outs[ahead][:, :cols] = codes
                outs[ahead][:, cols:] = exp

    def block_of(i, s):
        ahead = jnp.where(i == 0, order[0], jnp.where(i == 1, order[1], jnp.where(i == 2, order[2], order[3])))
        return (lax.rem(s[0] + ahead, N_X), 0)

    spec = pl.BlockSpec((block, cols), block_of)
    return pl.pallas_call(
        kernel,
        grid_spec=pltpu.PrefetchScalarGridSpec(
            num_scalar_prefetch=1,
            grid=(N_X,),
            in_specs=[spec, spec],
            out_specs=[pl.BlockSpec((block, cols + EXT), lambda i, s: (0, 0))] * N_X,
        ),
        out_shape=[jax.ShapeDtypeStruct((block, cols + EXT), jnp.int16)] * N_X,
        compiler_params=params(),
        name="add_and_code",
    )(own_x[None].astype(jnp.int32), keep, received)


def sum_codes(src, n, cols):
    total = 0.0
    for k in range(n):
        total = total + widen(src[k][:, :cols]) * jnp.exp2(widen(src[k][:, cols:])[:, EXT - 1 :] - 14.0)
    return total


def sum_and_code(blocks, losses):
    n = len(blocks)
    rows, wide = blocks[0].shape
    cols = wide - EXT
    block = 32

    def kernel(*refs):
        src, loss_ref, out = refs[:n], refs[n], refs[n + 1]
        out[:, :cols], exp = quantize(sum_codes(src, n, cols))
        loss = loss_ref[...]
        loss_code, loss_exp = quantize(loss)
        lane = lax.broadcasted_iota(jnp.int32, loss.shape, 1)
        extra = jnp.where(lane == EXT - 2, loss_exp, widen(loss_code))
        extra = jnp.where(lane == EXT - 1, exp, extra)
        out[:, cols:] = extra.astype(jnp.int32).astype(jnp.int16)

    spec = lambda c: pl.BlockSpec((block, c), lambda i: (i, 0))
    return pl.pallas_call(
        kernel,
        grid=(rows // block,),
        in_specs=[spec(wide)] * n + [spec(EXT)],
        out_specs=spec(wide),
        out_shape=jax.ShapeDtypeStruct((rows, wide), jnp.int16),
        compiler_params=params(),
        name="sum_and_code",
    )(*blocks, losses)


def sum_blocks(received):
    n, rows, wide = received.shape
    cols = wide - EXT

    def kernel(src, out, ext):
        out[...] = sum_codes([src[k] for k in range(n)], n, cols)
        total = 0.0
        for k in range(n):
            extra = widen(src[k, :, cols:])
            total = total + extra * jnp.exp2(extra[:, EXT - 2 : EXT - 1] - 14.0)
        ext[...] = total

    return pl.pallas_call(
        kernel,
        out_shape=[
            jax.ShapeDtypeStruct((rows, cols), jnp.float32),
            jax.ShapeDtypeStruct((rows, EXT), jnp.float32),
        ],
        compiler_params=params(),
        name="sum_blocks",
    )(received)


def local(
    student_feats,
    head_weight,
    teacher_cache,
    holder_index,
    valid_count,
    image_embed,
    text_embed,
    pair_ids,
):
    n_dp = lax.axis_size("dp")
    n_cache = lax.axis_size("cache")
    own_index = lax.axis_index("dp")
    cache_pos = lax.axis_index("cache")
    core = own_index % N_CORE
    img_dev, patch_rows, student_width = student_feats.shape
    slots, _, local_cols = teacher_cache.shape
    full_cols = local_cols * n_cache
    part = student_width // n_cache
    shard_rows, embed = image_embed.shape
    assert slots == n_dp and n_dp == N_X * N_Z * N_CORE

    def ring(x, step):
        return lax.ppermute(x, "cache", [(i, (i + step) % n_cache) for i in range(n_cache)])

    def flat(x):
        return x.reshape(-1, x.shape[-1])

    img_order = jnp.arange(img_dev, dtype=jnp.int32)
    own_holders = lax.dynamic_slice_in_dim(holder_index, own_index * img_dev, img_dev, 0)
    dp_order = jnp.arange(n_dp, dtype=jnp.int32)
    image_of = jnp.sum(
        jnp.where(own_holders[None, :] == dp_order[:, None], img_order[None, :], 0), axis=1
    )
    outgoing = dispatch_rows(student_feats, image_of, cache_pos, part)

    def swap(x, bit):
        return lax.ppermute(x, "dp", [(i, i ^ bit) for i in range(n_dp)])

    def both(x, bit):
        other = swap(x, bit)
        upper = (own_index // bit) % 2 == 1
        return jnp.concatenate([jnp.where(upper, other, x), jnp.where(upper, x, other)])

    with jax.named_scope("texts"):
        counts_line = jnp.zeros((shard_rows, EXT), jnp.bfloat16).at[0, :img_dev].set(
            valid_count.astype(jnp.bfloat16)
        )
        texts = both(jnp.concatenate([text_embed, counts_line], axis=1), 2)
        outgoing, texts, teacher_in = lax.optimization_barrier((outgoing, texts, teacher_cache))
        for bit in (4, 8):
            texts = both(texts, bit)

    with jax.named_scope("student_exchange"):
        mine = lax.all_to_all(outgoing, "dp", split_axis=0, concat_axis=0, tiled=True)
    mine, texts = lax.optimization_barrier((mine, texts))
    chunk = n_dp // 2
    chunks = []
    with jax.named_scope("student_ring"):
        for first in range(0, n_dp, chunk):
            own = mine[first : first + chunk]
            if chunks:
                own = lax.optimization_barrier((own, far_a, far_b))[0]
            from_prev = ring(own, 1)
            from_next = ring(own, -1)
            if chunks:
                break
            far_a = ring(from_prev[: chunk // 2], 1)
            far_b = ring(from_next[chunk // 2 :], -1)
            chunks.append([flat(x) for x in (own, from_prev, from_next, far_a, far_b)])

    with jax.named_scope("teacher_sums"):
        wide = teacher_in.astype(jnp.float32)
        sums = jnp.stack([jnp.sum(wide, axis=-1), jnp.sum(wide * wide, axis=-1)])
        pair_cols = jnp.concatenate(
            [
                (pair_ids // 64)[:, None],
                (pair_ids % 64)[:, None],
                jnp.zeros((shard_rows, EXT - 2), jnp.int32),
            ],
            axis=1,
        ).astype(jnp.float32)
        images = jnp.concatenate([image_embed.astype(jnp.float32), pair_cols], axis=1)
        packed = jnp.concatenate([sums.reshape(-1, EXT), images.reshape(-1, EXT)])
        packed = [packed] + [ring(packed, step) for step in range(1, n_cache)]
        n_sum = sums.size // EXT
        sums = sum(p[:n_sum] for p in packed).reshape(sums.shape)
        images = jnp.concatenate([p[n_sum:] for p in packed]).reshape(img_dev, embed + EXT)
    with jax.named_scope("texts"):
        for bit in (2 * N_Z, 4 * N_Z, 1):
            texts = both(texts, bit)
        counts_all = (
            texts.reshape(N_CORE, N_X, N_Z, shard_rows, embed + EXT)[:, :, :, 0, embed : embed + img_dev]
            .transpose(1, 2, 0, 3)
            .reshape(n_dp, img_dev)
        )
    with jax.named_scope("teacher_sums"):
        row_mean = sums[0] / full_cols
        inv_scale = lax.rsqrt(sums[1] / full_cols - row_mean * row_mean + eps)

    is_held = holder_index.reshape(n_dp, img_dev) == own_index
    place_of = jnp.sum(jnp.where(is_held, img_order[None, :], 0), axis=1)
    held_count = jnp.sum(jnp.where(is_held, counts_all.astype(jnp.float32), 0.0), axis=1)
    row_index = jnp.arange(patch_rows, dtype=jnp.int32).astype(jnp.float32)
    valid_mask = (row_index[None, :] < held_count[:, None]).astype(jnp.float32)
    row_weight = valid_mask / jnp.maximum(held_count, 1.0)[:, None]
    coef = 2.0 * loss_scale / full_cols * row_weight
    inv_scale = jnp.where(held_count[:, None] > 0, inv_scale, 0.0)
    row_info = jnp.stack([row_mean, inv_scale, coef, row_weight], axis=-1).reshape(
        n_dp * patch_rows, 4
    )

    scalars = jnp.stack([cache_pos, core]).astype(jnp.int32)
    before, r_first = head_terms(
        scalars, chunks[0], head_weight, flat(teacher_cache), row_info, 0, full_cols
    )
    with jax.named_scope("student_ring"):
        from_prev, from_next, before, images, texts = lax.optimization_barrier(
            (from_prev, from_next, before, images, texts)
        )
        far_a = ring(from_prev[: chunk // 2], 1)
        far_b = ring(from_next[chunk // 2 :], -1)
        second = [flat(x) for x in (own, from_prev, from_next, far_a, far_b)]
    with jax.named_scope("contrast"):
        pairs = images[:, embed].astype(jnp.int32) * 64 + images[:, embed + 1].astype(jnp.int32)
        logits = jnp.dot(
            images[:, :embed].astype(jnp.bfloat16),
            texts[:, :embed].T,
            preferred_element_type=jnp.float32,
        ) * (embed ** (-0.5))
        column = jnp.arange(texts.shape[0], dtype=jnp.int32)
        text_row, text_z = column % shard_rows, column // shard_rows % N_Z
        text_x = column // (shard_rows * N_Z) % N_X
        text_core = column // (shard_rows * N_Z * N_X)
        text_dp = (text_x * N_Z + text_z) * N_CORE + text_core
        text_id = text_dp * img_dev + cache_pos * shard_rows + text_row
        best = jnp.max(logits, axis=1)
        denom = jnp.sum(jnp.exp(logits - best[:, None]), axis=1)
        target = jnp.sum(jnp.where(pairs[:, None] == text_id[None, :], logits, 0.0), axis=1)
        partial = jnp.pad(jnp.stack([best, denom, target]), ((0, 5), (0, EXT - img_dev)))
        second[0], partial = lax.optimization_barrier((second[0], partial))
    keep, send, r_second = head_terms(
        scalars,
        second,
        head_weight,
        flat(teacher_cache),
        row_info,
        chunk * patch_rows,
        full_cols,
        before,
    )
    with jax.named_scope("grad_core"):
        received = swap(send, 1)
    with jax.named_scope("image_sums"):
        r = jnp.concatenate([r_first, r_second, partial])
        r = [r] + [ring(r, step) for step in range(1, n_cache)]
        partials = []
        for k, got in enumerate(r):
            first = (n_cache - k) % n_cache * shard_rows
            partials.append(got[n_dp : n_dp + 3, first : first + shard_rows])
        r = sum(got[:n_dp] for got in r)
    own_x = own_index // (N_Z * N_CORE)

    def to_x(x, step):
        stride = N_Z * N_CORE
        return lax.ppermute(x, "dp", [(i, (i + step * stride) % n_dp) for i in range(n_dp)])

    own_codes, *codes = add_and_code(own_x, keep, received)
    with jax.named_scope("grad_x"):
        far_codes = to_x(codes[1], 2)
        blocks = [own_codes, to_x(codes[0], 1), far_codes, to_x(codes[2], 3)]
    r = lax.optimization_barrier((r, *codes))[0]
    with jax.named_scope("image_sums"):
        other_r = swap(r, 1)
        other_held = holder_index.reshape(n_dp, img_dev) == (own_index ^ 1)
        other_place = jnp.sum(jnp.where(other_held, img_order[None, :], 0), axis=1)
        lane = jnp.arange(EXT, dtype=jnp.int32)[None, :]
        losses = jnp.where(lane == place_of[:, None], r, 0.0) + jnp.where(
            lane == other_place[:, None], other_r, 0.0
        )
        losses = losses.reshape(N_X, N_Z, N_CORE, EXT)
        losses = jnp.where(core == 0, losses[:, :, 0], losses[:, :, 1])

        def for_x(step):
            return lax.dynamic_index_in_dim(losses, (own_x + step) % N_X, 0, keepdims=False)

        total = for_x(0)
        for step in range(1, N_X):
            total = total + to_x(for_x(step), step)
        owner_rows = student_width // n_dp
        losses = jnp.zeros((N_Z, owner_rows, EXT), jnp.float32).at[:, 0].set(total)
        losses = losses.reshape(N_Z * owner_rows, EXT)
    codes = sum_and_code(blocks, losses)
    with jax.named_scope("contrast"):
        partials = jnp.stack(partials)
        best = jnp.max(partials[:, 0], axis=0)
        denom = jnp.sum(partials[:, 1] * jnp.exp(partials[:, 0] - best[None, :]), axis=0)
        contrast = best + jnp.log(denom) - jnp.sum(partials[:, 2], axis=0)
    with jax.named_scope("grad_z"):
        codes = lax.all_to_all(
            codes.reshape(N_Z, -1, local_cols + EXT), "dp", 0, 0, axis_index_groups=Z_GROUPS, tiled=True
        )
    head_grad, extra = sum_blocks(codes)

    regress = lax.dynamic_slice_in_dim(extra[0], cache_pos * shard_rows, shard_rows, 0)
    image_loss = regress + contrast
    return (head_grad, image_loss)


def solution(mesh):
    in_specs = (
        P("dp", None, None),
        P(None, "cache"),
        P("dp", None, "cache"),
        P(),
        P("dp"),
        P(("dp", "cache"), None),
        P(("dp", "cache"), None),
        P(("dp", "cache")),
    )
    out_specs = (P("dp", "cache"), P(("dp", "cache")))
    return jax.shard_map(local, mesh=mesh, in_specs=in_specs, out_specs=out_specs, check_vma=False)
```

```python
import jax
import jax.numpy as jnp
from jax import lax
from jax.experimental import pallas as pl
from jax.experimental.pallas import tpu as pltpu
from jax.sharding import PartitionSpec as P

eps = 1e-06
loss_scale = 128.0

N_X, N_Z, N_CORE = 4, 8, 2
EXT = 128
VMEM_BYTES = 60 * 1024 * 1024

Z_GROUPS = [
    [(x * N_Z + z) * N_CORE + c for z in range(N_Z)] for x in range(N_X) for c in range(N_CORE)
]


def params():
    return pltpu.CompilerParams(vmem_limit_bytes=VMEM_BYTES)


LANES = 128
COUNT_ROWS = 8


def dispatch_rows(student_feats, image_of, count_of, cache_pos, cols):
    n_dp = image_of.shape[0]
    images, rows, _ = student_feats.shape
    parts = cols // LANES

    def kernel(scalars, feats, out):
        for h in range(n_dp):
            block = feats[scalars[h]]
            for k in range(parts):
                out[h, k * rows : (k + 1) * rows, :] = block[:, k * LANES : (k + 1) * LANES]
            count = jnp.full((COUNT_ROWS, LANES), scalars[n_dp + h].astype(jnp.float32))
            out[h, parts * rows :, :] = count.astype(out.dtype)

    scalars = jnp.concatenate([image_of, count_of, cache_pos[None]]).astype(jnp.int32)
    out_rows = parts * rows + COUNT_ROWS
    return pl.pallas_call(
        kernel,
        grid_spec=pltpu.PrefetchScalarGridSpec(
            num_scalar_prefetch=1,
            grid=(1,),
            in_specs=[pl.BlockSpec((images, rows, cols), lambda i, s: (0, 0, s[2 * n_dp]))],
            out_specs=pl.BlockSpec((n_dp, out_rows, LANES), lambda i, s: (0, 0, 0)),
        ),
        out_shape=jax.ShapeDtypeStruct((n_dp, out_rows, LANES), student_feats.dtype),
        compiler_params=params(),
        name="dispatch_rows",
    )(scalars, student_feats)


OUTER = (((0,), (0,)), ((), ()))


def head_terms(scalars, rows_by_place, head_weight, teacher, row_info, full_cols):
    n_img, split_rows, lanes = rows_by_place[0].shape
    width, cols = head_weight.shape
    block, tile, patch = 512, 256, 32
    splits = split_rows // patch
    part = splits * lanes
    rows = n_img * patch
    n_part = width // part
    steps, tiles = rows // block, cols // tile
    half = steps // 2
    img_block = block // patch
    pairs = N_X * N_Z
    owner_rows = width // (pairs * N_CORE)
    out_rows = width // N_CORE

    def kernel(sc, x0, x1, x2, x3a, x3b, w_ref, t_ref, info_ref, keep, send, x_scr, g_scr, r_scr):
        step = pl.program_id(0)

        @pl.when(step < steps)
        def _():
            here = pl.ds(pl.multiple_of(step * block, block), block)
            far = jnp.where(step < half, x3a[...], x3b[...])
            xs = [x0[...], x1[...], x2[...], far]
            for x, off in zip(xs, (0, n_part - 1, 1, 2)):
                first = lax.rem(sc[0] + off, n_part) * part
                for k in range(splits):
                    x_scr[here, pl.ds(pl.multiple_of(first + k * lanes, lanes), lanes)] = x[
                        :, k * patch : (k + 1) * patch, :
                    ].reshape(block, lanes)
            pred = jnp.dot(x_scr[here, :], w_ref[...], preferred_element_type=jnp.float32)
            info = info_ref[...]
            mean, inv, coef, weight = (info[:, k : k + 1] for k in range(4))
            residue = pred - (t_ref[...].astype(jnp.float32) - mean) * inv
            g_scr[here, :] = (coef * residue).astype(jnp.bfloat16)
            row_loss = weight * jnp.sum(residue * residue, axis=-1, keepdims=True)
            row_loss = jnp.broadcast_to(row_loss, (block, EXT)).reshape(img_block, patch, EXT)
            r_scr[pl.ds(pl.multiple_of(step * img_block, img_block), img_block), :] = (
                jnp.sum(row_loss, axis=1) / full_cols
            )

        @pl.when((step >= steps) & (step < steps + tiles))
        def _():
            first = pl.multiple_of((step - steps) * tile, tile)
            term = lax.dot_general(
                x_scr[...], g_scr[:, pl.ds(first, tile)], OUTER, preferred_element_type=jnp.float32
            )
            term = term.reshape(pairs, N_CORE, owner_rows, tile)
            for mine, (one, two) in enumerate(((keep, send), (send, keep))):

                @pl.when(sc[1] == mine)
                def _():
                    one[...] = term[:, 0].reshape(out_rows, tile)
                    two[...] = term[:, 1].reshape(out_rows, tile)

        @pl.when(step == steps + tiles)
        def _():
            lane = lax.broadcasted_iota(jnp.int32, (1, EXT), 1)
            top = lax.broadcasted_iota(jnp.int32, (owner_rows, EXT), 0) == 0
            for ref, own in ((keep, sc[1]), (send, 1 - sc[1])):
                ref[...] = jnp.zeros_like(ref)
                for pair in range(pairs):
                    image = pair * N_CORE + own
                    line = jnp.where(lane == sc[2 + image], r_scr[pl.ds(image, 1), :], 0.0)
                    ref[pair * owner_rows : (pair + 1) * owner_rows, :EXT] = jnp.where(top, line, 0.0)

    row_at = lambda i: jnp.minimum(i, steps - 1)
    row_spec = lambda c: pl.BlockSpec((block, c), lambda i, s: (row_at(i), 0))
    img_spec = lambda f: pl.BlockSpec((img_block, split_rows, lanes), lambda i, s: (f(i), 0, 0))
    far_spec = lambda f: img_spec(lambda i: jnp.clip(f(i), 0, half - 1))
    out_spec = pl.BlockSpec((out_rows, tile), lambda i, s: (0, jnp.maximum(i - steps, 0)))
    out = jax.ShapeDtypeStruct((out_rows, cols + tile), jnp.float32)
    return pl.pallas_call(
        kernel,
        grid_spec=pltpu.PrefetchScalarGridSpec(
            num_scalar_prefetch=1,
            grid=(steps + tiles + 1,),
            in_specs=[
                img_spec(row_at),
                img_spec(row_at),
                img_spec(row_at),
                far_spec(lambda i: i),
                far_spec(lambda i: i - half),
                pl.BlockSpec((width, cols), lambda i, s: (0, 0)),
                row_spec(cols),
                row_spec(row_info.shape[1]),
            ],
            out_specs=[out_spec, out_spec],
            scratch_shapes=[
                pltpu.VMEM((rows, width), jnp.bfloat16),
                pltpu.VMEM((rows, cols), jnp.bfloat16),
                pltpu.VMEM((n_img, EXT), jnp.float32),
            ],
        ),
        out_shape=[out, out],
        compiler_params=params(),
        cost_estimate=pl.CostEstimate(
            flops=4 * rows * width * cols, bytes_accessed=25 * 2**20, transcendentals=0
        ),
        name="head_terms",
    )(scalars, *rows_by_place, head_weight, teacher, row_info)


def exponent(part):
    top = jnp.max(jnp.abs(part), axis=-1, keepdims=True)
    return jnp.ceil(jnp.log(jnp.maximum(top, 2.0**-100)) * 1.4426950408889634)


def code(main, extra):
    main_exp, extra_exp = exponent(main), exponent(extra)
    main_code = jnp.floor(main * jnp.exp2(14.0 - main_exp) + 0.5).astype(jnp.int32)
    extra_code = jnp.floor(extra * jnp.exp2(14.0 - extra_exp) + 0.5)
    lane = lax.broadcasted_iota(jnp.int32, extra.shape, 1)
    extra_code = jnp.where(
        lane == EXT - 2, main_exp, jnp.where(lane == EXT - 1, extra_exp, extra_code)
    ).astype(jnp.int32)
    return main_code.astype(jnp.int16), extra_code.astype(jnp.int16)


def decode(codes):
    cols = codes.shape[-1] - EXT
    wide = codes.astype(jnp.int32).astype(jnp.float32)
    main, extra = wide[:, :cols], wide[:, cols:]
    main_exp = extra[:, EXT - 2 : EXT - 1]
    extra_exp = extra[:, EXT - 1 :]
    lane = lax.broadcasted_iota(jnp.int32, extra.shape, 1)
    extra = jnp.where(lane < EXT - 2, extra, 0.0)
    return main * jnp.exp2(main_exp - 14.0), extra * jnp.exp2(extra_exp - 14.0)


def add_and_code(own_x, keep, received):
    rows, wide = keep.shape
    cols = wide - 2 * EXT
    block = rows // N_X
    order = (2, 1, 3, 0)

    def kernel(sc, a, b, *outs):
        main, extra = code(a[:, :cols] + b[:, :cols], a[:, cols : cols + EXT] + b[:, cols : cols + EXT])
        for k, ahead in enumerate(order):

            @pl.when(pl.program_id(0) == k)
            def _():
                outs[ahead][:, :cols] = main
                outs[ahead][:, cols:] = extra

    def block_of(i, s):
        ahead = jnp.where(i == 0, order[0], jnp.where(i == 1, order[1], jnp.where(i == 2, order[2], order[3])))
        return (lax.rem(s[0] + ahead, N_X), 0)

    spec = pl.BlockSpec((block, wide), block_of)
    return pl.pallas_call(
        kernel,
        grid_spec=pltpu.PrefetchScalarGridSpec(
            num_scalar_prefetch=1,
            grid=(N_X,),
            in_specs=[spec, spec],
            out_specs=[pl.BlockSpec((block, cols + EXT), lambda i, s: (0, 0))] * N_X,
        ),
        out_shape=[jax.ShapeDtypeStruct((block, cols + EXT), jnp.int16)] * N_X,
        compiler_params=params(),
        name="add_and_code",
    )(own_x[None].astype(jnp.int32), keep, received)


def sum_blocks(blocks):
    main, extra = decode(blocks[0])
    for block in blocks[1:]:
        m, e = decode(block)
        main, extra = main + m, extra + e
    return main, extra


def sum_and_code(blocks):
    rows, wide = blocks[0].shape
    cols = wide - EXT
    block = 32

    def kernel(*refs):
        *src, out = refs
        main, extra = code(*sum_blocks([ref[...] for ref in src]))
        out[:, :cols] = main
        out[:, cols:] = extra

    spec = pl.BlockSpec((block, wide), lambda i: (i, 0))
    return pl.pallas_call(
        kernel,
        grid=(rows // block,),
        in_specs=[spec] * len(blocks),
        out_specs=spec,
        out_shape=jax.ShapeDtypeStruct((rows, wide), jnp.int16),
        compiler_params=params(),
        name="sum_and_code",
    )(*blocks)


def sum_last(received):
    n, rows, wide = received.shape

    def kernel(src, out, ext):
        main, extra = sum_blocks([src[k] for k in range(n)])
        out[...] = main
        ext[...] = extra

    return pl.pallas_call(
        kernel,
        out_shape=[
            jax.ShapeDtypeStruct((rows, wide - EXT), jnp.float32),
            jax.ShapeDtypeStruct((rows, EXT), jnp.float32),
        ],
        compiler_params=params(),
        name="sum_last",
    )(received)


def local(
    student_feats,
    head_weight,
    teacher_cache,
    holder_index,
    valid_count,
    image_embed,
    text_embed,
    pair_ids,
):
    n_dp = lax.axis_size("dp")
    n_cache = lax.axis_size("cache")
    own_index = lax.axis_index("dp")
    cache_pos = lax.axis_index("cache")
    core = own_index % N_CORE
    img_dev, patch_rows, student_width = student_feats.shape
    slots, _, local_cols = teacher_cache.shape
    full_cols = local_cols * n_cache
    part = student_width // n_cache
    shard_rows, embed = image_embed.shape
    assert slots == n_dp and n_dp == N_X * N_Z * N_CORE

    def ring(x, step):
        return lax.ppermute(x, "cache", [(i, (i + step) % n_cache) for i in range(n_cache)])

    def flat(x):
        return x.reshape(-1, x.shape[-1])

    img_order = jnp.arange(img_dev, dtype=jnp.int32)
    own_holders = lax.dynamic_slice_in_dim(holder_index, own_index * img_dev, img_dev, 0)
    dp_order = jnp.arange(n_dp, dtype=jnp.int32)
    image_of = jnp.sum(
        jnp.where(own_holders[None, :] == dp_order[:, None], img_order[None, :], 0), axis=1
    )
    count_of = jnp.sum(
        jnp.where(own_holders[None, :] == dp_order[:, None], valid_count[None, :], 0), axis=1
    )
    outgoing = dispatch_rows(student_feats, image_of, count_of, cache_pos, part)

    def swap(x, bit):
        return lax.ppermute(x, "dp", [(i, i ^ bit) for i in range(n_dp)])

    def both(x, bit):
        other = swap(x, bit)
        upper = (own_index // bit) % 2 == 1
        return jnp.concatenate([jnp.where(upper, other, x), jnp.where(upper, x, other)])

    texts = both(text_embed, 2)
    outgoing, texts, teacher_in = lax.optimization_barrier((outgoing, texts, teacher_cache))

    with jax.named_scope("student_exchange"):
        mine = lax.all_to_all(outgoing, "dp", split_axis=0, concat_axis=0, tiled=True)
    with jax.named_scope("teacher_sums"):
        wide = teacher_in.astype(jnp.float32)
        sums = jnp.stack([jnp.sum(wide, axis=-1), jnp.sum(wide * wide, axis=-1)])
        pair_cols = jnp.concatenate(
            [
                (pair_ids // 64)[:, None],
                (pair_ids % 64)[:, None],
                jnp.zeros((shard_rows, EXT - 2), jnp.int32),
            ],
            axis=1,
        ).astype(jnp.float32)
        images = jnp.concatenate([image_embed.astype(jnp.float32), pair_cols], axis=1)
        packed = jnp.concatenate([sums.reshape(-1, EXT), images.reshape(-1, EXT)])
        packed = [packed] + [ring(packed, step) for step in range(1, n_cache)]
        n_sum = sums.size // EXT
        sums = sum(p[:n_sum] for p in packed).reshape(sums.shape)
        images = jnp.concatenate([p[n_sum:] for p in packed]).reshape(img_dev, embed + EXT)
    texts = both(texts, 4)
    mine, sums, images, texts = lax.optimization_barrier((mine, sums, images, texts))
    with jax.named_scope("student_ring"):
        counts_sent, mine = mine[:, -COUNT_ROWS:], mine[:, :-COUNT_ROWS]
        from_prev = ring(mine, 1)
        from_next = ring(mine, -1)
        from_prev, from_next, sums, counts_sent = lax.optimization_barrier(
            (from_prev, from_next, sums, counts_sent)
        )
        far_a = ring(from_prev[: n_dp // 2], 1)
        far_b = ring(from_next[n_dp // 2 :], -1)
    with jax.named_scope("teacher_sums"):
        row_mean = sums[0] / full_cols
        inv_scale = lax.rsqrt(sums[1] / full_cols - row_mean * row_mean + eps)

    is_held = holder_index.reshape(n_dp, img_dev) == own_index
    place_of = jnp.sum(jnp.where(is_held, img_order[None, :], 0), axis=1)
    held_any = jnp.sum(is_held.astype(jnp.int32), axis=1) > 0
    held_count = jnp.where(held_any, counts_sent[:, 0, 0].astype(jnp.float32), 0.0)
    row_index = jnp.arange(patch_rows, dtype=jnp.int32).astype(jnp.float32)
    valid_mask = (row_index[None, :] < held_count[:, None]).astype(jnp.float32)
    row_weight = valid_mask / jnp.maximum(held_count, 1.0)[:, None]
    coef = 2.0 * loss_scale / full_cols * row_weight
    inv_scale = jnp.where(held_count[:, None] > 0, inv_scale, 0.0)
    row_info = jnp.stack([row_mean, inv_scale, coef, row_weight], axis=-1).reshape(
        n_dp * patch_rows, 4
    )

    scalars = jnp.concatenate([jnp.stack([cache_pos, core]).astype(jnp.int32), place_of])
    far_a, far_b, texts = lax.optimization_barrier((far_a, far_b, texts))
    texts = both(texts, 8)
    keep, send = head_terms(
        scalars,
        [mine, from_prev, from_next, far_a, far_b],
        head_weight,
        flat(teacher_cache),
        row_info,
        full_cols,
    )
    keep, send, texts = lax.optimization_barrier((keep, send, texts))
    with jax.named_scope("grad_core"):
        received = swap(send, 1)
    texts = both(texts, 2 * N_Z)
    own_x = own_index // (N_Z * N_CORE)
    codes = add_and_code(own_x, keep, received)
    with jax.named_scope("grad_x"):
        blocks = [codes[0]] + [
            lax.ppermute(
                codes[step], "dp", [(i, (i + step * N_Z * N_CORE) % n_dp) for i in range(n_dp)]
            )
            for step in (2, 1, 3)
        ]
    texts = lax.optimization_barrier((texts, *codes))[0]
    texts = both(texts, 4 * N_Z)
    codes = sum_and_code(blocks)
    codes, images, texts = lax.optimization_barrier((codes, images, texts))
    texts = both(texts, 1)
    with jax.named_scope("contrast"):
        pairs = images[:, embed].astype(jnp.int32) * 64 + images[:, embed + 1].astype(jnp.int32)
        logits = jnp.dot(
            images[:, :embed].astype(jnp.bfloat16),
            texts.T,
            preferred_element_type=jnp.float32,
        ) * (embed ** (-0.5))
        column = jnp.arange(texts.shape[0], dtype=jnp.int32)
        text_row, text_z = column % shard_rows, column // shard_rows % N_Z
        text_x = column // (shard_rows * N_Z) % N_X
        text_core = column // (shard_rows * N_Z * N_X)
        text_dp = (text_x * N_Z + text_z) * N_CORE + text_core
        text_id = text_dp * img_dev + cache_pos * shard_rows + text_row
        best = jnp.max(logits, axis=1)
        denom = jnp.sum(jnp.exp(logits - best[:, None]), axis=1)
        target = jnp.sum(jnp.where(pairs[:, None] == text_id[None, :], logits, 0.0), axis=1)
        partial = jnp.pad(jnp.stack([best, denom, target]), ((0, 5), (0, EXT - img_dev)))
    with jax.named_scope("grad_z"):
        codes = lax.all_to_all(
            codes.reshape(N_Z, -1, local_cols + EXT), "dp", 0, 0, axis_index_groups=Z_GROUPS, tiled=True
        )
    head_grad, extra = sum_last(codes)

    with jax.named_scope("loss_parts"):
        parts = jnp.concatenate([partial[:3], extra[:1], partial[4:]])
        parts = [parts] + [ring(parts, step) for step in range(1, n_cache)]
        partials = []
        for k, got in enumerate(parts):
            first = (n_cache - k) % n_cache * shard_rows
            partials.append(got[:3, first : first + shard_rows])
        partials = jnp.stack(partials)
        best = jnp.max(partials[:, 0], axis=0)
        denom = jnp.sum(partials[:, 1] * jnp.exp(partials[:, 0] - best[None, :]), axis=0)
        contrast = best + jnp.log(denom) - jnp.sum(partials[:, 2], axis=0)
        regress = sum(got[3] for got in parts)
        regress = lax.dynamic_slice_in_dim(regress, cache_pos * shard_rows, shard_rows, 0)
    return (head_grad, regress + contrast)


def solution(mesh):
    in_specs = (
        P("dp", None, None),
        P(None, "cache"),
        P("dp", None, "cache"),
        P(),
        P("dp"),
        P(("dp", "cache"), None),
        P(("dp", "cache"), None),
        P(("dp", "cache")),
    )
    out_specs = (P("dp", "cache"), P(("dp", "cache")))
    return jax.shard_map(local, mesh=mesh, in_specs=in_specs, out_specs=out_specs, check_vma=False)
```

```python
import jax
import jax.numpy as jnp
from jax import lax
from jax.experimental import pallas as pl
from jax.experimental.pallas import tpu as pltpu
from jax.sharding import PartitionSpec as P

eps = 1e-06
loss_scale = 128.0

N_X, N_Z, N_CORE = 4, 8, 2
EXT = 128
VMEM_BYTES = 60 * 1024 * 1024

XZ_GROUPS = [[k * N_CORE + c for k in range(N_X * N_Z)] for c in range(N_CORE)]


def params():
    return pltpu.CompilerParams(vmem_limit_bytes=VMEM_BYTES)


LANES = 128
COUNT_ROWS = 8


def dispatch_rows(student_feats, holder_index, valid_count, own_index, cache_pos, cols):
    images, rows, width = student_feats.shape
    n_dp = holder_index.shape[0] // images
    parts = cols // LANES

    def kernel(place, holders, counts, feats, out):
        out[...] = jnp.zeros_like(out)
        for i in range(images):
            h = holders[place[0] * images + i]
            for k in range(parts):
                out[h, k * rows : (k + 1) * rows, :] = feats[i, :, k * LANES : (k + 1) * LANES]
            count = jnp.full((COUNT_ROWS, LANES), counts[i].astype(jnp.float32))
            out[h, parts * rows :, :] = count.astype(out.dtype)

    out_rows = parts * rows + COUNT_ROWS
    return pl.pallas_call(
        kernel,
        grid_spec=pltpu.PrefetchScalarGridSpec(
            num_scalar_prefetch=3,
            grid=(1,),
            in_specs=[pl.BlockSpec((images, rows, cols), lambda i, p, h, c: (0, 0, p[1]))],
            out_specs=pl.BlockSpec((n_dp, out_rows, LANES), lambda i, p, h, c: (0, 0, 0)),
        ),
        out_shape=jax.ShapeDtypeStruct((n_dp, out_rows, LANES), student_feats.dtype),
        compiler_params=params(),
        name="dispatch_rows",
    )(jnp.stack([own_index, cache_pos]).astype(jnp.int32), holder_index, valid_count, student_feats)


def near_terms(cache_pos, near, head_weight):
    n_img, split_rows, lanes = near[0].shape
    width, cols = head_weight.shape
    block, patch = 512, 32
    splits = split_rows // patch
    part = splits * lanes
    n_part = width // part
    rows = n_img * patch
    img_block = block // patch

    def kernel(sc, x0, x1, x2, w_ref, pred_out, xt_out):
        xt_out[...] = jnp.zeros_like(xt_out)
        pred = jnp.zeros((block, cols), jnp.float32)
        for ref, off in ((x0, 0), (x1, n_part - 1), (x2, 1)):
            first = lax.rem(sc[0] + off, n_part) * part
            pieces = [
                ref[:, k * patch : (k + 1) * patch, :].reshape(block, lanes) for k in range(splits)
            ]
            for k, piece in enumerate(pieces):
                xt_out[pl.ds(pl.multiple_of(first + k * lanes, lanes), lanes), :] = piece.T
            pred = pred + jnp.dot(
                jnp.concatenate(pieces, axis=1),
                w_ref[pl.ds(pl.multiple_of(first, part), part), :],
                preferred_element_type=jnp.float32,
            )
        pred_out[...] = pred

    img_spec = pl.BlockSpec((img_block, split_rows, lanes), lambda i, s: (i, 0, 0))
    return pl.pallas_call(
        kernel,
        grid_spec=pltpu.PrefetchScalarGridSpec(
            num_scalar_prefetch=1,
            grid=(rows // block,),
            in_specs=[img_spec] * 3 + [pl.BlockSpec((width, cols), lambda i, s: (0, 0))],
            out_specs=[
                pl.BlockSpec((block, cols), lambda i, s: (i, 0)),
                pl.BlockSpec((width, block), lambda i, s: (0, i)),
            ],
        ),
        out_shape=[
            jax.ShapeDtypeStruct((rows, cols), jnp.float32),
            jax.ShapeDtypeStruct((width, rows), near[0].dtype),
        ],
        compiler_params=params(),
        cost_estimate=pl.CostEstimate(
            flops=2 * rows * 3 * part * cols, bytes_accessed=20 * 2**20, transcendentals=0
        ),
        name="near_terms",
    )(cache_pos[None].astype(jnp.int32), *near, head_weight)


def head_terms(scalars, near_pred, near_cols, far_a, far_b, head_weight, teacher, row_info, full_cols):
    half_img, split_rows, lanes = far_a.shape
    n_img = 2 * half_img
    width, cols = head_weight.shape
    block, tile, patch = 512, 256, 32
    splits = split_rows // patch
    part = splits * lanes
    rows = n_img * patch
    n_part = width // part
    steps, tiles = rows // block, cols // tile
    half = steps // 2
    img_block = block // patch
    pairs = N_X * N_Z
    owner_rows = width // (pairs * N_CORE)
    out_rows = width // N_CORE

    def kernel(sc, pred_ref, xt_ref, fa, fb, w_ref, t_ref, info_ref, keep, send, x_scr, g_scr, r_scr):
        step = pl.program_id(0)

        @pl.when(step < steps)
        def _():
            here = pl.ds(pl.multiple_of(step * block, block), block)
            far = jnp.where(step < half, fa[...], fb[...])
            pieces = [far[:, k * patch : (k + 1) * patch, :].reshape(block, lanes) for k in range(splits)]
            x_scr[:, here] = xt_ref[...]
            first = lax.rem(sc[0] + 2, n_part) * part
            for k, piece in enumerate(pieces):
                x_scr[pl.ds(pl.multiple_of(first + k * lanes, lanes), lanes), here] = piece.T
            pred = pred_ref[...] + jnp.dot(
                jnp.concatenate(pieces, axis=1), w_ref[...], preferred_element_type=jnp.float32
            )
            info = info_ref[...]
            mean, inv, coef, weight = (info[:, k : k + 1] for k in range(4))
            residue = pred - (t_ref[...].astype(jnp.float32) - mean) * inv
            g_scr[here, :] = (coef * residue).astype(jnp.bfloat16)
            row_loss = weight * jnp.sum(residue * residue, axis=-1, keepdims=True)
            row_loss = jnp.broadcast_to(row_loss, (block, EXT)).reshape(img_block, patch, EXT)
            r_scr[pl.ds(pl.multiple_of(step * img_block, img_block), img_block), :] = (
                jnp.sum(row_loss, axis=1) / full_cols
            )

        @pl.when((step >= steps) & (step < steps + tiles))
        def _():
            first = pl.multiple_of((step - steps) * tile, tile)
            term = jnp.dot(x_scr[...], g_scr[:, pl.ds(first, tile)], preferred_element_type=jnp.float32)
            term = term.reshape(pairs, N_CORE, owner_rows, tile)
            for mine, (one, two) in enumerate(((keep, send), (send, keep))):

                @pl.when(sc[1] == mine)
                def _():
                    one[...] = term[:, 0].reshape(out_rows, tile)
                    two[...] = term[:, 1].reshape(out_rows, tile)

        @pl.when(step == steps + tiles)
        def _():
            lane = lax.broadcasted_iota(jnp.int32, (1, EXT), 1)
            top = lax.broadcasted_iota(jnp.int32, (owner_rows, EXT), 0) == 0
            for ref, own in ((keep, sc[1]), (send, 1 - sc[1])):
                ref[...] = jnp.zeros_like(ref)
                for pair in range(pairs):
                    image = pair * N_CORE + own
                    line = jnp.where(lane == sc[2 + image], r_scr[pl.ds(image, 1), :], 0.0)
                    ref[pair * owner_rows : (pair + 1) * owner_rows, :EXT] = jnp.where(top, line, 0.0)

    row_at = lambda i: jnp.minimum(i, steps - 1)
    row_spec = lambda c: pl.BlockSpec((block, c), lambda i, s: (row_at(i), 0))
    far_spec = lambda f: pl.BlockSpec(
        (img_block, split_rows, lanes), lambda i, s: (jnp.clip(f(i), 0, half - 1), 0, 0)
    )
    out_spec = pl.BlockSpec((out_rows, tile), lambda i, s: (0, jnp.maximum(i - steps, 0)))
    out = jax.ShapeDtypeStruct((out_rows, cols + tile), jnp.float32)
    return pl.pallas_call(
        kernel,
        grid_spec=pltpu.PrefetchScalarGridSpec(
            num_scalar_prefetch=1,
            grid=(steps + tiles + 1,),
            in_specs=[
                row_spec(cols),
                pl.BlockSpec((width, block), lambda i, s: (0, row_at(i))),
                far_spec(lambda i: i),
                far_spec(lambda i: i - half),
                pl.BlockSpec((part, cols), lambda i, s: (lax.rem(s[0] + 2, n_part), 0)),
                row_spec(cols),
                row_spec(row_info.shape[1]),
            ],
            out_specs=[out_spec, out_spec],
            scratch_shapes=[
                pltpu.VMEM((width, rows), jnp.bfloat16),
                pltpu.VMEM((rows, cols), jnp.bfloat16),
                pltpu.VMEM((n_img, EXT), jnp.float32),
            ],
        ),
        out_shape=[out, out],
        compiler_params=params(),
        cost_estimate=pl.CostEstimate(
            flops=3 * rows * width * cols, bytes_accessed=30 * 2**20, transcendentals=0
        ),
        name="head_terms",
    )(scalars, near_pred, near_cols, far_a, far_b, head_weight, teacher, row_info)


def exponent(part):
    top = jnp.max(jnp.abs(part), axis=-1, keepdims=True)
    return jnp.ceil(jnp.log(jnp.maximum(top, 2.0**-100)) * 1.4426950408889634)


def code(main, extra):
    main_exp, extra_exp = exponent(main), exponent(extra)
    main_code = jnp.floor(main * jnp.exp2(14.0 - main_exp) + 0.5).astype(jnp.int32)
    extra_code = jnp.floor(extra * jnp.exp2(14.0 - extra_exp) + 0.5)
    lane = lax.broadcasted_iota(jnp.int32, extra.shape, 1)
    extra_code = jnp.where(
        lane == EXT - 2, main_exp, jnp.where(lane == EXT - 1, extra_exp, extra_code)
    ).astype(jnp.int32)
    return main_code.astype(jnp.int16), extra_code.astype(jnp.int16)


def decode(codes):
    cols = codes.shape[-1] - EXT
    wide = codes.astype(jnp.int32).astype(jnp.float32)
    main, extra = wide[:, :cols], wide[:, cols:]
    main_exp = extra[:, EXT - 2 : EXT - 1]
    extra_exp = extra[:, EXT - 1 :]
    lane = lax.broadcasted_iota(jnp.int32, extra.shape, 1)
    extra = jnp.where(lane < EXT - 2, extra, 0.0)
    return main * jnp.exp2(main_exp - 14.0), extra * jnp.exp2(extra_exp - 14.0)


def add_and_code(keep, received):
    rows, wide = keep.shape
    cols = wide - 2 * EXT
    block = rows // 4

    def kernel(a, b, out):
        main, extra = code(a[:, :cols] + b[:, :cols], a[:, cols : cols + EXT] + b[:, cols : cols + EXT])
        out[:, :cols] = main
        out[:, cols:] = extra

    spec = pl.BlockSpec((block, wide), lambda i: (i, 0))
    return pl.pallas_call(
        kernel,
        grid=(rows // block,),
        in_specs=[spec, spec],
        out_specs=pl.BlockSpec((block, cols + EXT), lambda i: (i, 0)),
        out_shape=jax.ShapeDtypeStruct((rows, cols + EXT), jnp.int16),
        compiler_params=params(),
        name="add_and_code",
    )(keep, received)


def sum_blocks(blocks):
    main, extra = decode(blocks[0])
    for block in blocks[1:]:
        m, e = decode(block)
        main, extra = main + m, extra + e
    return main, extra


def sum_last(received):
    n, rows, wide = received.shape

    def kernel(src, out, ext):
        main, extra = sum_blocks([src[k] for k in range(n)])
        out[...] = main
        ext[...] = extra

    return pl.pallas_call(
        kernel,
        out_shape=[
            jax.ShapeDtypeStruct((rows, wide - EXT), jnp.float32),
            jax.ShapeDtypeStruct((rows, EXT), jnp.float32),
        ],
        compiler_params=params(),
        name="sum_last",
    )(received)


def local(
    student_feats,
    head_weight,
    teacher_cache,
    holder_index,
    valid_count,
    image_embed,
    text_embed,
    pair_ids,
):
    n_dp = lax.axis_size("dp")
    n_cache = lax.axis_size("cache")
    own_index = lax.axis_index("dp")
    cache_pos = lax.axis_index("cache")
    core = own_index % N_CORE
    img_dev, patch_rows, student_width = student_feats.shape
    slots, _, local_cols = teacher_cache.shape
    full_cols = local_cols * n_cache
    part = student_width // n_cache
    shard_rows, embed = image_embed.shape
    assert slots == n_dp and n_dp == N_X * N_Z * N_CORE

    def ring(x, step):
        return lax.ppermute(x, "cache", [(i, (i + step) % n_cache) for i in range(n_cache)])

    def flat(x):
        return x.reshape(-1, x.shape[-1])

    img_order = jnp.arange(img_dev, dtype=jnp.int32)
    outgoing = dispatch_rows(student_feats, holder_index, valid_count, own_index, cache_pos, part)

    def swap(x, bit):
        return lax.ppermute(x, "dp", [(i, i ^ bit) for i in range(n_dp)])

    def both(x, bit):
        other = swap(x, bit)
        upper = (own_index // bit) % 2 == 1
        return jnp.concatenate([jnp.where(upper, other, x), jnp.where(upper, x, other)])

    def four(x, bit):
        low, high = (own_index // bit) % 2 == 1, (own_index // (2 * bit)) % 2 == 1
        a, b, c, d = x, swap(x, bit), swap(x, 2 * bit), swap(x, 3 * bit)
        a, b = jnp.where(low, b, a), jnp.where(low, a, b)
        c, d = jnp.where(low, d, c), jnp.where(low, c, d)
        a, c = jnp.where(high, c, a), jnp.where(high, a, c)
        b, d = jnp.where(high, d, b), jnp.where(high, b, d)
        return jnp.concatenate([a, b, c, d])

    outgoing, texts, teacher_in = lax.optimization_barrier((outgoing, text_embed, teacher_cache))

    with jax.named_scope("student_exchange"):
        mine = lax.all_to_all(outgoing, "dp", split_axis=0, concat_axis=0, tiled=True)
    with jax.named_scope("teacher_sums"):
        wide = teacher_in.astype(jnp.float32)
        sums = jnp.stack([jnp.sum(wide, axis=-1), jnp.sum(wide * wide, axis=-1)])
        pair_cols = jnp.concatenate(
            [
                (pair_ids // 64)[:, None],
                (pair_ids % 64)[:, None],
                jnp.zeros((shard_rows, EXT - 2), jnp.int32),
            ],
            axis=1,
        ).astype(jnp.float32)
        images = jnp.concatenate([image_embed.astype(jnp.float32), pair_cols], axis=1)
        packed = jnp.concatenate([sums.reshape(-1, EXT), images.reshape(-1, EXT)])
        packed = [packed] + [ring(packed, step) for step in range(1, n_cache)]
        n_sum = sums.size // EXT
        sums = sum(p[:n_sum] for p in packed).reshape(sums.shape)
        images = jnp.concatenate([p[n_sum:] for p in packed]).reshape(img_dev, embed + EXT)
    texts = four(both(texts, 1), 2)
    mine, sums, images, texts = lax.optimization_barrier((mine, sums, images, texts))
    with jax.named_scope("student_ring"):
        counts_sent, mine = mine[:, -COUNT_ROWS:], mine[:, :-COUNT_ROWS]
        from_prev = ring(mine, 1)
        from_next = ring(mine, -1)
        from_prev, from_next, sums, counts_sent = lax.optimization_barrier(
            (from_prev, from_next, sums, counts_sent)
        )
        far_a = ring(from_prev[: n_dp // 2], 1)
        far_b = ring(from_next[n_dp // 2 :], -1)
    near_pred, near_cols = near_terms(cache_pos, [mine, from_prev, from_next], head_weight)
    with jax.named_scope("teacher_sums"):
        row_mean = sums[0] / full_cols
        inv_scale = lax.rsqrt(sums[1] / full_cols - row_mean * row_mean + eps)

    is_held = holder_index.reshape(n_dp, img_dev) == own_index
    place_of = jnp.sum(jnp.where(is_held, img_order[None, :], 0), axis=1)
    held_any = jnp.sum(is_held.astype(jnp.int32), axis=1) > 0
    held_count = jnp.where(held_any, counts_sent[:, 0, 0].astype(jnp.float32), 0.0)
    row_index = jnp.arange(patch_rows, dtype=jnp.int32).astype(jnp.float32)
    valid_mask = (row_index[None, :] < held_count[:, None]).astype(jnp.float32)
    row_weight = valid_mask / jnp.maximum(held_count, 1.0)[:, None]
    coef = 2.0 * loss_scale / full_cols * row_weight
    inv_scale = jnp.where(held_count[:, None] > 0, inv_scale, 0.0)
    row_info = jnp.stack([row_mean, inv_scale, coef, row_weight], axis=-1).reshape(
        n_dp * patch_rows, 4
    )

    scalars = jnp.concatenate([jnp.stack([cache_pos, core]).astype(jnp.int32), place_of])
    far_a, far_b, texts = lax.optimization_barrier((far_a, far_b, texts))
    texts = both(texts, N_Z)
    keep, send = head_terms(
        scalars,
        near_pred,
        near_cols,
        far_a,
        far_b,
        head_weight,
        flat(teacher_cache),
        row_info,
        full_cols,
    )
    keep, send, texts = lax.optimization_barrier((keep, send, texts))
    with jax.named_scope("grad_core"):
        received = swap(send, 1)
    texts = both(texts, 2 * N_Z)
    codes = add_and_code(keep, received)
    codes, images, texts = lax.optimization_barrier((codes, images, texts))
    texts = both(texts, 4 * N_Z)
    with jax.named_scope("contrast"):
        pairs = images[:, embed].astype(jnp.int32) * 64 + images[:, embed + 1].astype(jnp.int32)
        logits = jnp.dot(
            images[:, :embed].astype(jnp.bfloat16),
            texts.T,
            preferred_element_type=jnp.float32,
        ) * (embed ** (-0.5))
        column = jnp.arange(texts.shape[0], dtype=jnp.int32)
        text_id = column // shard_rows * img_dev + cache_pos * shard_rows + column % shard_rows
        best = jnp.max(logits, axis=1)
        denom = jnp.sum(jnp.exp(logits - best[:, None]), axis=1)
        target = jnp.sum(jnp.where(pairs[:, None] == text_id[None, :], logits, 0.0), axis=1)
        partial = jnp.pad(jnp.stack([best, denom, target]), ((0, 5), (0, EXT - img_dev)))
    with jax.named_scope("grad_xz"):
        codes = lax.all_to_all(
            codes.reshape(N_X * N_Z, -1, local_cols + EXT), "dp", 0, 0, axis_index_groups=XZ_GROUPS, tiled=True
        )
    head_grad, extra = sum_last(codes)

    with jax.named_scope("loss_parts"):
        parts = jnp.concatenate([partial[:3], extra[:1], partial[4:]])
        parts = [parts] + [ring(parts, step) for step in range(1, n_cache)]
        partials = []
        for k, got in enumerate(parts):
            first = (n_cache - k) % n_cache * shard_rows
            partials.append(got[:3, first : first + shard_rows])
        partials = jnp.stack(partials)
        best = jnp.max(partials[:, 0], axis=0)
        denom = jnp.sum(partials[:, 1] * jnp.exp(partials[:, 0] - best[None, :]), axis=0)
        contrast = best + jnp.log(denom) - jnp.sum(partials[:, 2], axis=0)
        regress = sum(got[3] for got in parts)
        regress = lax.dynamic_slice_in_dim(regress, cache_pos * shard_rows, shard_rows, 0)
    return (head_grad, regress + contrast)


def solution(mesh):
    in_specs = (
        P("dp", None, None),
        P(None, "cache"),
        P("dp", None, "cache"),
        P(),
        P("dp"),
        P(("dp", "cache"), None),
        P(("dp", "cache"), None),
        P(("dp", "cache")),
    )
    out_specs = (P("dp", "cache"), P(("dp", "cache")))
    return jax.shard_map(local, mesh=mesh, in_specs=in_specs, out_specs=out_specs, check_vma=False)
```

```python
import jax
import jax.numpy as jnp
from jax import lax
from jax.experimental import pallas as pl
from jax.experimental.pallas import tpu as pltpu
from jax.sharding import PartitionSpec as P

eps = 1e-06
loss_scale = 128.0

N_X, N_Z, N_CORE = 4, 8, 2
EXT = 128
VMEM_BYTES = 62 * 1024 * 1024

XZ_GROUPS = [[k * N_CORE + c for k in range(N_X * N_Z)] for c in range(N_CORE)]


def params():
    return pltpu.CompilerParams(vmem_limit_bytes=VMEM_BYTES)


LANES = 128
COUNT_ROWS = 8


def dispatch_rows(student_feats, holder_index, valid_count, own_index, cache_pos, cols):
    images, rows, width = student_feats.shape
    n_dp = holder_index.shape[0] // images
    parts = cols // LANES

    def kernel(place, holders, counts, feats, out):
        out[...] = jnp.zeros_like(out)
        for i in range(images):
            h = holders[place[0] * images + i]
            for k in range(parts):
                out[h, k * rows : (k + 1) * rows, :] = feats[i, :, k * LANES : (k + 1) * LANES]
            count = jnp.full((COUNT_ROWS, LANES), counts[i].astype(jnp.float32))
            out[h, parts * rows :, :] = count.astype(out.dtype)

    out_rows = parts * rows + COUNT_ROWS
    return pl.pallas_call(
        kernel,
        grid_spec=pltpu.PrefetchScalarGridSpec(
            num_scalar_prefetch=3,
            grid=(1,),
            in_specs=[pl.BlockSpec((images, rows, cols), lambda i, p, h, c: (0, 0, p[1]))],
            out_specs=pl.BlockSpec((n_dp, out_rows, LANES), lambda i, p, h, c: (0, 0, 0)),
        ),
        out_shape=jax.ShapeDtypeStruct((n_dp, out_rows, LANES), student_feats.dtype),
        compiler_params=params(),
        name="dispatch_rows",
    )(jnp.stack([own_index, cache_pos]).astype(jnp.int32), holder_index, valid_count, student_feats)


def near_terms(cache_pos, near, head_weight):
    n_img, split_rows, lanes = near[0].shape
    width, cols = head_weight.shape
    block, patch = 512, 32
    splits = split_rows // patch
    part = splits * lanes
    n_part = width // part
    rows = n_img * patch
    img_block = block // patch

    def kernel(sc, x0, x1, x2, w_ref, pred_out, xt_out):
        xt_out[...] = jnp.zeros_like(xt_out)
        pred = jnp.zeros((block, cols), jnp.float32)
        for ref, off in ((x0, 0), (x1, n_part - 1), (x2, 1)):
            first = lax.rem(sc[0] + off, n_part) * part
            pieces = [
                ref[:, k * patch : (k + 1) * patch, :].reshape(block, lanes) for k in range(splits)
            ]
            for k, piece in enumerate(pieces):
                xt_out[pl.ds(pl.multiple_of(first + k * lanes, lanes), lanes), :] = piece.T
            pred = pred + jnp.dot(
                jnp.concatenate(pieces, axis=1),
                w_ref[pl.ds(pl.multiple_of(first, part), part), :],
                preferred_element_type=jnp.float32,
            )
        pred_out[...] = pred

    img_spec = pl.BlockSpec((img_block, split_rows, lanes), lambda i, s: (i, 0, 0))
    return pl.pallas_call(
        kernel,
        grid_spec=pltpu.PrefetchScalarGridSpec(
            num_scalar_prefetch=1,
            grid=(rows // block,),
            in_specs=[img_spec] * 3 + [pl.BlockSpec((width, cols), lambda i, s: (0, 0))],
            out_specs=[
                pl.BlockSpec((block, cols), lambda i, s: (i, 0)),
                pl.BlockSpec((width, block), lambda i, s: (0, i)),
            ],
        ),
        out_shape=[
            jax.ShapeDtypeStruct((rows, cols), jnp.float32),
            jax.ShapeDtypeStruct((width, rows), near[0].dtype),
        ],
        compiler_params=params(),
        cost_estimate=pl.CostEstimate(
            flops=2 * rows * 3 * part * cols, bytes_accessed=20 * 2**20, transcendentals=0
        ),
        name="near_terms",
    )(cache_pos[None].astype(jnp.int32), *near, head_weight)


def head_terms(scalars, near_pred, near_cols, far_a, far_b, head_weight, teacher, row_info, full_cols):
    half_img, split_rows, lanes = far_a.shape
    n_img = 2 * half_img
    width, cols = head_weight.shape
    block, tile, patch = 512, 256, 32
    splits = split_rows // patch
    part = splits * lanes
    rows = n_img * patch
    n_part = width // part
    steps, tiles = rows // block, cols // tile
    half = steps // 2
    img_block = block // patch
    pairs = N_X * N_Z
    owner_rows = width // (pairs * N_CORE)
    out_rows = width // N_CORE

    def kernel(sc, pred_ref, xt_ref, fa, fb, w_ref, t_ref, info_ref, keep, send, x_scr, g_scr, r_scr):
        step = pl.program_id(0)

        @pl.when(step < steps)
        def _():
            here = pl.ds(pl.multiple_of(step * block, block), block)
            far = jnp.where(step < half, fa[...], fb[...])
            pieces = [far[:, k * patch : (k + 1) * patch, :].reshape(block, lanes) for k in range(splits)]
            x_scr[:, here] = xt_ref[...]
            first = lax.rem(sc[0] + 2, n_part) * part
            for k, piece in enumerate(pieces):
                x_scr[pl.ds(pl.multiple_of(first + k * lanes, lanes), lanes), here] = piece.T
            pred = pred_ref[...] + jnp.dot(
                jnp.concatenate(pieces, axis=1), w_ref[...], preferred_element_type=jnp.float32
            )
            info = info_ref[...]
            mean, inv, coef, weight = (info[:, k : k + 1] for k in range(4))
            residue = pred - (t_ref[...].astype(jnp.float32) - mean) * inv
            g_scr[here, :] = (coef * residue).astype(jnp.bfloat16)
            row_loss = weight * jnp.sum(residue * residue, axis=-1, keepdims=True)
            row_loss = jnp.broadcast_to(row_loss, (block, EXT)).reshape(img_block, patch, EXT)
            r_scr[pl.ds(pl.multiple_of(step * img_block, img_block), img_block), :] = (
                jnp.sum(row_loss, axis=1) / full_cols
            )

        @pl.when((step >= steps) & (step < steps + tiles))
        def _():
            first = pl.multiple_of((step - steps) * tile, tile)
            term = jnp.dot(x_scr[...], g_scr[:, pl.ds(first, tile)], preferred_element_type=jnp.float32)
            term = term.reshape(pairs, N_CORE, owner_rows, tile)
            for mine, (one, two) in enumerate(((keep, send), (send, keep))):

                @pl.when(sc[1] == mine)
                def _():
                    one[...] = term[:, 0].reshape(out_rows, tile)
                    two[...] = term[:, 1].reshape(out_rows, tile)

        @pl.when(step == steps + tiles)
        def _():
            lane = lax.broadcasted_iota(jnp.int32, (1, EXT), 1)
            top = lax.broadcasted_iota(jnp.int32, (owner_rows, EXT), 0) == 0
            for ref, own in ((keep, sc[1]), (send, 1 - sc[1])):
                ref[...] = jnp.zeros_like(ref)
                for pair in range(pairs):
                    image = pair * N_CORE + own
                    line = jnp.where(lane == sc[2 + image], r_scr[pl.ds(image, 1), :], 0.0)
                    ref[pair * owner_rows : (pair + 1) * owner_rows, :EXT] = jnp.where(top, line, 0.0)

    row_at = lambda i: jnp.minimum(i, steps - 1)
    row_spec = lambda c: pl.BlockSpec((block, c), lambda i, s: (row_at(i), 0))
    far_spec = lambda f: pl.BlockSpec(
        (img_block, split_rows, lanes), lambda i, s: (jnp.clip(f(i), 0, half - 1), 0, 0)
    )
    out_spec = pl.BlockSpec((out_rows, tile), lambda i, s: (0, jnp.maximum(i - steps, 0)))
    out = jax.ShapeDtypeStruct((out_rows, cols + tile), jnp.float32)
    return pl.pallas_call(
        kernel,
        grid_spec=pltpu.PrefetchScalarGridSpec(
            num_scalar_prefetch=1,
            grid=(steps + tiles + 1,),
            in_specs=[
                row_spec(cols),
                pl.BlockSpec((width, block), lambda i, s: (0, row_at(i))),
                far_spec(lambda i: i),
                far_spec(lambda i: i - half),
                pl.BlockSpec((part, cols), lambda i, s: (lax.rem(s[0] + 2, n_part), 0)),
                row_spec(cols),
                row_spec(row_info.shape[1]),
            ],
            out_specs=[out_spec, out_spec],
            scratch_shapes=[
                pltpu.VMEM((width, rows), jnp.bfloat16),
                pltpu.VMEM((rows, cols), jnp.bfloat16),
                pltpu.VMEM((n_img, EXT), jnp.float32),
            ],
        ),
        out_shape=[out, out],
        compiler_params=params(),
        cost_estimate=pl.CostEstimate(
            flops=3 * rows * width * cols, bytes_accessed=30 * 2**20, transcendentals=0
        ),
        name="head_terms",
    )(scalars, near_pred, near_cols, far_a, far_b, head_weight, teacher, row_info)


def exponent(part):
    top = jnp.max(jnp.abs(part), axis=-1, keepdims=True)
    return jnp.ceil(jnp.log(jnp.maximum(top, 2.0**-100)) * 1.4426950408889634)


def code(main, extra):
    main_exp, extra_exp = exponent(main), exponent(extra)
    main_code = jnp.floor(main * jnp.exp2(14.0 - main_exp) + 0.5).astype(jnp.int32)
    extra_code = jnp.floor(extra * jnp.exp2(14.0 - extra_exp) + 0.5)
    lane = lax.broadcasted_iota(jnp.int32, extra.shape, 1)
    extra_code = jnp.where(
        lane == EXT - 2, main_exp, jnp.where(lane == EXT - 1, extra_exp, extra_code)
    ).astype(jnp.int32)
    return main_code.astype(jnp.int16), extra_code.astype(jnp.int16)


def decode(codes):
    cols = codes.shape[-1] - EXT
    wide = codes.astype(jnp.int32).astype(jnp.float32)
    main, extra = wide[:, :cols], wide[:, cols:]
    main_exp = extra[:, EXT - 2 : EXT - 1]
    extra_exp = extra[:, EXT - 1 :]
    lane = lax.broadcasted_iota(jnp.int32, extra.shape, 1)
    extra = jnp.where(lane < EXT - 2, extra, 0.0)
    return main * jnp.exp2(main_exp - 14.0), extra * jnp.exp2(extra_exp - 14.0)


def add_and_code(keep, received):
    rows, wide = keep.shape
    cols = wide - 2 * EXT
    block = rows // 4

    def kernel(a, b, out):
        main, extra = code(a[:, :cols] + b[:, :cols], a[:, cols : cols + EXT] + b[:, cols : cols + EXT])
        out[:, :cols] = main
        out[:, cols:] = extra

    spec = pl.BlockSpec((block, wide), lambda i: (i, 0))
    return pl.pallas_call(
        kernel,
        grid=(rows // block,),
        in_specs=[spec, spec],
        out_specs=pl.BlockSpec((block, cols + EXT), lambda i: (i, 0)),
        out_shape=jax.ShapeDtypeStruct((rows, cols + EXT), jnp.int16),
        compiler_params=params(),
        name="add_and_code",
    )(keep, received)


def sum_blocks(blocks):
    main, extra = decode(blocks[0])
    for block in blocks[1:]:
        m, e = decode(block)
        main, extra = main + m, extra + e
    return main, extra


def sum_last(received):
    n, rows, wide = received.shape

    def kernel(src, out, ext):
        main, extra = sum_blocks([src[k] for k in range(n)])
        out[...] = main
        ext[...] = extra

    return pl.pallas_call(
        kernel,
        out_shape=[
            jax.ShapeDtypeStruct((rows, wide - EXT), jnp.float32),
            jax.ShapeDtypeStruct((rows, EXT), jnp.float32),
        ],
        compiler_params=params(),
        name="sum_last",
    )(received)


def local(
    student_feats,
    head_weight,
    teacher_cache,
    holder_index,
    valid_count,
    image_embed,
    text_embed,
    pair_ids,
):
    n_dp = lax.axis_size("dp")
    n_cache = lax.axis_size("cache")
    own_index = lax.axis_index("dp")
    cache_pos = lax.axis_index("cache")
    core = own_index % N_CORE
    img_dev, patch_rows, student_width = student_feats.shape
    slots, _, local_cols = teacher_cache.shape
    full_cols = local_cols * n_cache
    part = student_width // n_cache
    shard_rows, embed = image_embed.shape
    assert slots == n_dp and n_dp == N_X * N_Z * N_CORE

    def ring(x, step):
        return lax.ppermute(x, "cache", [(i, (i + step) % n_cache) for i in range(n_cache)])

    def flat(x):
        return x.reshape(-1, x.shape[-1])

    img_order = jnp.arange(img_dev, dtype=jnp.int32)
    outgoing = dispatch_rows(student_feats, holder_index, valid_count, own_index, cache_pos, part)

    def swap(x, bit):
        return lax.ppermute(x, "dp", [(i, i ^ bit) for i in range(n_dp)])

    def both(x, bit):
        other = swap(x, bit)
        upper = (own_index // bit) % 2 == 1
        return jnp.concatenate([jnp.where(upper, other, x), jnp.where(upper, x, other)])

    def spread(x, bit, count):
        blocks = [x] + [swap(x, bit * k) for k in range(1, 2**count)]
        for n in range(count):
            upper = (own_index // (bit * 2**n)) % 2 == 1
            blocks = [jnp.where(upper, blocks[k ^ 2**n], blocks[k]) for k in range(2**count)]
        return jnp.concatenate(blocks)

    outgoing, texts, teacher_in = lax.optimization_barrier((outgoing, text_embed, teacher_cache))

    with jax.named_scope("student_exchange"):
        mine = lax.all_to_all(outgoing, "dp", split_axis=0, concat_axis=0, tiled=True)
    with jax.named_scope("teacher_sums"):
        wide = teacher_in.astype(jnp.float32)
        sums = jnp.stack([jnp.sum(wide, axis=-1), jnp.sum(wide * wide, axis=-1)])
        pair_cols = jnp.concatenate(
            [
                (pair_ids // 64)[:, None],
                (pair_ids % 64)[:, None],
                jnp.zeros((shard_rows, EXT - 2), jnp.int32),
            ],
            axis=1,
        ).astype(jnp.float32)
        images = jnp.concatenate([image_embed.astype(jnp.float32), pair_cols], axis=1)
        packed = jnp.concatenate([sums.reshape(-1, EXT), images.reshape(-1, EXT)])
        packed = [packed] + [ring(packed, step) for step in range(1, n_cache)]
        n_sum = sums.size // EXT
        sums = sum(p[:n_sum] for p in packed).reshape(sums.shape)
        images = jnp.concatenate([p[n_sum:] for p in packed]).reshape(img_dev, embed + EXT)
    texts, sums, images = lax.optimization_barrier((both(texts, 1), sums, images))
    texts = spread(texts, 2, 3)
    mine, sums, images, texts = lax.optimization_barrier((mine, sums, images, texts))
    with jax.named_scope("student_ring"):
        counts_sent, mine = mine[:, -COUNT_ROWS:], mine[:, :-COUNT_ROWS]
        from_prev = ring(mine, 1)
        from_next = ring(mine, -1)
        from_prev, from_next, sums, counts_sent = lax.optimization_barrier(
            (from_prev, from_next, sums, counts_sent)
        )
        far_a = ring(from_prev[: n_dp // 2], 1)
        far_b = ring(from_next[n_dp // 2 :], -1)
    near_pred, near_cols = near_terms(cache_pos, [mine, from_prev, from_next], head_weight)
    with jax.named_scope("teacher_sums"):
        row_mean = sums[0] / full_cols
        inv_scale = lax.rsqrt(sums[1] / full_cols - row_mean * row_mean + eps)

    is_held = holder_index.reshape(n_dp, img_dev) == own_index
    place_of = jnp.sum(jnp.where(is_held, img_order[None, :], 0), axis=1)
    held_any = jnp.sum(is_held.astype(jnp.int32), axis=1) > 0
    held_count = jnp.where(held_any, counts_sent[:, 0, 0].astype(jnp.float32), 0.0)
    row_index = jnp.arange(patch_rows, dtype=jnp.int32).astype(jnp.float32)
    valid_mask = (row_index[None, :] < held_count[:, None]).astype(jnp.float32)
    row_weight = valid_mask / jnp.maximum(held_count, 1.0)[:, None]
    coef = 2.0 * loss_scale / full_cols * row_weight
    inv_scale = jnp.where(held_count[:, None] > 0, inv_scale, 0.0)
    row_info = jnp.stack([row_mean, inv_scale, coef, row_weight], axis=-1).reshape(
        n_dp * patch_rows, 4
    )

    scalars = jnp.concatenate([jnp.stack([cache_pos, core]).astype(jnp.int32), place_of])
    keep, send = head_terms(
        scalars,
        near_pred,
        near_cols,
        far_a,
        far_b,
        head_weight,
        flat(teacher_cache),
        row_info,
        full_cols,
    )
    with jax.named_scope("grad_core"):
        received = swap(send, 1)
    codes = add_and_code(keep, received)
    codes, images, texts = lax.optimization_barrier((codes, images, texts))
    texts = spread(texts, 2 * N_Z, 2)
    with jax.named_scope("contrast"):
        pairs = images[:, embed].astype(jnp.int32) * 64 + images[:, embed + 1].astype(jnp.int32)
        logits = jnp.dot(
            images[:, :embed].astype(jnp.bfloat16),
            texts.T,
            preferred_element_type=jnp.float32,
        ) * (embed ** (-0.5))
        column = jnp.arange(texts.shape[0], dtype=jnp.int32)
        text_id = column // shard_rows * img_dev + cache_pos * shard_rows + column % shard_rows
        best = jnp.max(logits, axis=1)
        denom = jnp.sum(jnp.exp(logits - best[:, None]), axis=1)
        target = jnp.sum(jnp.where(pairs[:, None] == text_id[None, :], logits, 0.0), axis=1)
        partial = jnp.pad(jnp.stack([best, denom, target]), ((0, 5), (0, EXT - img_dev)))
    with jax.named_scope("grad_xz"):
        codes = lax.all_to_all(
            codes.reshape(N_X * N_Z, -1, local_cols + EXT), "dp", 0, 0, axis_index_groups=XZ_GROUPS, tiled=True
        )
    head_grad, extra = sum_last(codes)

    with jax.named_scope("loss_parts"):
        parts = jnp.concatenate([partial[:3], extra[:1], partial[4:]])
        parts = [parts] + [ring(parts, step) for step in range(1, n_cache)]
        partials = []
        for k, got in enumerate(parts):
            first = (n_cache - k) % n_cache * shard_rows
            partials.append(got[:3, first : first + shard_rows])
        partials = jnp.stack(partials)
        best = jnp.max(partials[:, 0], axis=0)
        denom = jnp.sum(partials[:, 1] * jnp.exp(partials[:, 0] - best[None, :]), axis=0)
        contrast = best + jnp.log(denom) - jnp.sum(partials[:, 2], axis=0)
        regress = sum(got[3] for got in parts)
        regress = lax.dynamic_slice_in_dim(regress, cache_pos * shard_rows, shard_rows, 0)
    return (head_grad, regress + contrast)


def solution(mesh):
    in_specs = (
        P("dp", None, None),
        P(None, "cache"),
        P("dp", None, "cache"),
        P(),
        P("dp"),
        P(("dp", "cache"), None),
        P(("dp", "cache"), None),
        P(("dp", "cache")),
    )
    out_specs = (P("dp", "cache"), P(("dp", "cache")))
    return jax.shard_map(local, mesh=mesh, in_specs=in_specs, out_specs=out_specs, check_vma=False)
```

```python
import jax
import jax.numpy as jnp
from jax import lax
from jax.experimental import pallas as pl
from jax.experimental.pallas import tpu as pltpu
from jax.sharding import PartitionSpec as P

eps = 1e-06
loss_scale = 128.0

N_X, N_Z, N_CORE = 4, 8, 2
EXT = 128
VMEM_BYTES = 62 * 1024 * 1024

XZ_GROUPS = [[k * N_CORE + c for k in range(N_X * N_Z)] for c in range(N_CORE)]


def params():
    return pltpu.CompilerParams(vmem_limit_bytes=VMEM_BYTES)


LANES = 128
COUNT_ROWS = 8


def dispatch_rows(student_feats, holder_index, valid_count, own_index, cache_pos, cols):
    images, rows, width = student_feats.shape
    n_dp = holder_index.shape[0] // images
    parts = cols // LANES

    def kernel(place, holders, counts, feats, out):
        out[...] = jnp.zeros_like(out)
        for i in range(images):
            h = holders[place[0] * images + i]
            for k in range(parts):
                out[h, k * rows : (k + 1) * rows, :] = feats[i, :, k * LANES : (k + 1) * LANES]
            count = jnp.full((COUNT_ROWS, LANES), counts[i].astype(jnp.float32))
            out[h, parts * rows :, :] = count.astype(out.dtype)

    out_rows = parts * rows + COUNT_ROWS
    return pl.pallas_call(
        kernel,
        grid_spec=pltpu.PrefetchScalarGridSpec(
            num_scalar_prefetch=3,
            grid=(1,),
            in_specs=[pl.BlockSpec((images, rows, cols), lambda i, p, h, c: (0, 0, p[1]))],
            out_specs=pl.BlockSpec((n_dp, out_rows, LANES), lambda i, p, h, c: (0, 0, 0)),
        ),
        out_shape=jax.ShapeDtypeStruct((n_dp, out_rows, LANES), student_feats.dtype),
        compiler_params=params(),
        name="dispatch_rows",
    )(jnp.stack([own_index, cache_pos]).astype(jnp.int32), holder_index, valid_count, student_feats)


def near_terms(cache_pos, near, head_weight):
    n_img, split_rows, lanes = near[0].shape
    width, cols = head_weight.shape
    block, patch = 512, 32
    splits = split_rows // patch
    part = splits * lanes
    n_part = width // part
    rows = n_img * patch
    img_block = block // patch

    def kernel(sc, x0, x1, x2, w_ref, pred_out, xt_out):
        xt_out[...] = jnp.zeros_like(xt_out)
        pred = jnp.zeros((block, cols), jnp.float32)
        for ref, off in ((x0, 0), (x1, n_part - 1), (x2, 1)):
            first = lax.rem(sc[0] + off, n_part) * part
            pieces = [
                ref[:, k * patch : (k + 1) * patch, :].reshape(block, lanes) for k in range(splits)
            ]
            for k, piece in enumerate(pieces):
                xt_out[pl.ds(pl.multiple_of(first + k * lanes, lanes), lanes), :] = piece.T
            pred = pred + jnp.dot(
                jnp.concatenate(pieces, axis=1),
                w_ref[pl.ds(pl.multiple_of(first, part), part), :],
                preferred_element_type=jnp.float32,
            )
        pred_out[...] = pred

    img_spec = pl.BlockSpec((img_block, split_rows, lanes), lambda i, s: (i, 0, 0))
    return pl.pallas_call(
        kernel,
        grid_spec=pltpu.PrefetchScalarGridSpec(
            num_scalar_prefetch=1,
            grid=(rows // block,),
            in_specs=[img_spec] * 3 + [pl.BlockSpec((width, cols), lambda i, s: (0, 0))],
            out_specs=[
                pl.BlockSpec((block, cols), lambda i, s: (i, 0)),
                pl.BlockSpec((width, block), lambda i, s: (0, i)),
            ],
        ),
        out_shape=[
            jax.ShapeDtypeStruct((rows, cols), jnp.float32),
            jax.ShapeDtypeStruct((width, rows), near[0].dtype),
        ],
        compiler_params=params(),
        cost_estimate=pl.CostEstimate(
            flops=2 * rows * 3 * part * cols, bytes_accessed=20 * 2**20, transcendentals=0
        ),
        name="near_terms",
    )(cache_pos[None].astype(jnp.int32), *near, head_weight)


def head_terms(scalars, near_pred, near_cols, far_a, far_b, head_weight, teacher, row_info, full_cols):
    half_img, split_rows, lanes = far_a.shape
    n_img = 2 * half_img
    width, cols = head_weight.shape
    block, tile, patch = 512, 256, 32
    splits = split_rows // patch
    part = splits * lanes
    rows = n_img * patch
    n_part = width // part
    steps, tiles = rows // block, cols // tile
    half = steps // 2
    img_block = block // patch
    pairs = N_X * N_Z
    owner_rows = width // (pairs * N_CORE)
    out_rows = width // N_CORE

    def kernel(sc, pred_ref, xt_ref, fa, fb, w_ref, t_ref, info_ref, keep, send, x_scr, g_scr, r_scr):
        step = pl.program_id(0)

        @pl.when(step < steps)
        def _():
            here = pl.ds(pl.multiple_of(step * block, block), block)
            far = jnp.where(step < half, fa[...], fb[...])
            pieces = [far[:, k * patch : (k + 1) * patch, :].reshape(block, lanes) for k in range(splits)]
            x_scr[:, here] = xt_ref[...]
            first = lax.rem(sc[0] + 2, n_part) * part
            for k, piece in enumerate(pieces):
                x_scr[pl.ds(pl.multiple_of(first + k * lanes, lanes), lanes), here] = piece.T
            pred = pred_ref[...] + jnp.dot(
                jnp.concatenate(pieces, axis=1), w_ref[...], preferred_element_type=jnp.float32
            )
            info = info_ref[...]
            mean, inv, coef, weight = (info[:, k : k + 1] for k in range(4))
            residue = pred - (t_ref[...].astype(jnp.float32) - mean) * inv
            g_scr[here, :] = (coef * residue).astype(jnp.bfloat16)
            row_loss = weight * jnp.sum(residue * residue, axis=-1, keepdims=True)
            row_loss = jnp.broadcast_to(row_loss, (block, EXT)).reshape(img_block, patch, EXT)
            r_scr[pl.ds(pl.multiple_of(step * img_block, img_block), img_block), :] = (
                jnp.sum(row_loss, axis=1) / full_cols
            )

        @pl.when((step >= steps) & (step < steps + tiles))
        def _():
            first = pl.multiple_of((step - steps) * tile, tile)
            term = jnp.dot(x_scr[...], g_scr[:, pl.ds(first, tile)], preferred_element_type=jnp.float32)
            term = term.reshape(pairs, N_CORE, owner_rows, tile)
            for mine, (one, two) in enumerate(((keep, send), (send, keep))):

                @pl.when(sc[1] == mine)
                def _():
                    one[...] = term[:, 0].reshape(out_rows, tile)
                    two[...] = term[:, 1].reshape(out_rows, tile)

        @pl.when(step == steps + tiles)
        def _():
            lane = lax.broadcasted_iota(jnp.int32, (1, EXT), 1)
            top = lax.broadcasted_iota(jnp.int32, (owner_rows, EXT), 0) == 0
            for ref, own in ((keep, sc[1]), (send, 1 - sc[1])):
                ref[...] = jnp.zeros_like(ref)
                for pair in range(pairs):
                    image = pair * N_CORE + own
                    line = jnp.where(lane == sc[2 + image], r_scr[pl.ds(image, 1), :], 0.0)
                    ref[pair * owner_rows : (pair + 1) * owner_rows, :EXT] = jnp.where(top, line, 0.0)

    row_at = lambda i: jnp.minimum(i, steps - 1)
    row_spec = lambda c: pl.BlockSpec((block, c), lambda i, s: (row_at(i), 0))
    far_spec = lambda f: pl.BlockSpec(
        (img_block, split_rows, lanes), lambda i, s: (jnp.clip(f(i), 0, half - 1), 0, 0)
    )
    out_spec = pl.BlockSpec((out_rows, tile), lambda i, s: (0, jnp.maximum(i - steps, 0)))
    out = jax.ShapeDtypeStruct((out_rows, cols + tile), jnp.float32)
    return pl.pallas_call(
        kernel,
        grid_spec=pltpu.PrefetchScalarGridSpec(
            num_scalar_prefetch=1,
            grid=(steps + tiles + 1,),
            in_specs=[
                row_spec(cols),
                pl.BlockSpec((width, block), lambda i, s: (0, row_at(i))),
                far_spec(lambda i: i),
                far_spec(lambda i: i - half),
                pl.BlockSpec((part, cols), lambda i, s: (lax.rem(s[0] + 2, n_part), 0)),
                row_spec(cols),
                row_spec(row_info.shape[1]),
            ],
            out_specs=[out_spec, out_spec],
            scratch_shapes=[
                pltpu.VMEM((width, rows), jnp.bfloat16),
                pltpu.VMEM((rows, cols), jnp.bfloat16),
                pltpu.VMEM((n_img, EXT), jnp.float32),
            ],
        ),
        out_shape=[out, out],
        compiler_params=params(),
        cost_estimate=pl.CostEstimate(
            flops=3 * rows * width * cols, bytes_accessed=30 * 2**20, transcendentals=0
        ),
        name="head_terms",
    )(scalars, near_pred, near_cols, far_a, far_b, head_weight, teacher, row_info)


def exponent(part):
    top = jnp.max(jnp.abs(part), axis=-1, keepdims=True)
    return jnp.ceil(jnp.log(jnp.maximum(top, 2.0**-100)) * 1.4426950408889634)


def code(main, extra):
    main_exp, extra_exp = exponent(main), exponent(extra)
    main_code = jnp.floor(main * jnp.exp2(14.0 - main_exp) + 0.5).astype(jnp.int32)
    extra_code = jnp.floor(extra * jnp.exp2(14.0 - extra_exp) + 0.5)
    lane = lax.broadcasted_iota(jnp.int32, extra.shape, 1)
    extra_code = jnp.where(
        lane == EXT - 2, main_exp, jnp.where(lane == EXT - 1, extra_exp, extra_code)
    ).astype(jnp.int32)
    return main_code.astype(jnp.int16), extra_code.astype(jnp.int16)


def decode(codes):
    cols = codes.shape[-1] - EXT
    wide = codes.astype(jnp.int32).astype(jnp.float32)
    main, extra = wide[:, :cols], wide[:, cols:]
    main_exp = extra[:, EXT - 2 : EXT - 1]
    extra_exp = extra[:, EXT - 1 :]
    lane = lax.broadcasted_iota(jnp.int32, extra.shape, 1)
    extra = jnp.where(lane < EXT - 2, extra, 0.0)
    return main * jnp.exp2(main_exp - 14.0), extra * jnp.exp2(extra_exp - 14.0)


def add_and_code(keep, received):
    rows, wide = keep.shape
    cols = wide - 2 * EXT
    block = rows // 4

    def kernel(a, b, out):
        main, extra = code(a[:, :cols] + b[:, :cols], a[:, cols : cols + EXT] + b[:, cols : cols + EXT])
        out[:, :cols] = main
        out[:, cols:] = extra

    spec = pl.BlockSpec((block, wide), lambda i: (i, 0))
    return pl.pallas_call(
        kernel,
        grid=(rows // block,),
        in_specs=[spec, spec],
        out_specs=pl.BlockSpec((block, cols + EXT), lambda i: (i, 0)),
        out_shape=jax.ShapeDtypeStruct((rows, cols + EXT), jnp.int16),
        compiler_params=params(),
        name="add_and_code",
    )(keep, received)


def sum_blocks(blocks):
    main, extra = decode(blocks[0])
    for block in blocks[1:]:
        m, e = decode(block)
        main, extra = main + m, extra + e
    return main, extra


def sum_last(received, partial):
    n, rows, wide = received.shape

    def kernel(src, partial_ref, out, parts):
        main, extra = sum_blocks([src[k] for k in range(n)])
        out[...] = main
        row = lax.broadcasted_iota(jnp.int32, partial.shape, 0)
        parts[...] = jnp.where(row == 3, extra[:1], partial_ref[...])

    return pl.pallas_call(
        kernel,
        out_shape=[
            jax.ShapeDtypeStruct((rows, wide - EXT), jnp.float32),
            jax.ShapeDtypeStruct(partial.shape, jnp.float32),
        ],
        compiler_params=params(),
        name="sum_last",
    )(received, partial)


def local(
    student_feats,
    head_weight,
    teacher_cache,
    holder_index,
    valid_count,
    image_embed,
    text_embed,
    pair_ids,
):
    n_dp = lax.axis_size("dp")
    n_cache = lax.axis_size("cache")
    own_index = lax.axis_index("dp")
    cache_pos = lax.axis_index("cache")
    core = own_index % N_CORE
    img_dev, patch_rows, student_width = student_feats.shape
    slots, _, local_cols = teacher_cache.shape
    full_cols = local_cols * n_cache
    part = student_width // n_cache
    shard_rows, embed = image_embed.shape
    assert slots == n_dp and n_dp == N_X * N_Z * N_CORE

    def ring(x, step):
        return lax.ppermute(x, "cache", [(i, (i + step) % n_cache) for i in range(n_cache)])

    def flat(x):
        return x.reshape(-1, x.shape[-1])

    img_order = jnp.arange(img_dev, dtype=jnp.int32)
    outgoing = dispatch_rows(student_feats, holder_index, valid_count, own_index, cache_pos, part)

    def swap(x, bit):
        return lax.ppermute(x, "dp", [(i, i ^ bit) for i in range(n_dp)])

    def both(x, bit):
        other = swap(x, bit)
        upper = (own_index // bit) % 2 == 1
        return jnp.concatenate([jnp.where(upper, other, x), jnp.where(upper, x, other)])

    def spread(x, bit, count):
        blocks = [x] + [swap(x, bit * k) for k in range(1, 2**count)]
        for n in range(count):
            upper = (own_index // (bit * 2**n)) % 2 == 1
            blocks = [jnp.where(upper, blocks[k ^ 2**n], blocks[k]) for k in range(2**count)]
        return jnp.concatenate(blocks)

    outgoing, texts = lax.optimization_barrier((outgoing, both(text_embed, N_Z)))
    texts, teacher_in = lax.optimization_barrier((both(texts, 1), teacher_cache))

    with jax.named_scope("student_exchange"):
        mine = lax.all_to_all(outgoing, "dp", split_axis=0, concat_axis=0, tiled=True)
    with jax.named_scope("teacher_sums"):
        wide = teacher_in.astype(jnp.float32)
        sums = jnp.stack([jnp.sum(wide, axis=-1), jnp.sum(wide * wide, axis=-1)])
        pair_cols = jnp.concatenate(
            [
                (pair_ids // 64)[:, None],
                (pair_ids % 64)[:, None],
                jnp.zeros((shard_rows, EXT - 2), jnp.int32),
            ],
            axis=1,
        ).astype(jnp.float32)
        images = jnp.concatenate([image_embed.astype(jnp.float32), pair_cols], axis=1)
        packed = jnp.concatenate([sums.reshape(-1, EXT), images.reshape(-1, EXT)])
        packed = [packed] + [ring(packed, step) for step in range(1, n_cache)]
        n_sum = sums.size // EXT
        sums = sum(p[:n_sum] for p in packed).reshape(sums.shape)
        images = jnp.concatenate([p[n_sum:] for p in packed]).reshape(img_dev, embed + EXT)
    texts = both(texts, 4)
    mine, sums, images, texts = lax.optimization_barrier((mine, sums, images, texts))
    with jax.named_scope("student_ring"):
        counts_sent, mine = mine[:, -COUNT_ROWS:], mine[:, :-COUNT_ROWS]
        from_prev = ring(mine, 1)
        from_next = ring(mine, -1)
        from_prev, from_next, sums, counts_sent = lax.optimization_barrier(
            (from_prev, from_next, sums, counts_sent)
        )
        far_a = ring(from_prev[: n_dp // 2], 1)
        far_b = ring(from_next[n_dp // 2 :], -1)
    near_pred, near_cols = near_terms(cache_pos, [mine, from_prev, from_next], head_weight)
    with jax.named_scope("teacher_sums"):
        row_mean = sums[0] / full_cols
        inv_scale = lax.rsqrt(sums[1] / full_cols - row_mean * row_mean + eps)

    is_held = holder_index.reshape(n_dp, img_dev) == own_index
    place_of = jnp.sum(jnp.where(is_held, img_order[None, :], 0), axis=1)
    held_any = jnp.sum(is_held.astype(jnp.int32), axis=1) > 0
    held_count = jnp.where(held_any, counts_sent[:, 0, 0].astype(jnp.float32), 0.0)
    row_index = jnp.arange(patch_rows, dtype=jnp.int32).astype(jnp.float32)
    valid_mask = (row_index[None, :] < held_count[:, None]).astype(jnp.float32)
    row_weight = valid_mask / jnp.maximum(held_count, 1.0)[:, None]
    coef = 2.0 * loss_scale / full_cols * row_weight
    inv_scale = jnp.where(held_count[:, None] > 0, inv_scale, 0.0)
    row_info = jnp.stack([row_mean, inv_scale, coef, row_weight], axis=-1).reshape(
        n_dp * patch_rows, 4
    )

    scalars = jnp.concatenate([jnp.stack([cache_pos, core]).astype(jnp.int32), place_of])
    keep, send = head_terms(
        scalars,
        near_pred,
        near_cols,
        far_a,
        far_b,
        head_weight,
        flat(teacher_cache),
        row_info,
        full_cols,
    )
    with jax.named_scope("grad_core"):
        received = swap(send, 1)
    texts = both(lax.optimization_barrier((texts, send))[0], 2)
    codes = add_and_code(keep, received)
    codes, images, texts = lax.optimization_barrier((codes, images, texts))
    texts = spread(texts, 2 * N_Z, 2)
    with jax.named_scope("contrast"):
        pairs = images[:, embed].astype(jnp.int32) * 64 + images[:, embed + 1].astype(jnp.int32)
        logits = jnp.dot(
            images[:, :embed].astype(jnp.bfloat16),
            texts.T,
            preferred_element_type=jnp.float32,
        ) * (embed ** (-0.5))
        column = jnp.arange(texts.shape[0], dtype=jnp.int32)
        text_dp = column // (16 * shard_rows) * 16
        for n, bit in enumerate((N_Z, 1, 4, 2)):
            text_dp = text_dp + column // (shard_rows * 2**n) % 2 * bit
        text_id = text_dp * img_dev + cache_pos * shard_rows + column % shard_rows
        best = jnp.max(logits, axis=1)
        denom = jnp.sum(jnp.exp(logits - best[:, None]), axis=1)
        target = jnp.sum(jnp.where(pairs[:, None] == text_id[None, :], logits, 0.0), axis=1)
        partial = jnp.pad(jnp.stack([best, denom, target]), ((0, 5), (0, EXT - img_dev)))
    with jax.named_scope("grad_xz"):
        codes = lax.all_to_all(
            codes.reshape(N_X * N_Z, -1, local_cols + EXT), "dp", 0, 0, axis_index_groups=XZ_GROUPS, tiled=True
        )
    head_grad, parts = sum_last(codes, partial)

    with jax.named_scope("loss_parts"):
        parts = [parts] + [ring(parts, step) for step in range(1, n_cache)]
        partials = []
        for k, got in enumerate(parts):
            first = (n_cache - k) % n_cache * shard_rows
            partials.append(got[:3, first : first + shard_rows])
        partials = jnp.stack(partials)
        best = jnp.max(partials[:, 0], axis=0)
        denom = jnp.sum(partials[:, 1] * jnp.exp(partials[:, 0] - best[None, :]), axis=0)
        contrast = best + jnp.log(denom) - jnp.sum(partials[:, 2], axis=0)
        regress = sum(got[3] for got in parts)
        regress = lax.dynamic_slice_in_dim(regress, cache_pos * shard_rows, shard_rows, 0)
    return (head_grad, regress + contrast)


def solution(mesh):
    in_specs = (
        P("dp", None, None),
        P(None, "cache"),
        P("dp", None, "cache"),
        P(),
        P("dp"),
        P(("dp", "cache"), None),
        P(("dp", "cache"), None),
        P(("dp", "cache")),
    )
    out_specs = (P("dp", "cache"), P(("dp", "cache")))
    return jax.shard_map(local, mesh=mesh, in_specs=in_specs, out_specs=out_specs, check_vma=False)
```

```python
import jax
import jax.numpy as jnp
from jax import lax
from jax.experimental import pallas as pl
from jax.experimental.pallas import tpu as pltpu
from jax.sharding import PartitionSpec as P

eps = 1e-06
loss_scale = 128.0

N_X, N_Z, N_CORE = 4, 8, 2
EXT = 128
VMEM_BYTES = 62 * 1024 * 1024

XZ_GROUPS = [[k * N_CORE + c for k in range(N_X * N_Z)] for c in range(N_CORE)]


def params():
    return pltpu.CompilerParams(vmem_limit_bytes=VMEM_BYTES)


LANES = 128
COUNT_ROWS = 8


def dispatch_rows(student_feats, holder_index, valid_count, own_index, cache_pos, cols):
    images, rows, width = student_feats.shape
    n_dp = holder_index.shape[0] // images
    parts = cols // LANES

    def kernel(place, holders, counts, feats, out):
        out[...] = jnp.zeros_like(out)
        for i in range(images):
            h = holders[place[0] * images + i]
            for k in range(parts):
                out[h, k * rows : (k + 1) * rows, :] = feats[i, :, k * LANES : (k + 1) * LANES]
            count = jnp.full((COUNT_ROWS, LANES), counts[i].astype(jnp.float32))
            out[h, parts * rows :, :] = count.astype(out.dtype)

    out_rows = parts * rows + COUNT_ROWS
    return pl.pallas_call(
        kernel,
        grid_spec=pltpu.PrefetchScalarGridSpec(
            num_scalar_prefetch=3,
            grid=(1,),
            in_specs=[pl.BlockSpec((images, rows, cols), lambda i, p, h, c: (0, 0, p[1]))],
            out_specs=pl.BlockSpec((n_dp, out_rows, LANES), lambda i, p, h, c: (0, 0, 0)),
        ),
        out_shape=jax.ShapeDtypeStruct((n_dp, out_rows, LANES), student_feats.dtype),
        compiler_params=params(),
        name="dispatch_rows",
    )(jnp.stack([own_index, cache_pos]).astype(jnp.int32), holder_index, valid_count, student_feats)


def near_terms(cache_pos, near, head_weight):
    n_img, split_rows, lanes = near[0].shape
    width, cols = head_weight.shape
    block, patch = 512, 32
    splits = split_rows // patch
    part = splits * lanes
    n_part = width // part
    rows = n_img * patch
    img_block = block // patch

    def kernel(sc, x0, x1, x2, w_ref, pred_out, xt_out):
        xt_out[...] = jnp.zeros_like(xt_out)
        pred = jnp.zeros((block, cols), jnp.float32)
        for ref, off in ((x0, 0), (x1, n_part - 1), (x2, 1)):
            first = lax.rem(sc[0] + off, n_part) * part
            pieces = [
                ref[:, k * patch : (k + 1) * patch, :].reshape(block, lanes) for k in range(splits)
            ]
            for k, piece in enumerate(pieces):
                xt_out[pl.ds(pl.multiple_of(first + k * lanes, lanes), lanes), :] = piece.T
            pred = pred + jnp.dot(
                jnp.concatenate(pieces, axis=1),
                w_ref[pl.ds(pl.multiple_of(first, part), part), :],
                preferred_element_type=jnp.float32,
            )
        pred_out[...] = pred

    img_spec = pl.BlockSpec((img_block, split_rows, lanes), lambda i, s: (i, 0, 0))
    return pl.pallas_call(
        kernel,
        grid_spec=pltpu.PrefetchScalarGridSpec(
            num_scalar_prefetch=1,
            grid=(rows // block,),
            in_specs=[img_spec] * 3 + [pl.BlockSpec((width, cols), lambda i, s: (0, 0))],
            out_specs=[
                pl.BlockSpec((block, cols), lambda i, s: (i, 0)),
                pl.BlockSpec((width, block), lambda i, s: (0, i)),
            ],
        ),
        out_shape=[
            jax.ShapeDtypeStruct((rows, cols), jnp.float32),
            jax.ShapeDtypeStruct((width, rows), near[0].dtype),
        ],
        compiler_params=params(),
        cost_estimate=pl.CostEstimate(
            flops=2 * rows * 3 * part * cols, bytes_accessed=20 * 2**20, transcendentals=0
        ),
        name="near_terms",
    )(cache_pos[None].astype(jnp.int32), *near, head_weight)


def head_terms(scalars, near_pred, near_cols, far_a, far_b, head_weight, teacher, row_info, full_cols):
    half_img, split_rows, lanes = far_a.shape
    n_img = 2 * half_img
    width, cols = head_weight.shape
    block, tile, patch = 512, 256, 32
    splits = split_rows // patch
    part = splits * lanes
    rows = n_img * patch
    n_part = width // part
    steps, tiles = rows // block, cols // tile
    half = steps // 2
    img_block = block // patch
    pairs = N_X * N_Z
    owner_rows = width // (pairs * N_CORE)
    out_rows = width // N_CORE

    def kernel(sc, pred_ref, xt_ref, fa, fb, w_ref, t_ref, info_ref, keep, send, x_scr, g_scr, r_scr):
        step = pl.program_id(0)

        @pl.when(step < steps)
        def _():
            here = pl.ds(pl.multiple_of(step * block, block), block)
            far = jnp.where(step < half, fa[...], fb[...])
            pieces = [far[:, k * patch : (k + 1) * patch, :].reshape(block, lanes) for k in range(splits)]
            x_scr[:, here] = xt_ref[...]
            first = lax.rem(sc[0] + 2, n_part) * part
            for k, piece in enumerate(pieces):
                x_scr[pl.ds(pl.multiple_of(first + k * lanes, lanes), lanes), here] = piece.T
            pred = pred_ref[...] + jnp.dot(
                jnp.concatenate(pieces, axis=1), w_ref[...], preferred_element_type=jnp.float32
            )
            info = info_ref[...]
            mean, inv, coef, weight = (info[:, k : k + 1] for k in range(4))
            residue = pred - (t_ref[...].astype(jnp.float32) - mean) * inv
            g_scr[here, :] = (coef * residue).astype(jnp.bfloat16)
            row_loss = weight * jnp.sum(residue * residue, axis=-1, keepdims=True)
            row_loss = jnp.broadcast_to(row_loss, (block, EXT)).reshape(img_block, patch, EXT)
            r_scr[pl.ds(pl.multiple_of(step * img_block, img_block), img_block), :] = (
                jnp.sum(row_loss, axis=1) / full_cols
            )

        @pl.when((step >= steps) & (step < steps + tiles))
        def _():
            first = pl.multiple_of((step - steps) * tile, tile)
            term = jnp.dot(x_scr[...], g_scr[:, pl.ds(first, tile)], preferred_element_type=jnp.float32)
            term = term.reshape(pairs, N_CORE, owner_rows, tile)
            for mine, (one, two) in enumerate(((keep, send), (send, keep))):

                @pl.when(sc[1] == mine)
                def _():
                    one[...] = term[:, 0].reshape(out_rows, tile)
                    two[...] = term[:, 1].reshape(out_rows, tile)

        @pl.when(step == steps + tiles)
        def _():
            lane = lax.broadcasted_iota(jnp.int32, (1, EXT), 1)
            top = lax.broadcasted_iota(jnp.int32, (owner_rows, EXT), 0) == 0
            for ref, own in ((keep, sc[1]), (send, 1 - sc[1])):
                ref[...] = jnp.zeros_like(ref)
                for pair in range(pairs):
                    image = pair * N_CORE + own
                    line = jnp.where(lane == sc[2 + image], r_scr[pl.ds(image, 1), :], 0.0)
                    ref[pair * owner_rows : (pair + 1) * owner_rows, :EXT] = jnp.where(top, line, 0.0)

    row_at = lambda i: jnp.minimum(i, steps - 1)
    row_spec = lambda c: pl.BlockSpec((block, c), lambda i, s: (row_at(i), 0))
    far_spec = lambda f: pl.BlockSpec(
        (img_block, split_rows, lanes), lambda i, s: (jnp.clip(f(i), 0, half - 1), 0, 0)
    )
    out_spec = pl.BlockSpec((out_rows, tile), lambda i, s: (0, jnp.maximum(i - steps, 0)))
    out = jax.ShapeDtypeStruct((out_rows, cols + tile), jnp.float32)
    return pl.pallas_call(
        kernel,
        grid_spec=pltpu.PrefetchScalarGridSpec(
            num_scalar_prefetch=1,
            grid=(steps + tiles + 1,),
            in_specs=[
                row_spec(cols),
                pl.BlockSpec((width, block), lambda i, s: (0, row_at(i))),
                far_spec(lambda i: i),
                far_spec(lambda i: i - half),
                pl.BlockSpec((part, cols), lambda i, s: (lax.rem(s[0] + 2, n_part), 0)),
                row_spec(cols),
                row_spec(row_info.shape[1]),
            ],
            out_specs=[out_spec, out_spec],
            scratch_shapes=[
                pltpu.VMEM((width, rows), jnp.bfloat16),
                pltpu.VMEM((rows, cols), jnp.bfloat16),
                pltpu.VMEM((n_img, EXT), jnp.float32),
            ],
        ),
        out_shape=[out, out],
        compiler_params=params(),
        cost_estimate=pl.CostEstimate(
            flops=3 * rows * width * cols, bytes_accessed=30 * 2**20, transcendentals=0
        ),
        name="head_terms",
    )(scalars, near_pred, near_cols, far_a, far_b, head_weight, teacher, row_info)


def exponent(part):
    top = jnp.max(jnp.abs(part), axis=-1, keepdims=True)
    return jnp.ceil(jnp.log(jnp.maximum(top, 2.0**-100)) * 1.4426950408889634)


def code(main, extra):
    main_exp, extra_exp = exponent(main), exponent(extra)
    main_code = jnp.floor(main * jnp.exp2(14.0 - main_exp) + 0.5).astype(jnp.int32)
    extra_code = jnp.floor(extra * jnp.exp2(14.0 - extra_exp) + 0.5)
    lane = lax.broadcasted_iota(jnp.int32, extra.shape, 1)
    extra_code = jnp.where(
        lane == EXT - 2, main_exp, jnp.where(lane == EXT - 1, extra_exp, extra_code)
    ).astype(jnp.int32)
    return main_code.astype(jnp.int16), extra_code.astype(jnp.int16)


def decode(codes):
    cols = codes.shape[-1] - EXT
    wide = codes.astype(jnp.int32).astype(jnp.float32)
    main, extra = wide[:, :cols], wide[:, cols:]
    main_exp = extra[:, EXT - 2 : EXT - 1]
    extra_exp = extra[:, EXT - 1 :]
    lane = lax.broadcasted_iota(jnp.int32, extra.shape, 1)
    extra = jnp.where(lane < EXT - 2, extra, 0.0)
    return main * jnp.exp2(main_exp - 14.0), extra * jnp.exp2(extra_exp - 14.0)


def add_and_code(keep, received):
    rows, wide = keep.shape
    cols = wide - 2 * EXT
    block = rows // 8

    def kernel(a, b, out):
        main, extra = code(a[:, :cols] + b[:, :cols], a[:, cols : cols + EXT] + b[:, cols : cols + EXT])
        out[:, :cols] = main
        out[:, cols:] = extra

    spec = pl.BlockSpec((block, wide), lambda i: (i, 0))
    return pl.pallas_call(
        kernel,
        grid=(rows // block,),
        in_specs=[spec, spec],
        out_specs=pl.BlockSpec((block, cols + EXT), lambda i: (i, 0)),
        out_shape=jax.ShapeDtypeStruct((rows, cols + EXT), jnp.int16),
        compiler_params=params(),
        name="add_and_code",
    )(keep, received)


def sum_blocks(blocks):
    main, extra = decode(blocks[0])
    for block in blocks[1:]:
        m, e = decode(block)
        main, extra = main + m, extra + e
    return main, extra


def sum_last(received, partial):
    n, rows, wide = received.shape
    cols = wide - EXT
    block = n // 4

    def kernel(src, partial_ref, out, parts):
        main, extra = sum_blocks([src[k] for k in range(block)])
        regress = lax.broadcasted_iota(jnp.int32, partial.shape, 0) == 3

        @pl.when(pl.program_id(0) == 0)
        def _():
            out[...] = main
            parts[...] = jnp.where(regress, extra[:1], partial_ref[...])

        @pl.when(pl.program_id(0) > 0)
        def _():
            out[...] += main
            parts[...] += jnp.where(regress, extra[:1], 0.0)

    return pl.pallas_call(
        kernel,
        grid=(n // block,),
        in_specs=[
            pl.BlockSpec((block, rows, wide), lambda i: (i, 0, 0)),
            pl.BlockSpec(partial.shape, lambda i: (0, 0)),
        ],
        out_specs=[
            pl.BlockSpec((rows, cols), lambda i: (0, 0)),
            pl.BlockSpec(partial.shape, lambda i: (0, 0)),
        ],
        out_shape=[
            jax.ShapeDtypeStruct((rows, cols), jnp.float32),
            jax.ShapeDtypeStruct(partial.shape, jnp.float32),
        ],
        compiler_params=params(),
        name="sum_last",
    )(received, partial)


def local(
    student_feats,
    head_weight,
    teacher_cache,
    holder_index,
    valid_count,
    image_embed,
    text_embed,
    pair_ids,
):
    n_dp = lax.axis_size("dp")
    n_cache = lax.axis_size("cache")
    own_index = lax.axis_index("dp")
    cache_pos = lax.axis_index("cache")
    core = own_index % N_CORE
    img_dev, patch_rows, student_width = student_feats.shape
    slots, _, local_cols = teacher_cache.shape
    full_cols = local_cols * n_cache
    part = student_width // n_cache
    shard_rows, embed = image_embed.shape
    assert slots == n_dp and n_dp == N_X * N_Z * N_CORE

    def ring(x, step):
        return lax.ppermute(x, "cache", [(i, (i + step) % n_cache) for i in range(n_cache)])

    def flat(x):
        return x.reshape(-1, x.shape[-1])

    img_order = jnp.arange(img_dev, dtype=jnp.int32)
    outgoing = dispatch_rows(student_feats, holder_index, valid_count, own_index, cache_pos, part)

    def swap(x, bit):
        return lax.ppermute(x, "dp", [(i, i ^ bit) for i in range(n_dp)])

    def both(x, bit):
        other = swap(x, bit)
        upper = (own_index // bit) % 2 == 1
        return jnp.concatenate([jnp.where(upper, other, x), jnp.where(upper, x, other)])

    def spread(x, bit, count):
        blocks = [x] + [swap(x, bit * k) for k in range(1, 2**count)]
        for n in range(count):
            upper = (own_index // (bit * 2**n)) % 2 == 1
            blocks = [jnp.where(upper, blocks[k ^ 2**n], blocks[k]) for k in range(2**count)]
        return jnp.concatenate(blocks)

    outgoing, texts = lax.optimization_barrier((outgoing, text_embed))
    texts, teacher_in = lax.optimization_barrier((both(texts, 1), teacher_cache))

    with jax.named_scope("student_exchange"):
        mine = lax.all_to_all(outgoing, "dp", split_axis=0, concat_axis=0, tiled=True)
    with jax.named_scope("teacher_sums"):
        wide = teacher_in.astype(jnp.float32)
        sums = jnp.stack([jnp.sum(wide, axis=-1), jnp.sum(wide * wide, axis=-1)])
        pair_cols = jnp.concatenate(
            [
                (pair_ids // 64)[:, None],
                (pair_ids % 64)[:, None],
                jnp.zeros((shard_rows, EXT - 2), jnp.int32),
            ],
            axis=1,
        ).astype(jnp.float32)
        images = jnp.concatenate([image_embed.astype(jnp.float32), pair_cols], axis=1)
        packed = jnp.concatenate([sums.reshape(-1, EXT), images.reshape(-1, EXT)])
        packed = [packed] + [ring(packed, step) for step in range(1, n_cache)]
        n_sum = sums.size // EXT
        sums = sum(p[:n_sum] for p in packed).reshape(sums.shape)
        images = jnp.concatenate([p[n_sum:] for p in packed]).reshape(img_dev, embed + EXT)
    texts, sums, images = lax.optimization_barrier((texts, sums, images))
    texts = spread(texts, 4, 2)
    mine, sums, images, texts = lax.optimization_barrier((mine, sums, images, texts))
    with jax.named_scope("student_ring"):
        counts_sent, mine = mine[:, -COUNT_ROWS:], mine[:, :-COUNT_ROWS]
        from_prev = ring(mine, 1)
        from_next = ring(mine, -1)
        from_prev, from_next, sums, counts_sent = lax.optimization_barrier(
            (from_prev, from_next, sums, counts_sent)
        )
        far_a = ring(from_prev[: n_dp // 2], 1)
        far_b = ring(from_next[n_dp // 2 :], -1)
    near_pred, near_cols = near_terms(cache_pos, [mine, from_prev, from_next], head_weight)
    with jax.named_scope("teacher_sums"):
        row_mean = sums[0] / full_cols
        inv_scale = lax.rsqrt(sums[1] / full_cols - row_mean * row_mean + eps)

    is_held = holder_index.reshape(n_dp, img_dev) == own_index
    place_of = jnp.sum(jnp.where(is_held, img_order[None, :], 0), axis=1)
    held_any = jnp.sum(is_held.astype(jnp.int32), axis=1) > 0
    held_count = jnp.where(held_any, counts_sent[:, 0, 0].astype(jnp.float32), 0.0)
    row_index = jnp.arange(patch_rows, dtype=jnp.int32).astype(jnp.float32)
    valid_mask = (row_index[None, :] < held_count[:, None]).astype(jnp.float32)
    row_weight = valid_mask / jnp.maximum(held_count, 1.0)[:, None]
    coef = 2.0 * loss_scale / full_cols * row_weight
    inv_scale = jnp.where(held_count[:, None] > 0, inv_scale, 0.0)
    row_info = jnp.stack([row_mean, inv_scale, coef, row_weight], axis=-1).reshape(
        n_dp * patch_rows, 4
    )

    scalars = jnp.concatenate([jnp.stack([cache_pos, core]).astype(jnp.int32), place_of])
    keep, send = head_terms(
        scalars,
        near_pred,
        near_cols,
        far_a,
        far_b,
        head_weight,
        flat(teacher_cache),
        row_info,
        full_cols,
    )
    with jax.named_scope("grad_core"):
        received = swap(send, 1)
    texts = both(lax.optimization_barrier((texts, send))[0], 2)
    codes = add_and_code(keep, received)
    codes, images, texts = lax.optimization_barrier((codes, images, texts))
    texts = spread(texts, 2 * N_Z, 2)
    with jax.named_scope("contrast"):
        pairs = images[:, embed].astype(jnp.int32) * 64 + images[:, embed + 1].astype(jnp.int32)
        logits = jnp.dot(
            images[:, :embed].astype(jnp.bfloat16),
            texts.T,
            preferred_element_type=jnp.float32,
        ) * (embed ** (-0.5))
        column = jnp.arange(texts.shape[0], dtype=jnp.int32)
        text_dp = column // (16 * shard_rows) * 16
        for n, bit in enumerate((1, 4, 8, 2)):
            text_dp = text_dp + column // (shard_rows * 2**n) % 2 * bit
        text_id = text_dp * img_dev + cache_pos * shard_rows + column % shard_rows
        best = jnp.max(logits, axis=1)
        denom = jnp.sum(jnp.exp(logits - best[:, None]), axis=1)
        target = jnp.sum(jnp.where(pairs[:, None] == text_id[None, :], logits, 0.0), axis=1)
        partial = jnp.pad(jnp.stack([best, denom, target]), ((0, 5), (0, EXT - img_dev)))
    with jax.named_scope("grad_xz"):
        codes = lax.all_to_all(
            codes.reshape(N_X * N_Z, -1, local_cols + EXT), "dp", 0, 0, axis_index_groups=XZ_GROUPS, tiled=True
        )
    head_grad, parts = sum_last(codes, partial)

    with jax.named_scope("loss_parts"):
        parts = [parts] + [ring(parts, step) for step in range(1, n_cache)]
        partials = []
        for k, got in enumerate(parts):
            first = (n_cache - k) % n_cache * shard_rows
            partials.append(got[:3, first : first + shard_rows])
        partials = jnp.stack(partials)
        best = jnp.max(partials[:, 0], axis=0)
        denom = jnp.sum(partials[:, 1] * jnp.exp(partials[:, 0] - best[None, :]), axis=0)
        contrast = best + jnp.log(denom) - jnp.sum(partials[:, 2], axis=0)
        regress = sum(got[3] for got in parts)
        regress = lax.dynamic_slice_in_dim(regress, cache_pos * shard_rows, shard_rows, 0)
    return (head_grad, regress + contrast)


def solution(mesh):
    in_specs = (
        P("dp", None, None),
        P(None, "cache"),
        P("dp", None, "cache"),
        P(),
        P("dp"),
        P(("dp", "cache"), None),
        P(("dp", "cache"), None),
        P(("dp", "cache")),
    )
    out_specs = (P("dp", "cache"), P(("dp", "cache")))
    return jax.shard_map(local, mesh=mesh, in_specs=in_specs, out_specs=out_specs, check_vma=False)
```

```python
import jax
import jax.numpy as jnp
from jax import lax
from jax.experimental import pallas as pl
from jax.experimental.pallas import tpu as pltpu
from jax.sharding import PartitionSpec as P

eps = 1e-06
loss_scale = 128.0

N_X, N_Z, N_CORE = 4, 8, 2
EXT = 128
VMEM_BYTES = 62 * 1024 * 1024

XZ_GROUPS = [[k * N_CORE + c for k in range(N_X * N_Z)] for c in range(N_CORE)]


def params():
    return pltpu.CompilerParams(vmem_limit_bytes=VMEM_BYTES)


LANES = 128
COUNT_ROWS = 8


def dispatch_rows(student_feats, holder_index, valid_count, own_index, cache_pos, cols):
    images, rows, width = student_feats.shape
    n_dp = holder_index.shape[0] // images
    parts = cols // LANES

    def kernel(place, holders, counts, feats, out):
        out[...] = jnp.zeros_like(out)
        for i in range(images):
            h = holders[place[0] * images + i]
            for k in range(parts):
                out[h, k * rows : (k + 1) * rows, :] = feats[i, :, k * LANES : (k + 1) * LANES]
            count = jnp.full((COUNT_ROWS, LANES), counts[i].astype(jnp.float32))
            out[h, parts * rows :, :] = count.astype(out.dtype)

    out_rows = parts * rows + COUNT_ROWS
    return pl.pallas_call(
        kernel,
        grid_spec=pltpu.PrefetchScalarGridSpec(
            num_scalar_prefetch=3,
            grid=(1,),
            in_specs=[pl.BlockSpec((images, rows, cols), lambda i, p, h, c: (0, 0, p[1]))],
            out_specs=pl.BlockSpec((n_dp, out_rows, LANES), lambda i, p, h, c: (0, 0, 0)),
        ),
        out_shape=jax.ShapeDtypeStruct((n_dp, out_rows, LANES), student_feats.dtype),
        compiler_params=params(),
        name="dispatch_rows",
    )(jnp.stack([own_index, cache_pos]).astype(jnp.int32), holder_index, valid_count, student_feats)


def near_terms(cache_pos, near, head_weight):
    n_img, split_rows, lanes = near[0].shape
    width, cols = head_weight.shape
    block, patch = 512, 32
    splits = split_rows // patch
    part = splits * lanes
    n_part = width // part
    rows = n_img * patch
    img_block = block // patch

    def kernel(sc, x0, x1, x2, w_ref, pred_out, xt_out):
        xt_out[...] = jnp.zeros_like(xt_out)
        pred = jnp.zeros((block, cols), jnp.float32)
        for ref, off in ((x0, 0), (x1, n_part - 1), (x2, 1)):
            first = lax.rem(sc[0] + off, n_part) * part
            pieces = [
                ref[:, k * patch : (k + 1) * patch, :].reshape(block, lanes) for k in range(splits)
            ]
            for k, piece in enumerate(pieces):
                xt_out[pl.ds(pl.multiple_of(first + k * lanes, lanes), lanes), :] = piece.T
            pred = pred + jnp.dot(
                jnp.concatenate(pieces, axis=1),
                w_ref[pl.ds(pl.multiple_of(first, part), part), :],
                preferred_element_type=jnp.float32,
            )
        pred_out[...] = pred

    img_spec = pl.BlockSpec((img_block, split_rows, lanes), lambda i, s: (i, 0, 0))
    return pl.pallas_call(
        kernel,
        grid_spec=pltpu.PrefetchScalarGridSpec(
            num_scalar_prefetch=1,
            grid=(rows // block,),
            in_specs=[img_spec] * 3 + [pl.BlockSpec((width, cols), lambda i, s: (0, 0))],
            out_specs=[
                pl.BlockSpec((block, cols), lambda i, s: (i, 0)),
                pl.BlockSpec((width, block), lambda i, s: (0, i)),
            ],
        ),
        out_shape=[
            jax.ShapeDtypeStruct((rows, cols), jnp.float32),
            jax.ShapeDtypeStruct((width, rows), near[0].dtype),
        ],
        compiler_params=params(),
        cost_estimate=pl.CostEstimate(
            flops=2 * rows * 3 * part * cols, bytes_accessed=20 * 2**20, transcendentals=0
        ),
        name="near_terms",
    )(cache_pos[None].astype(jnp.int32), *near, head_weight)


def head_terms(scalars, near_pred, near_cols, far_a, far_b, head_weight, teacher, row_info, full_cols):
    half_img, split_rows, lanes = far_a.shape
    n_img = 2 * half_img
    width, cols = head_weight.shape
    block, tile, patch = 512, 256, 32
    splits = split_rows // patch
    part = splits * lanes
    rows = n_img * patch
    n_part = width // part
    steps, tiles = rows // block, cols // tile
    half = steps // 2
    img_block = block // patch
    pairs = N_X * N_Z
    owner_rows = width // (pairs * N_CORE)
    out_rows = width // N_CORE

    def kernel(sc, pred_ref, xt_ref, fa, fb, w_ref, t_ref, info_ref, keep, send, x_scr, g_scr, r_scr):
        step = pl.program_id(0)

        @pl.when(step < steps)
        def _():
            here = pl.ds(pl.multiple_of(step * block, block), block)
            far = jnp.where(step < half, fa[...], fb[...])
            pieces = [far[:, k * patch : (k + 1) * patch, :].reshape(block, lanes) for k in range(splits)]
            x_scr[:, here] = xt_ref[...]
            first = lax.rem(sc[0] + 2, n_part) * part
            for k, piece in enumerate(pieces):
                x_scr[pl.ds(pl.multiple_of(first + k * lanes, lanes), lanes), here] = piece.T
            pred = pred_ref[...] + jnp.dot(
                jnp.concatenate(pieces, axis=1), w_ref[...], preferred_element_type=jnp.float32
            )
            info = info_ref[...]
            mean, inv, coef, weight = (info[:, k : k + 1] for k in range(4))
            residue = pred - (t_ref[...].astype(jnp.float32) - mean) * inv
            g_scr[here, :] = (coef * residue).astype(jnp.bfloat16)
            row_loss = weight * jnp.sum(residue * residue, axis=-1, keepdims=True)
            row_loss = jnp.broadcast_to(row_loss, (block, EXT)).reshape(img_block, patch, EXT)
            r_scr[pl.ds(pl.multiple_of(step * img_block, img_block), img_block), :] = (
                jnp.sum(row_loss, axis=1) / full_cols
            )

        @pl.when((step >= steps) & (step < steps + tiles))
        def _():
            first = pl.multiple_of((step - steps) * tile, tile)
            term = jnp.dot(x_scr[...], g_scr[:, pl.ds(first, tile)], preferred_element_type=jnp.float32)
            term = term.reshape(pairs, N_CORE, owner_rows, tile)
            for mine, (one, two) in enumerate(((keep, send), (send, keep))):

                @pl.when(sc[1] == mine)
                def _():
                    one[...] = term[:, 0].reshape(out_rows, tile)
                    two[...] = term[:, 1].reshape(out_rows, tile)

        @pl.when(step == steps + tiles)
        def _():
            lane = lax.broadcasted_iota(jnp.int32, (1, EXT), 1)
            top = lax.broadcasted_iota(jnp.int32, (owner_rows, EXT), 0) == 0
            for ref, own in ((keep, sc[1]), (send, 1 - sc[1])):
                ref[...] = jnp.zeros_like(ref)
                for pair in range(pairs):
                    image = pair * N_CORE + own
                    line = jnp.where(lane == sc[2 + image], r_scr[pl.ds(image, 1), :], 0.0)
                    ref[pair * owner_rows : (pair + 1) * owner_rows, :EXT] = jnp.where(top, line, 0.0)

    row_at = lambda i: jnp.minimum(i, steps - 1)
    row_spec = lambda c: pl.BlockSpec((block, c), lambda i, s: (row_at(i), 0))
    far_spec = lambda f: pl.BlockSpec(
        (img_block, split_rows, lanes), lambda i, s: (jnp.clip(f(i), 0, half - 1), 0, 0)
    )
    out_spec = pl.BlockSpec((out_rows, tile), lambda i, s: (0, jnp.maximum(i - steps, 0)))
    out = jax.ShapeDtypeStruct((out_rows, cols + tile), jnp.float32)
    return pl.pallas_call(
        kernel,
        grid_spec=pltpu.PrefetchScalarGridSpec(
            num_scalar_prefetch=1,
            grid=(steps + tiles + 1,),
            in_specs=[
                row_spec(cols),
                pl.BlockSpec((width, block), lambda i, s: (0, row_at(i))),
                far_spec(lambda i: i),
                far_spec(lambda i: i - half),
                pl.BlockSpec((part, cols), lambda i, s: (lax.rem(s[0] + 2, n_part), 0)),
                row_spec(cols),
                row_spec(row_info.shape[1]),
            ],
            out_specs=[out_spec, out_spec],
            scratch_shapes=[
                pltpu.VMEM((width, rows), jnp.bfloat16),
                pltpu.VMEM((rows, cols), jnp.bfloat16),
                pltpu.VMEM((n_img, EXT), jnp.float32),
            ],
        ),
        out_shape=[out, out],
        compiler_params=params(),
        cost_estimate=pl.CostEstimate(
            flops=3 * rows * width * cols, bytes_accessed=30 * 2**20, transcendentals=0
        ),
        name="head_terms",
    )(scalars, near_pred, near_cols, far_a, far_b, head_weight, teacher, row_info)


def exponent(part):
    top = jnp.max(jnp.abs(part), axis=-1, keepdims=True)
    return jnp.ceil(jnp.log(jnp.maximum(top, 2.0**-100)) * 1.4426950408889634)


def code(main, extra):
    main_exp, extra_exp = exponent(main), exponent(extra)
    main_code = jnp.floor(main * jnp.exp2(14.0 - main_exp) + 0.5).astype(jnp.int32)
    extra_code = jnp.floor(extra * jnp.exp2(14.0 - extra_exp) + 0.5)
    lane = lax.broadcasted_iota(jnp.int32, extra.shape, 1)
    extra_code = jnp.where(
        lane == EXT - 2, main_exp, jnp.where(lane == EXT - 1, extra_exp, extra_code)
    ).astype(jnp.int32)
    return main_code.astype(jnp.int16), extra_code.astype(jnp.int16)


def decode(codes):
    cols = codes.shape[-1] - EXT
    wide = codes.astype(jnp.int32).astype(jnp.float32)
    main, extra = wide[:, :cols], wide[:, cols:]
    main_exp = extra[:, EXT - 2 : EXT - 1]
    extra_exp = extra[:, EXT - 1 :]
    lane = lax.broadcasted_iota(jnp.int32, extra.shape, 1)
    extra = jnp.where(lane < EXT - 2, extra, 0.0)
    return main * jnp.exp2(main_exp - 14.0), extra * jnp.exp2(extra_exp - 14.0)


def add_and_code(keep, received):
    rows, wide = keep.shape
    cols = wide - 2 * EXT
    block = rows // 2

    def kernel(a, b, out):
        main, extra = code(a[:, :cols] + b[:, :cols], a[:, cols : cols + EXT] + b[:, cols : cols + EXT])
        out[:, :cols] = main
        out[:, cols:] = extra

    spec = pl.BlockSpec((block, wide), lambda i: (i, 0))
    return pl.pallas_call(
        kernel,
        grid=(rows // block,),
        in_specs=[spec, spec],
        out_specs=pl.BlockSpec((block, cols + EXT), lambda i: (i, 0)),
        out_shape=jax.ShapeDtypeStruct((rows, cols + EXT), jnp.int16),
        compiler_params=params(),
        name="add_and_code",
    )(keep, received)


def sum_blocks(blocks):
    main, extra = decode(blocks[0])
    for block in blocks[1:]:
        m, e = decode(block)
        main, extra = main + m, extra + e
    return main, extra


def sum_last(received, partial):
    n, rows, wide = received.shape

    def kernel(src, partial_ref, out, parts):
        main, extra = sum_blocks([src[k] for k in range(n)])
        out[...] = main
        row = lax.broadcasted_iota(jnp.int32, partial.shape, 0)
        parts[...] = jnp.where(row == 3, extra[:1], partial_ref[...])

    return pl.pallas_call(
        kernel,
        out_shape=[
            jax.ShapeDtypeStruct((rows, wide - EXT), jnp.float32),
            jax.ShapeDtypeStruct(partial.shape, jnp.float32),
        ],
        compiler_params=params(),
        name="sum_last",
    )(received, partial)


def local(
    student_feats,
    head_weight,
    teacher_cache,
    holder_index,
    valid_count,
    image_embed,
    text_embed,
    pair_ids,
):
    n_dp = lax.axis_size("dp")
    n_cache = lax.axis_size("cache")
    own_index = lax.axis_index("dp")
    cache_pos = lax.axis_index("cache")
    core = own_index % N_CORE
    img_dev, patch_rows, student_width = student_feats.shape
    slots, _, local_cols = teacher_cache.shape
    full_cols = local_cols * n_cache
    part = student_width // n_cache
    shard_rows, embed = image_embed.shape
    assert slots == n_dp and n_dp == N_X * N_Z * N_CORE

    def ring(x, step):
        return lax.ppermute(x, "cache", [(i, (i + step) % n_cache) for i in range(n_cache)])

    def flat(x):
        return x.reshape(-1, x.shape[-1])

    img_order = jnp.arange(img_dev, dtype=jnp.int32)
    outgoing = dispatch_rows(student_feats, holder_index, valid_count, own_index, cache_pos, part)

    def swap(x, bit):
        return lax.ppermute(x, "dp", [(i, i ^ bit) for i in range(n_dp)])

    def both(x, bit):
        other = swap(x, bit)
        upper = (own_index // bit) % 2 == 1
        return jnp.concatenate([jnp.where(upper, other, x), jnp.where(upper, x, other)])

    def spread(x, bit, count):
        blocks = [x] + [swap(x, bit * k) for k in range(1, 2**count)]
        for n in range(count):
            upper = (own_index // (bit * 2**n)) % 2 == 1
            blocks = [jnp.where(upper, blocks[k ^ 2**n], blocks[k]) for k in range(2**count)]
        return jnp.concatenate(blocks)

    outgoing, texts = lax.optimization_barrier((outgoing, text_embed))
    texts, teacher_in = lax.optimization_barrier((both(texts, 1), teacher_cache))

    with jax.named_scope("student_exchange"):
        mine = lax.all_to_all(outgoing, "dp", split_axis=0, concat_axis=0, tiled=True)
    with jax.named_scope("teacher_sums"):
        wide = teacher_in.astype(jnp.float32)
        sums = jnp.stack([jnp.sum(wide, axis=-1), jnp.sum(wide * wide, axis=-1)])
        pair_cols = jnp.concatenate(
            [
                (pair_ids // 64)[:, None],
                (pair_ids % 64)[:, None],
                jnp.zeros((shard_rows, EXT - 2), jnp.int32),
            ],
            axis=1,
        ).astype(jnp.float32)
        images = jnp.concatenate([image_embed.astype(jnp.float32), pair_cols], axis=1)
        packed = jnp.concatenate([sums.reshape(-1, EXT), images.reshape(-1, EXT)])
        packed = [packed] + [ring(packed, step) for step in range(1, n_cache)]
        n_sum = sums.size // EXT
        sums = sum(p[:n_sum] for p in packed).reshape(sums.shape)
        images = jnp.concatenate([p[n_sum:] for p in packed]).reshape(img_dev, embed + EXT)
    texts, sums, images = lax.optimization_barrier((texts, sums, images))
    texts = spread(texts, 4, 2)
    mine, sums, images, texts = lax.optimization_barrier((mine, sums, images, texts))
    with jax.named_scope("student_ring"):
        counts_sent, mine = mine[:, -COUNT_ROWS:], mine[:, :-COUNT_ROWS]
        from_prev = ring(mine, 1)
        from_next = ring(mine, -1)
        from_prev, from_next, sums, counts_sent = lax.optimization_barrier(
            (from_prev, from_next, sums, counts_sent)
        )
        far_a = ring(from_prev[: n_dp // 2], 1)
        far_b = ring(from_next[n_dp // 2 :], -1)
    near_pred, near_cols = near_terms(cache_pos, [mine, from_prev, from_next], head_weight)
    with jax.named_scope("teacher_sums"):
        row_mean = sums[0] / full_cols
        inv_scale = lax.rsqrt(sums[1] / full_cols - row_mean * row_mean + eps)

    is_held = holder_index.reshape(n_dp, img_dev) == own_index
    place_of = jnp.sum(jnp.where(is_held, img_order[None, :], 0), axis=1)
    held_any = jnp.sum(is_held.astype(jnp.int32), axis=1) > 0
    held_count = jnp.where(held_any, counts_sent[:, 0, 0].astype(jnp.float32), 0.0)
    row_index = jnp.arange(patch_rows, dtype=jnp.int32).astype(jnp.float32)
    valid_mask = (row_index[None, :] < held_count[:, None]).astype(jnp.float32)
    row_weight = valid_mask / jnp.maximum(held_count, 1.0)[:, None]
    coef = 2.0 * loss_scale / full_cols * row_weight
    inv_scale = jnp.where(held_count[:, None] > 0, inv_scale, 0.0)
    row_info = jnp.stack([row_mean, inv_scale, coef, row_weight], axis=-1).reshape(
        n_dp * patch_rows, 4
    )

    scalars = jnp.concatenate([jnp.stack([cache_pos, core]).astype(jnp.int32), place_of])
    keep, send = head_terms(
        scalars,
        near_pred,
        near_cols,
        far_a,
        far_b,
        head_weight,
        flat(teacher_cache),
        row_info,
        full_cols,
    )
    with jax.named_scope("grad_core"):
        received = swap(send, 1)
    texts = both(lax.optimization_barrier((texts, send))[0], 2)
    codes = add_and_code(keep, received)
    codes, images, texts = lax.optimization_barrier((codes, images, texts))
    texts = spread(texts, 2 * N_Z, 2)
    with jax.named_scope("contrast"):
        pairs = images[:, embed].astype(jnp.int32) * 64 + images[:, embed + 1].astype(jnp.int32)
        logits = jnp.dot(
            images[:, :embed].astype(jnp.bfloat16),
            texts.T,
            preferred_element_type=jnp.float32,
        ) * (embed ** (-0.5))
        column = jnp.arange(texts.shape[0], dtype=jnp.int32)
        text_dp = column // (16 * shard_rows) * 16
        for n, bit in enumerate((1, 4, 8, 2)):
            text_dp = text_dp + column // (shard_rows * 2**n) % 2 * bit
        text_id = text_dp * img_dev + cache_pos * shard_rows + column % shard_rows
        best = jnp.max(logits, axis=1)
        denom = jnp.sum(jnp.exp(logits - best[:, None]), axis=1)
        target = jnp.sum(jnp.where(pairs[:, None] == text_id[None, :], logits, 0.0), axis=1)
        partial = jnp.pad(jnp.stack([best, denom, target]), ((0, 5), (0, EXT - img_dev)))
    with jax.named_scope("grad_xz"):
        codes = lax.all_to_all(
            codes.reshape(N_X * N_Z, -1, local_cols + EXT), "dp", 0, 0, axis_index_groups=XZ_GROUPS, tiled=True
        )
    head_grad, parts = sum_last(codes, partial)

    with jax.named_scope("loss_parts"):
        parts = [parts] + [ring(parts, step) for step in range(1, n_cache)]
        partials = []
        for k, got in enumerate(parts):
            first = (n_cache - k) % n_cache * shard_rows
            partials.append(got[:3, first : first + shard_rows])
        partials = jnp.stack(partials)
        best = jnp.max(partials[:, 0], axis=0)
        denom = jnp.sum(partials[:, 1] * jnp.exp(partials[:, 0] - best[None, :]), axis=0)
        contrast = best + jnp.log(denom) - jnp.sum(partials[:, 2], axis=0)
        regress = sum(got[3] for got in parts)
        regress = lax.dynamic_slice_in_dim(regress, cache_pos * shard_rows, shard_rows, 0)
    return (head_grad, regress + contrast)


def solution(mesh):
    in_specs = (
        P("dp", None, None),
        P(None, "cache"),
        P("dp", None, "cache"),
        P(),
        P("dp"),
        P(("dp", "cache"), None),
        P(("dp", "cache"), None),
        P(("dp", "cache")),
    )
    out_specs = (P("dp", "cache"), P(("dp", "cache")))
    return jax.shard_map(local, mesh=mesh, in_specs=in_specs, out_specs=out_specs, check_vma=False)
```

```python
import jax
import jax.numpy as jnp
from jax import lax
from jax.experimental import pallas as pl
from jax.experimental.pallas import tpu as pltpu
from jax.sharding import PartitionSpec as P

eps = 1e-06
loss_scale = 128.0

N_X, N_Z, N_CORE = 4, 8, 2
EXT = 128
VMEM_BYTES = 62 * 1024 * 1024

XZ_GROUPS = [[k * N_CORE + c for k in range(N_X * N_Z)] for c in range(N_CORE)]


def params():
    return pltpu.CompilerParams(vmem_limit_bytes=VMEM_BYTES)


LANES = 128
COUNT_ROWS = 8


def dispatch_rows(student_feats, holder_index, valid_count, own_index, cache_pos, cols):
    images, rows, width = student_feats.shape
    n_dp = holder_index.shape[0] // images
    parts = cols // LANES

    def kernel(place, holders, counts, feats, out):
        out[...] = jnp.zeros_like(out)
        for i in range(images):
            h = holders[place[0] * images + i]
            for k in range(parts):
                out[h, k * rows : (k + 1) * rows, :] = feats[i, :, k * LANES : (k + 1) * LANES]
            count = jnp.full((COUNT_ROWS, LANES), counts[i].astype(jnp.float32))
            out[h, parts * rows :, :] = count.astype(out.dtype)

    out_rows = parts * rows + COUNT_ROWS
    return pl.pallas_call(
        kernel,
        grid_spec=pltpu.PrefetchScalarGridSpec(
            num_scalar_prefetch=3,
            grid=(1,),
            in_specs=[pl.BlockSpec((images, rows, cols), lambda i, p, h, c: (0, 0, p[1]))],
            out_specs=pl.BlockSpec((n_dp, out_rows, LANES), lambda i, p, h, c: (0, 0, 0)),
        ),
        out_shape=jax.ShapeDtypeStruct((n_dp, out_rows, LANES), student_feats.dtype),
        compiler_params=params(),
        name="dispatch_rows",
    )(jnp.stack([own_index, cache_pos]).astype(jnp.int32), holder_index, valid_count, student_feats)


def near_terms(cache_pos, near, head_weight):
    half_img, split_rows, lanes = near[0][0].shape
    n_img = 2 * half_img
    width, cols = head_weight.shape
    block, patch = 512, 32
    splits = split_rows // patch
    part = splits * lanes
    n_part = width // part
    rows = n_img * patch
    img_block = block // patch

    half = rows // block // 2

    def kernel(sc, x0a, x0b, x1a, x1b, x2a, x2b, w_ref, pred_out, xt_out):
        xt_out[...] = jnp.zeros_like(xt_out)
        lower = pl.program_id(0) < half
        pred = jnp.zeros((block, cols), jnp.float32)
        for a, b, off in ((x0a, x0b, 0), (x1a, x1b, n_part - 1), (x2a, x2b, 1)):
            first = lax.rem(sc[0] + off, n_part) * part
            x = jnp.where(lower, a[...], b[...])
            pieces = [x[:, k * patch : (k + 1) * patch, :].reshape(block, lanes) for k in range(splits)]
            for k, piece in enumerate(pieces):
                xt_out[pl.ds(pl.multiple_of(first + k * lanes, lanes), lanes), :] = piece.T
            pred = pred + jnp.dot(
                jnp.concatenate(pieces, axis=1),
                w_ref[pl.ds(pl.multiple_of(first, part), part), :],
                preferred_element_type=jnp.float32,
            )
        pred_out[...] = pred

    img_spec = lambda f: pl.BlockSpec(
        (img_block, split_rows, lanes), lambda i, s: (jnp.clip(f(i), 0, half - 1), 0, 0)
    )
    halves = [img_spec(lambda i: i), img_spec(lambda i: i - half)]
    return pl.pallas_call(
        kernel,
        grid_spec=pltpu.PrefetchScalarGridSpec(
            num_scalar_prefetch=1,
            grid=(rows // block,),
            in_specs=halves * 3 + [pl.BlockSpec((width, cols), lambda i, s: (0, 0))],
            out_specs=[
                pl.BlockSpec((block, cols), lambda i, s: (i, 0)),
                pl.BlockSpec((width, block), lambda i, s: (0, i)),
            ],
        ),
        out_shape=[
            jax.ShapeDtypeStruct((rows, cols), jnp.float32),
            jax.ShapeDtypeStruct((width, rows), near[0][0].dtype),
        ],
        compiler_params=params(),
        cost_estimate=pl.CostEstimate(
            flops=2 * rows * 3 * part * cols, bytes_accessed=20 * 2**20, transcendentals=0
        ),
        name="near_terms",
    )(cache_pos[None].astype(jnp.int32), *[x for pair in near for x in pair], head_weight)


def head_terms(scalars, near_pred, near_cols, far_a, far_b, head_weight, teacher, row_info, full_cols):
    half_img, split_rows, lanes = far_a.shape
    n_img = 2 * half_img
    width, cols = head_weight.shape
    block, tile, patch = 512, 256, 32
    splits = split_rows // patch
    part = splits * lanes
    rows = n_img * patch
    n_part = width // part
    steps, tiles = rows // block, cols // tile
    half = steps // 2
    img_block = block // patch
    pairs = N_X * N_Z
    owner_rows = width // (pairs * N_CORE)
    out_rows = width // N_CORE

    def kernel(sc, pred_ref, xt_ref, fa, fb, w_ref, t_ref, info_ref, keep, send, x_scr, g_scr, r_scr):
        step = pl.program_id(0)

        @pl.when(step < steps)
        def _():
            here = pl.ds(pl.multiple_of(step * block, block), block)
            far = jnp.where(step < half, fa[...], fb[...])
            pieces = [far[:, k * patch : (k + 1) * patch, :].reshape(block, lanes) for k in range(splits)]
            x_scr[:, here] = xt_ref[...]
            first = lax.rem(sc[0] + 2, n_part) * part
            for k, piece in enumerate(pieces):
                x_scr[pl.ds(pl.multiple_of(first + k * lanes, lanes), lanes), here] = piece.T
            pred = pred_ref[...] + jnp.dot(
                jnp.concatenate(pieces, axis=1), w_ref[...], preferred_element_type=jnp.float32
            )
            info = info_ref[...]
            mean, inv, coef, weight = (info[:, k : k + 1] for k in range(4))
            residue = pred - (t_ref[...].astype(jnp.float32) - mean) * inv
            g_scr[here, :] = (coef * residue).astype(jnp.bfloat16)
            row_loss = weight * jnp.sum(residue * residue, axis=-1, keepdims=True)
            row_loss = jnp.broadcast_to(row_loss, (block, EXT)).reshape(img_block, patch, EXT)
            r_scr[pl.ds(pl.multiple_of(step * img_block, img_block), img_block), :] = (
                jnp.sum(row_loss, axis=1) / full_cols
            )

        @pl.when((step >= steps) & (step < steps + tiles))
        def _():
            first = pl.multiple_of((step - steps) * tile, tile)
            term = jnp.dot(x_scr[...], g_scr[:, pl.ds(first, tile)], preferred_element_type=jnp.float32)
            term = term.reshape(pairs, N_CORE, owner_rows, tile)
            for mine, (one, two) in enumerate(((keep, send), (send, keep))):

                @pl.when(sc[1] == mine)
                def _():
                    one[...] = term[:, 0].reshape(out_rows, tile)
                    two[...] = term[:, 1].reshape(out_rows, tile)

        @pl.when(step == steps + tiles)
        def _():
            lane = lax.broadcasted_iota(jnp.int32, (1, EXT), 1)
            top = lax.broadcasted_iota(jnp.int32, (owner_rows, EXT), 0) == 0
            for ref, own in ((keep, sc[1]), (send, 1 - sc[1])):
                ref[...] = jnp.zeros_like(ref)
                for pair in range(pairs):
                    image = pair * N_CORE + own
                    line = jnp.where(lane == sc[2 + image], r_scr[pl.ds(image, 1), :], 0.0)
                    ref[pair * owner_rows : (pair + 1) * owner_rows, :EXT] = jnp.where(top, line, 0.0)

    row_at = lambda i: jnp.minimum(i, steps - 1)
    row_spec = lambda c: pl.BlockSpec((block, c), lambda i, s: (row_at(i), 0))
    far_spec = lambda f: pl.BlockSpec(
        (img_block, split_rows, lanes), lambda i, s: (jnp.clip(f(i), 0, half - 1), 0, 0)
    )
    out_spec = pl.BlockSpec((out_rows, tile), lambda i, s: (0, jnp.maximum(i - steps, 0)))
    out = jax.ShapeDtypeStruct((out_rows, cols + tile), jnp.float32)
    return pl.pallas_call(
        kernel,
        grid_spec=pltpu.PrefetchScalarGridSpec(
            num_scalar_prefetch=1,
            grid=(steps + tiles + 1,),
            in_specs=[
                row_spec(cols),
                pl.BlockSpec((width, block), lambda i, s: (0, row_at(i))),
                far_spec(lambda i: i),
                far_spec(lambda i: i - half),
                pl.BlockSpec((part, cols), lambda i, s: (lax.rem(s[0] + 2, n_part), 0)),
                row_spec(cols),
                row_spec(row_info.shape[1]),
            ],
            out_specs=[out_spec, out_spec],
            scratch_shapes=[
                pltpu.VMEM((width, rows), jnp.bfloat16),
                pltpu.VMEM((rows, cols), jnp.bfloat16),
                pltpu.VMEM((n_img, EXT), jnp.float32),
            ],
        ),
        out_shape=[out, out],
        compiler_params=params(),
        cost_estimate=pl.CostEstimate(
            flops=3 * rows * width * cols, bytes_accessed=30 * 2**20, transcendentals=0
        ),
        name="head_terms",
    )(scalars, near_pred, near_cols, far_a, far_b, head_weight, teacher, row_info)


def exponent(part):
    top = jnp.max(jnp.abs(part), axis=-1, keepdims=True)
    return jnp.ceil(jnp.log(jnp.maximum(top, 2.0**-100)) * 1.4426950408889634)


def code(main, extra):
    main_exp, extra_exp = exponent(main), exponent(extra)
    main_code = jnp.floor(main * jnp.exp2(14.0 - main_exp) + 0.5).astype(jnp.int32)
    extra_code = jnp.floor(extra * jnp.exp2(14.0 - extra_exp) + 0.5)
    lane = lax.broadcasted_iota(jnp.int32, extra.shape, 1)
    extra_code = jnp.where(
        lane == EXT - 2, main_exp, jnp.where(lane == EXT - 1, extra_exp, extra_code)
    ).astype(jnp.int32)
    return main_code.astype(jnp.int16), extra_code.astype(jnp.int16)


def decode(codes):
    cols = codes.shape[-1] - EXT
    wide = codes.astype(jnp.int32).astype(jnp.float32)
    main, extra = wide[:, :cols], wide[:, cols:]
    main_exp = extra[:, EXT - 2 : EXT - 1]
    extra_exp = extra[:, EXT - 1 :]
    lane = lax.broadcasted_iota(jnp.int32, extra.shape, 1)
    extra = jnp.where(lane < EXT - 2, extra, 0.0)
    return main * jnp.exp2(main_exp - 14.0), extra * jnp.exp2(extra_exp - 14.0)


def add_and_code(keep, received):
    rows, wide = keep.shape
    cols = wide - 2 * EXT
    block = rows // 2

    def kernel(a, b, out):
        main, extra = code(a[:, :cols] + b[:, :cols], a[:, cols : cols + EXT] + b[:, cols : cols + EXT])
        out[:, :cols] = main
        out[:, cols:] = extra

    spec = pl.BlockSpec((block, wide), lambda i: (i, 0))
    return pl.pallas_call(
        kernel,
        grid=(rows // block,),
        in_specs=[spec, spec],
        out_specs=pl.BlockSpec((block, cols + EXT), lambda i: (i, 0)),
        out_shape=jax.ShapeDtypeStruct((rows, cols + EXT), jnp.int16),
        compiler_params=params(),
        name="add_and_code",
    )(keep, received)


def sum_blocks(blocks):
    main, extra = decode(blocks[0])
    for block in blocks[1:]:
        m, e = decode(block)
        main, extra = main + m, extra + e
    return main, extra


def sum_last(received, partial):
    n, rows, wide = received.shape

    def kernel(src, partial_ref, out, parts):
        main, extra = sum_blocks([src[k] for k in range(n)])
        out[...] = main
        row = lax.broadcasted_iota(jnp.int32, partial.shape, 0)
        parts[...] = jnp.where(row == 3, extra[:1], partial_ref[...])

    return pl.pallas_call(
        kernel,
        out_shape=[
            jax.ShapeDtypeStruct((rows, wide - EXT), jnp.float32),
            jax.ShapeDtypeStruct(partial.shape, jnp.float32),
        ],
        compiler_params=params(),
        name="sum_last",
    )(received, partial)


def local(
    student_feats,
    head_weight,
    teacher_cache,
    holder_index,
    valid_count,
    image_embed,
    text_embed,
    pair_ids,
):
    n_dp = lax.axis_size("dp")
    n_cache = lax.axis_size("cache")
    own_index = lax.axis_index("dp")
    cache_pos = lax.axis_index("cache")
    core = own_index % N_CORE
    img_dev, patch_rows, student_width = student_feats.shape
    slots, _, local_cols = teacher_cache.shape
    full_cols = local_cols * n_cache
    part = student_width // n_cache
    shard_rows, embed = image_embed.shape
    assert slots == n_dp and n_dp == N_X * N_Z * N_CORE

    def ring(x, step):
        return lax.ppermute(x, "cache", [(i, (i + step) % n_cache) for i in range(n_cache)])

    def flat(x):
        return x.reshape(-1, x.shape[-1])

    img_order = jnp.arange(img_dev, dtype=jnp.int32)
    outgoing = dispatch_rows(student_feats, holder_index, valid_count, own_index, cache_pos, part)

    def swap(x, bit):
        return lax.ppermute(x, "dp", [(i, i ^ bit) for i in range(n_dp)])

    def both(x, bit):
        other = swap(x, bit)
        upper = (own_index // bit) % 2 == 1
        return jnp.concatenate([jnp.where(upper, other, x), jnp.where(upper, x, other)])

    def spread(x, bit, count):
        blocks = [x] + [swap(x, bit * k) for k in range(1, 2**count)]
        for n in range(count):
            upper = (own_index // (bit * 2**n)) % 2 == 1
            blocks = [jnp.where(upper, blocks[k ^ 2**n], blocks[k]) for k in range(2**count)]
        return jnp.concatenate(blocks)

    outgoing, texts = lax.optimization_barrier((outgoing, text_embed))
    texts, teacher_in = lax.optimization_barrier((both(texts, 1), teacher_cache))

    with jax.named_scope("student_exchange"):
        mine = lax.all_to_all(outgoing, "dp", split_axis=0, concat_axis=0, tiled=True)
    with jax.named_scope("teacher_sums"):
        wide = teacher_in.astype(jnp.float32)
        sums = jnp.stack([jnp.sum(wide, axis=-1), jnp.sum(wide * wide, axis=-1)])
        pair_cols = jnp.concatenate(
            [
                (pair_ids // 64)[:, None],
                (pair_ids % 64)[:, None],
                jnp.zeros((shard_rows, EXT - 2), jnp.int32),
            ],
            axis=1,
        ).astype(jnp.float32)
        images = jnp.concatenate([image_embed.astype(jnp.float32), pair_cols], axis=1)
        packed = jnp.concatenate([sums.reshape(-1, EXT), images.reshape(-1, EXT)])
        packed = [packed] + [ring(packed, step) for step in range(1, n_cache)]
        n_sum = sums.size // EXT
        sums = sum(p[:n_sum] for p in packed).reshape(sums.shape)
        images = jnp.concatenate([p[n_sum:] for p in packed]).reshape(img_dev, embed + EXT)
    texts, sums, images = lax.optimization_barrier((texts, sums, images))
    texts = spread(texts, 4, 2)
    mine, sums, images, texts = lax.optimization_barrier((mine, sums, images, texts))
    with jax.named_scope("student_ring"):
        counts_sent = mine[:, -COUNT_ROWS:]
        own = [mine[: n_dp // 2, :-COUNT_ROWS], mine[n_dp // 2 :, :-COUNT_ROWS]]
        from_prev = [ring(x, 1) for x in own]
        from_next = [ring(x, -1) for x in own]
        from_prev, from_next, sums, counts_sent = lax.optimization_barrier(
            (from_prev, from_next, sums, counts_sent)
        )
        far_a = ring(from_prev[0], 1)
        far_b = ring(from_next[1], -1)
    near_pred, near_cols = near_terms(cache_pos, [own, from_prev, from_next], head_weight)
    with jax.named_scope("teacher_sums"):
        row_mean = sums[0] / full_cols
        inv_scale = lax.rsqrt(sums[1] / full_cols - row_mean * row_mean + eps)

    is_held = holder_index.reshape(n_dp, img_dev) == own_index
    place_of = jnp.sum(jnp.where(is_held, img_order[None, :], 0), axis=1)
    held_any = jnp.sum(is_held.astype(jnp.int32), axis=1) > 0
    held_count = jnp.where(held_any, counts_sent[:, 0, 0].astype(jnp.float32), 0.0)
    row_index = jnp.arange(patch_rows, dtype=jnp.int32).astype(jnp.float32)
    valid_mask = (row_index[None, :] < held_count[:, None]).astype(jnp.float32)
    row_weight = valid_mask / jnp.maximum(held_count, 1.0)[:, None]
    coef = 2.0 * loss_scale / full_cols * row_weight
    inv_scale = jnp.where(held_count[:, None] > 0, inv_scale, 0.0)
    row_info = jnp.stack([row_mean, inv_scale, coef, row_weight], axis=-1).reshape(
        n_dp * patch_rows, 4
    )

    scalars = jnp.concatenate([jnp.stack([cache_pos, core]).astype(jnp.int32), place_of])
    keep, send = head_terms(
        scalars,
        near_pred,
        near_cols,
        far_a,
        far_b,
        head_weight,
        flat(teacher_cache),
        row_info,
        full_cols,
    )
    with jax.named_scope("grad_core"):
        received = swap(send, 1)
    texts = both(lax.optimization_barrier((texts, send))[0], 2)
    codes = add_and_code(keep, received)
    codes, images, texts = lax.optimization_barrier((codes, images, texts))
    texts = spread(texts, 2 * N_Z, 2)
    with jax.named_scope("contrast"):
        pairs = images[:, embed].astype(jnp.int32) * 64 + images[:, embed + 1].astype(jnp.int32)
        logits = jnp.dot(
            images[:, :embed].astype(jnp.bfloat16),
            texts.T,
            preferred_element_type=jnp.float32,
        ) * (embed ** (-0.5))
        column = jnp.arange(texts.shape[0], dtype=jnp.int32)
        text_dp = column // (16 * shard_rows) * 16
        for n, bit in enumerate((1, 4, 8, 2)):
            text_dp = text_dp + column // (shard_rows * 2**n) % 2 * bit
        text_id = text_dp * img_dev + cache_pos * shard_rows + column % shard_rows
        best = jnp.max(logits, axis=1)
        denom = jnp.sum(jnp.exp(logits - best[:, None]), axis=1)
        target = jnp.sum(jnp.where(pairs[:, None] == text_id[None, :], logits, 0.0), axis=1)
        partial = jnp.pad(jnp.stack([best, denom, target]), ((0, 5), (0, EXT - img_dev)))
    with jax.named_scope("grad_xz"):
        codes = lax.all_to_all(
            codes.reshape(N_X * N_Z, -1, local_cols + EXT), "dp", 0, 0, axis_index_groups=XZ_GROUPS, tiled=True
        )
    head_grad, parts = sum_last(codes, partial)

    with jax.named_scope("loss_parts"):
        parts = [parts] + [ring(parts, step) for step in range(1, n_cache)]
        partials = []
        for k, got in enumerate(parts):
            first = (n_cache - k) % n_cache * shard_rows
            partials.append(got[:3, first : first + shard_rows])
        partials = jnp.stack(partials)
        best = jnp.max(partials[:, 0], axis=0)
        denom = jnp.sum(partials[:, 1] * jnp.exp(partials[:, 0] - best[None, :]), axis=0)
        contrast = best + jnp.log(denom) - jnp.sum(partials[:, 2], axis=0)
        regress = sum(got[3] for got in parts)
        regress = lax.dynamic_slice_in_dim(regress, cache_pos * shard_rows, shard_rows, 0)
    return (head_grad, regress + contrast)


def solution(mesh):
    in_specs = (
        P("dp", None, None),
        P(None, "cache"),
        P("dp", None, "cache"),
        P(),
        P("dp"),
        P(("dp", "cache"), None),
        P(("dp", "cache"), None),
        P(("dp", "cache")),
    )
    out_specs = (P("dp", "cache"), P(("dp", "cache")))
    return jax.shard_map(local, mesh=mesh, in_specs=in_specs, out_specs=out_specs, check_vma=False)
```
